32 devices in a mesh: expert: 8 (over z, x), fsdp: 4 (over y, core).
Axes of the slice: x: 2, y: 2, z: 4, core: 2. Of those that a mesh axis runs over, the one named last changes fastest.
Arguments:
- hidden_in: bfloat16 [2, 2048, 2048], P(None, ('expert', 'fsdp')), may hold values from -6 to 6
- seg_ids: int32 [2, 2048], P(None, ('expert', 'fsdp')), may hold values from 0 to 63, as said below
- routes: int32 [2, 2048, 4], P(None, ('expert', 'fsdp')), may hold values from 0 to 7, all different within a row; in each aligned block of 64 rows (0 to 63, 64 to 127, ..., all dimensions but the last counted through in order) at most 48 rows name the same one
- out_grad: bfloat16 [2, 2048, 2048], P(None, ('expert', 'fsdp')), may hold values from -6 to 6
- norm_gain1: bfloat16 [2048], P(('expert', 'fsdp')), may hold values from 0.5 to 1.5
- w_query: bfloat16 [2048, 2048], P(('expert', 'fsdp')), may hold values from -0.125 to 0.125
- w_key: bfloat16 [2048, 2048], P(('expert', 'fsdp')), may hold values from -0.125 to 0.125
- w_value: bfloat16 [2048, 2048], P(('expert', 'fsdp')), may hold values from -0.125 to 0.125
- b_qkv: bfloat16 [3, 2048], P(None, ('expert', 'fsdp')), may hold values from -3 to 3
- w_out: bfloat16 [2048, 2048], P(('expert', 'fsdp')), may hold values from -0.375 to 0.375
- norm_gain2: bfloat16 [2048], P(('expert', 'fsdp')), may hold values from 0.5 to 1.5
- w_router: bfloat16 [2048, 8], P(('expert', 'fsdp')), may hold values from -0.0625 to 0.0625
- shared_gate: bfloat16 [2048], P(('expert', 'fsdp')), may hold values from -0.125 to 0.125
- sh_gate: bfloat16 [2048, 5632], P(('expert', 'fsdp')), may hold values from -0.125 to 0.125
- sh_up: bfloat16 [2048, 5632], P(('expert', 'fsdp')), may hold values from -0.125 to 0.125
- sh_down: bfloat16 [2048, 5632], P(('expert', 'fsdp')), may hold values from -0.078125 to 0.078125
- ex_gate: bfloat16 [8, 2048, 1408], P('expert', None, 'fsdp'), may hold values from -0.125 to 0.125
- ex_up: bfloat16 [8, 2048, 1408], P('expert', None, 'fsdp'), may hold values from -0.125 to 0.125
- ex_down: bfloat16 [8, 1408, 2048], P('expert', 'fsdp'), may hold values from -0.625 to 0.625
Outputs:
- hidden_out: bfloat16 [2, 2048, 2048], P(None, ('expert', 'fsdp'))
- hidden_in_grad: float32 [2, 2048, 2048], P(None, ('expert', 'fsdp'))
- gain1_grad: float32 [2048], P(('expert', 'fsdp'))
- query_grad: float32 [2048, 2048], P(('expert', 'fsdp'))
- key_grad: float32 [2048, 2048], P(('expert', 'fsdp'))
- value_grad: float32 [2048, 2048], P(('expert', 'fsdp'))
- bias_grad: float32 [3, 2048], P(None, ('expert', 'fsdp'))
- out_proj_grad: float32 [2048, 2048], P(('expert', 'fsdp'))
- gain2_grad: float32 [2048], P(('expert', 'fsdp'))
- router_grad: float32 [2048, 8], P(('expert', 'fsdp'))
- shared_gate_grad: float32 [2048], P(('expert', 'fsdp'))
- sh_gate_grad: float32 [2048, 5632], P(('expert', 'fsdp'))
- sh_up_grad: float32 [2048, 5632], P(('expert', 'fsdp'))
- sh_down_grad: float32 [2048, 5632], P(('expert', 'fsdp'))
- ex_gate_grad: float32 [8, 2048, 1408], P('expert', None, 'fsdp')
- ex_up_grad: float32 [8, 2048, 1408], P('expert', None, 'fsdp')
- ex_down_grad: float32 [8, 1408, 2048], P('expert', 'fsdp')
The draws below stay inside these ranges and needn't reach their ends.
Inputs may be any that keep to these rules, and one draw needn't show every extreme that they name: `seg_ids`: within each sequence of 256 tokens the ids start at 0 and rise by 0 or 1 from token to token; in each micro-batch one sequence is a single document, and another reaches the largest id. `routes`: each token names 4 different experts; among the 64 tokens of one device in one micro-batch no expert is named more than 48 times, and some device has an expert named exactly 48 times.
All inputs are finite; a program needn't handle non-finite values.
Results may differ from the reference program's by a relative error of at most 0.015.
Values may be sent and summed in bfloat16 or wider, within the bound.
No kernel may reach another device: no remote copies, remote signals or barrier semaphores. Data moves between devices by JAX's collectives and lax.ppermute only.
A program may use at most 720 MiB of HBM per device.

```python
import math
from functools import partial
import jax
import jax.numpy as jnp
import numpy as np
from jax import lax

D = 2048
HEADS = 16
HEAD = 128
EXPERT_FF = 1408
SHARED_FF = 5632
TOPK = 4
MICRO = 2
TOK_MB = 64
EXPERTS = 8
SEQ = 256
TOKENS = 2048
CAP = 48


def draw_seg_ids(key, part):
    key = jax.random.fold_in(key, 7)
    rate_key, start_key, single_key = jax.random.split(key, 3)
    seq_count = TOKENS // SEQ
    periods = jnp.array([4, 8, 16, 32, 64, 128], jnp.int32)[jax.random.randint(rate_key, (MICRO, seq_count, 1), 0, 6)]
    raw_bits = jax.random.randint(start_key, (MICRO, seq_count, SEQ), 0, 1 << 20)
    starts = raw_bits % periods == 0
    position = jnp.arange(SEQ)[None, None, :]
    seq_index = jnp.arange(seq_count)[None, :, None]
    single_seq = jax.random.randint(single_key, (MICRO, 1, 1), 0, seq_count)
    dense_seq = (single_seq + 1) % seq_count
    forced = (seq_index == dense_seq) & (position % 4 == 0)
    starts = (starts | forced) & (position > 0) & (seq_index != single_seq)
    doc_ids = jnp.minimum(jnp.cumsum(starts.astype(jnp.int32), axis=-1), (SEQ - 1) // 4)
    return doc_ids.reshape(MICRO, TOKENS).astype(jnp.int32)


def level_of(own_key, shape, shards, least, top_value):
    loudness, own = 1.0, jax.random.fold_in(own_key, 6)
    for dim, shards_of in shards:
        draws = jnp.exp(jax.random.uniform(jax.random.fold_in(own, dim), (shards_of,), jnp.float32, least / len(shards), top_value / len(shards)))
        loudness = loudness * jnp.repeat(draws, shape[dim] // shards_of).reshape([-1 if axis == dim else 1 for axis in range(len(shape))])
    return loudness


def assign_block(rng, own, number, rows, count, top, most, slope):
    order = jax.random.permutation(rng, count)
    crowded, ordinary = shares(count, rows * top, most, slope, True), shares(count, rows * top, most, slope, False)
    places = jnp.arange(count)

    def named(tallies, rotation):
        used = int((tallies > 0).sum())
        fixed = max(1, used // 4)
        moved = fixed + (places - fixed + rotation * (used - fixed)) % max(1, count - fixed)
        return jnp.zeros((count,), jnp.int32).at[order[jnp.where(places < fixed, places, moved)]].set(jnp.asarray(tallies, jnp.int32))

    tallies = jnp.where(number % 4 == 0, named(crowded, number // 4), named(ordinary, number - number // 4 - 1))
    mixed = jax.random.permutation(jax.random.fold_in(own, 3), count)
    giver, taker = mixed[0:count // 2 * 2:2], mixed[1:count // 2 * 2:2]
    margin = jnp.minimum(tallies[giver] - 1, most - tallies[taker]) // 2
    margin = jnp.where((giver == order[0]) | (taker == order[0]) | (tallies[taker] == 0), 0, jnp.maximum(margin, 0))
    moved = jax.random.randint(jax.random.fold_in(own, 4), (count // 2,), 0, 1 << 20) % (margin + 1)
    tallies = tallies.at[giver].add(-moved).at[taker].add(moved)
    labels = jnp.searchsorted(jnp.cumsum(tallies), jnp.arange(rows * top), side="right").astype(jnp.int32)
    grid = labels.reshape(top, rows).T
    grid = grid[jax.random.permutation(jax.random.fold_in(own, 1), rows)]
    rotation = jax.random.randint(jax.random.fold_in(own, 2), (rows, 1), 0, top)
    return jnp.take_along_axis(grid, (jnp.arange(top)[None, :] + rotation) % top, axis=1)


def shares(amount, total, limit, lean, full):
    loads = [(1 << 20) // math.isqrt(standing ** lean) + 1 for standing in range(1, amount + 1)]
    largest = limit if full else min(limit, max(-(-total // amount), total * loads[0] // sum(loads)))
    least = 1 if total - largest >= amount - 1 else 0
    holding, rest = [largest] + [least] * (amount - 1), total - largest - least * (amount - 1)
    while rest > 0:
        candidates = [i for i in range(1, amount) if holding[i] < largest] or [i for i in range(1, amount) if holding[i] < limit]
        whole, budget = sum([loads[i] for i in candidates]), rest
        for i in candidates:
            addition = min(limit - holding[i], max(1, budget * loads[i] // whole), rest)
            holding[i] = holding[i] + addition
            rest = rest - addition
    return np.array(holding)


def centred(rng, extent, deviation, reach, cuts=(), kind=jnp.bfloat16):
    level = level_of(rng, extent, cuts, -0.22, 0.18) if cuts else 1.0
    values = jax.random.normal(rng, extent, jnp.float32) * deviation * level
    return jnp.minimum(jnp.maximum(values, -reach), reach).astype(kind)


def setup_inputs(seed: int = 0) -> dict:
    keys = jax.random.split(jax.random.key(seed), 20)
    hidden_in = centred(keys[0], (MICRO, TOKENS, D), 1.0, 6.0, ((1, 32),))
    seg_ids = draw_seg_ids(jax.random.fold_in(keys[19], 71), 0)
    routes_keys = jax.random.split(jax.random.fold_in(keys[2], 1), MICRO * TOKENS // TOK_MB)
    routes_turns = jax.random.permutation(jax.random.fold_in(keys[2], 3), MICRO * TOKENS // TOK_MB)
    routes = jax.vmap(lambda own, number: assign_block(jax.random.fold_in(keys[2], 2), own, number, TOK_MB, EXPERTS, TOPK, CAP, 2))(routes_keys, routes_turns).reshape((MICRO, TOKENS, TOPK))
    out_grad = centred(keys[3], (MICRO, TOKENS, D), 1.0, 6.0, ((1, 32),))
    norm_gain1 = jnp.clip(1.0 + 0.1 * jax.random.normal(keys[4], (D,), jnp.float32), 0.5, 1.5).astype(jnp.bfloat16)
    w_query = centred(keys[5], (D, D), D ** -0.5, 0.125, ((0, 32),))
    w_key = centred(keys[6], (D, D), D ** -0.5, 0.125, ((0, 32),))
    w_value = centred(keys[7], (D, D), D ** -0.5, 0.125, ((0, 32),))
    b_qkv = centred(keys[8], (3, D), 0.5, 3.0, ((1, 32),))
    w_out = centred(keys[9], (D, D), (D // 8) ** -0.5, 0.375, ((0, 32),))
    norm_gain2 = jnp.clip(1.0 + 0.1 * jax.random.normal(keys[10], (D,), jnp.float32), 0.5, 1.5).astype(jnp.bfloat16)
    w_router = centred(keys[11], (D, EXPERTS), (4 * D) ** -0.5, 0.0625, ((0, 32),))
    shared_gate = centred(keys[12], (D,), D ** -0.5, 0.125, ((0, 32),))
    sh_gate = centred(keys[13], (D, SHARED_FF), D ** -0.5, 0.125, ((0, 32),))
    sh_up = centred(keys[14], (D, SHARED_FF), D ** -0.5, 0.125, ((0, 32),))
    sh_down = centred(keys[15], (D, SHARED_FF), SHARED_FF ** -0.5, 0.078125, ((0, 32),))
    ex_gate = centred(keys[16], (EXPERTS, D, EXPERT_FF), D ** -0.5, 0.125, ((0, 8), (2, 4)))
    ex_up = centred(keys[17], (EXPERTS, D, EXPERT_FF), D ** -0.5, 0.125, ((0, 8), (2, 4)))
    ex_down = centred(keys[18], (EXPERTS, EXPERT_FF, D), (max(1, 4 * EXPERT_FF // (EXPERTS * EXPERTS))) ** -0.5, 0.625, ((0, 8), (1, 4)))
    return {"hidden_in": hidden_in, "seg_ids": seg_ids, "routes": routes, "out_grad": out_grad, "norm_gain1": norm_gain1, "w_query": w_query, "w_key": w_key, "w_value": w_value, "b_qkv": b_qkv, "w_out": w_out, "norm_gain2": norm_gain2, "w_router": w_router, "shared_gate": shared_gate, "sh_gate": sh_gate, "sh_up": sh_up, "sh_down": sh_down, "ex_gate": ex_gate, "ex_up": ex_up, "ex_down": ex_down}


EPSILON = 1e-06
ROPE_BASE = 1000000.0
MASKED = -1e+30

@jax.custom_vjp
def low(v):
    return lax.optimization_barrier(v.astype(jnp.bfloat16)).astype(jnp.float32)

@jax.custom_vjp
def low_back(v):
    return v

def low_keep(v):
    return (low(v), None)

def low_pass(kept, grad):
    return (grad,)

def back_keep(v):
    return (v, None)

def back_low(kept, grad):
    return (low(grad),)
low.defvjp(low_keep, low_pass)
low_back.defvjp(back_keep, back_low)

def matmul(left_op, right_op):
    return jnp.dot(left_op, right_op, precision=lax.Precision.HIGHEST)

def normalize(values, gain_vec):
    mean_sq = lax.optimization_barrier(jnp.mean(values * values, axis=-1, keepdims=True))
    return values * lax.rsqrt(mean_sq + EPSILON) * gain_vec

def angle_tables(positions):
    inverse = 1.0 / ROPE_BASE ** (jnp.arange(0, HEAD, 2).astype(jnp.float32) / HEAD)
    angles = positions.astype(jnp.float32)[:, None] * inverse[None, :]
    return (jnp.cos(angles)[:, None, :], jnp.sin(angles)[:, None, :])

def rotate(values, cosine, sine):
    half_size = values.shape[-1] // 2
    first_half = values[..., :half_size]
    second_half = values[..., half_size:]
    return jnp.concatenate([first_half * cosine - second_half * sine, second_half * cosine + first_half * sine], axis=-1)

def attend(seq_block):
    q_blk, k_blk, v_blk, s_blk = seq_block
    scores = low_back(jnp.einsum('qhd,khd->hqk', q_blk, k_blk, precision=lax.Precision.HIGHEST) * HEAD ** (-0.5))
    places = jnp.arange(SEQ)
    visible = (places[None, :] <= places[:, None]) & (s_blk[None, :] == s_blk[:, None])
    scores = jnp.where(visible[None], scores, MASKED)
    attn_probs = jax.nn.softmax(scores, axis=-1)
    return jnp.einsum('hqk,khd->qhd', low(attn_probs), v_blk, precision=lax.Precision.HIGHEST)

def forward(params, residual, segments, routes_mb):
    gain_one, w_query, w_key, w_value, b_qkv, w_out, gain_two, w_router, shared_gate, sh_gate, sh_up, sh_down, ex_gate, ex_up, ex_down = params
    token_count = residual.shape[0]
    seq_count = token_count // SEQ
    normed = low(normalize(residual, gain_one))
    query_lin = low_back(matmul(normed, w_query) + b_qkv[0])
    key_lin = low_back(matmul(normed, w_key) + b_qkv[1])
    value_lin = low_back(matmul(normed, w_value) + b_qkv[2])
    cosine, sine = angle_tables(jnp.arange(token_count) % SEQ)
    queries = low(rotate(query_lin.reshape(token_count, HEADS, HEAD), cosine, sine))
    keys_all = low(rotate(key_lin.reshape(token_count, HEADS, HEAD), cosine, sine))
    values_all = low(value_lin).reshape(token_count, HEADS, HEAD)
    attn_mixed = lax.map(jax.checkpoint(attend), (queries.reshape(seq_count, SEQ, HEADS, HEAD), keys_all.reshape(seq_count, SEQ, HEADS, HEAD), values_all.reshape(seq_count, SEQ, HEADS, HEAD), segments.reshape(seq_count, SEQ)))
    attended = low(low_back(attn_mixed.reshape(token_count, D)))
    after_attn = residual + low_back(matmul(attended, w_out))
    normed_two = low(normalize(after_attn, gain_two))
    logits = low_back(matmul(normed_two, jnp.concatenate([w_router, shared_gate[:, None]], axis=1)))
    router_probs = jax.nn.softmax(logits[:, :EXPERTS], axis=-1)
    shared_scale = jax.nn.sigmoid(logits[:, EXPERTS])
    gate_lin = low_back(matmul(normed_two, sh_gate))
    up_lin = low_back(matmul(normed_two, sh_up))
    shared_hidden = low(jax.nn.silu(gate_lin) * up_lin)
    shared_out = low_back(matmul(shared_hidden, sh_down.T))
    picked = lax.optimization_barrier(jnp.sum((routes_mb[:, :, None] == jnp.arange(EXPERTS)[None, None, :]).astype(jnp.float32), axis=1))
    weights_all = router_probs * picked

    def expert_step(running, inputs):
        gate_w, up_w, down_w, column = inputs
        rows_in = low_back(normed_two)
        gate_e = low_back(matmul(rows_in, gate_w))
        up_e = low_back(matmul(rows_in, up_w))
        hidden_e = low(jax.nn.silu(gate_e) * up_e)
        result_e = low(low_back(matmul(hidden_e, down_w)))
        return (running + column[:, None] * result_e, None)
    routed, leftover = lax.scan(jax.checkpoint(expert_step), jnp.zeros_like(residual), (ex_gate, ex_up, ex_down, weights_all.T))
    return after_attn + shared_scale[:, None] * shared_out + routed

def reference(hidden_in, seg_ids, routes, out_grad, norm_gain1, w_query, w_key, w_value, b_qkv, w_out, norm_gain2, w_router, shared_gate, sh_gate, sh_up, sh_down, ex_gate, ex_up, ex_down):
    params = tuple((weight.astype(jnp.float32) for weight in (norm_gain1, w_query, w_key, w_value, b_qkv, w_out, norm_gain2, w_router, shared_gate, sh_gate, sh_up, sh_down, ex_gate, ex_up, ex_down)))
    totals = None
    outputs = []
    in_grads = []
    for micro_idx in range(MICRO):
        local_forward = partial(forward, segments=seg_ids[micro_idx], routes_mb=routes[micro_idx])
        result, pullback = jax.vjp(local_forward, params, hidden_in[micro_idx].astype(jnp.float32))
        grad_params, grad_input = pullback(out_grad[micro_idx].astype(jnp.float32))
        totals = grad_params if totals is None else jax.tree.map(jnp.add, totals, grad_params)
        outputs.append(result.astype(jnp.bfloat16))
        in_grads.append(grad_input)
    return (jnp.stack(outputs), jnp.stack(in_grads), totals[0], totals[1], totals[2], totals[3], totals[4], totals[5], totals[6], totals[7], totals[8], totals[9], totals[10], totals[11], totals[12], totals[13], totals[14])
```

```python
import functools

import jax
import jax.numpy as jnp
from jax import lax
from jax.experimental import pallas as pl
from jax.experimental.pallas import tpu as pltpu
from jax.sharding import PartitionSpec as P

HEADS = 16
HEAD = 128
SHARED_FF = 5632
EPSILON = 1e-06
ROPE_BASE = 1000000.0
MASKED = -1e30
ALL = ("expert", "fsdp")
BF = jnp.bfloat16
F32 = jnp.float32
LANES = 128
TILE = 256


def normalize(values):
    inverse = lax.rsqrt(jnp.mean(values * values, axis=-1, keepdims=True) + EPSILON)
    return (values * inverse, inverse)


def norm_back(grad_normed, scaled, inverse, gain_vec):
    grad_scaled = grad_normed * gain_vec
    return inverse * (grad_scaled - scaled * jnp.mean(grad_scaled * scaled, axis=-1, keepdims=True))


def angle_tables(places):
    inverse = 1.0 / ROPE_BASE ** (jnp.arange(0, HEAD, 2).astype(F32) / HEAD)
    angles = places.astype(F32)[:, None] * inverse[None, :]
    cosine, sine = jnp.cos(angles), jnp.sin(angles)
    return jnp.concatenate([cosine, cosine], axis=1), jnp.concatenate([-sine, sine], axis=1)


def silu_parts(pre_act):
    logistic = 1.0 / (1.0 + jnp.exp(-pre_act))
    return (pre_act * logistic, logistic * (1.0 + pre_act * (1.0 - logistic)))


def contract(pattern, left_op, right_op):
    return jnp.einsum(pattern, left_op, right_op, preferred_element_type=F32)


def dot_nt(left_op, right_op):
    return lax.dot_general(left_op, right_op, (((1,), (1,)), ((), ())), preferred_element_type=F32)


def dot_nn(left_op, right_op):
    return lax.dot_general(left_op, right_op, (((1,), (0,)), ((), ())), preferred_element_type=F32)


def dot_tn(left_op, right_op):
    return lax.dot_general(left_op, right_op, (((0,), (0,)), ((), ())), preferred_element_type=F32)


def after(value, *earlier):
    return lax.optimization_barrier((value, earlier))[0]


def partner_perm(n_exp, n_fsdp, bit):
    return [(e * n_fsdp + f, e * n_fsdp + (f ^ bit)) for e in range(n_exp) for f in range(n_fsdp)]


def expert_perm(n_exp, n_fsdp, move):
    return [(e * n_fsdp + f, move(e) * n_fsdp + f) for e in range(n_exp) for f in range(n_fsdp)]


class Links:
    def __init__(self):
        self.n_exp = lax.axis_size("expert")
        self.n_fsdp = lax.axis_size("fsdp")
        self.my_exp = lax.axis_index("expert")
        self.my_fsdp = lax.axis_index("fsdp")
        self.n_all = self.n_exp * self.n_fsdp
        self.ring = self.n_exp == 8

    def partner(self, value, bit):
        return lax.ppermute(value, ALL, partner_perm(self.n_exp, self.n_fsdp, bit))

    def pair(self, value):
        return lax.ppermute(value, ALL, expert_perm(self.n_exp, self.n_fsdp, lambda e: e ^ 1))

    def forward(self, value):
        return lax.ppermute(value, ALL, expert_perm(self.n_exp, self.n_fsdp, lambda e: (e + 2) % 8))

    def slot(self, step, other):
        z = lax.rem(self.my_exp // 2 + 4 - step, 4)
        x = lax.rem(self.my_exp, 2)
        return z * 2 + (1 - x if other else x)

    def ring_gather(self, value):
        parts, current = [], value
        for step in range(4):
            following = self.forward(current) if step < 3 else None
            parts.append([current, self.pair(current)])
            current = following
        return parts

    def ring_sum(self, parts, kind=BF):
        arriving = None
        for step in (1, 2, 3, 0):
            own, other = parts(step)
            total = own.astype(F32) + self.pair(other.astype(kind)).astype(F32)
            if arriving is not None:
                total = total + arriving.astype(F32)
            arriving = self.forward(total.astype(kind)) if step else None
        return total

    def gather_rows(self, value):
        if not self.ring:
            return lax.all_gather(value, "expert", axis=0)
        parts = self.ring_gather(value)
        full = jnp.zeros((8,) + value.shape, value.dtype)
        for step in range(4):
            for other in range(2):
                full = lax.dynamic_update_index_in_dim(full, parts[step][other], self.slot(step, other), 0)
        return full

    def sum_rows(self, value, kind=BF):
        if not self.ring:
            return lax.psum_scatter(value.astype(kind), "expert", scatter_dimension=0).astype(F32)

        def parts(step):
            return [
                lax.dynamic_index_in_dim(value, self.slot(step, other), 0, keepdims=False) for other in range(2)
            ]

        return self.ring_sum(parts, kind)

    def swap_fsdp(self, value):
        mine = lax.dynamic_index_in_dim(value, self.my_fsdp, 0, keepdims=False)
        result = lax.dynamic_update_index_in_dim(value, mine, self.my_fsdp, 0)
        for bit in range(1, self.n_fsdp):
            other = lax.bitwise_xor(self.my_fsdp, bit)
            block = lax.dynamic_index_in_dim(value, other, 0, keepdims=False)
            result = lax.dynamic_update_index_in_dim(result, self.partner(block, bit), other, 0)
        return result

    def gather_four(self, value):
        far = self.partner(value, 2)
        return [value, self.partner(value, 1), far, self.partner(far, 1)]

    def gather_seq(self, value):
        return jnp.concatenate(self.gather_four(value), axis=1)

    def sum_four(self, parts, kind=BF):
        far = (parts[2].astype(F32) + self.partner(parts[3].astype(kind), 1).astype(F32)).astype(kind)
        near = parts[0].astype(F32) + self.partner(parts[1].astype(kind), 1).astype(F32)
        return near + self.partner(far, 2).astype(F32)

    def gather_small(self, value):
        rows, columns = value.shape
        if not self.ring:
            full = lax.all_gather(value, ALL, axis=0)
        else:
            four = jnp.stack(self.gather_four(value.reshape(rows * columns)))
            parts = self.ring_gather(four)
            blocks = jnp.concatenate([parts[step][other] for step in range(4) for other in range(2)])
            places = jnp.stack([self.slot(step, other) for step in range(4) for other in range(2)])
            inner = lax.bitwise_xor(self.my_fsdp, jnp.arange(4))
            places = (places[:, None] * 4 + inner[None]).reshape(-1)
            choice = (jnp.arange(self.n_all)[:, None] == places[None]).astype(value.dtype)
            full = dot_nn(choice, blocks).astype(value.dtype).reshape(self.n_all, rows, columns)
        return full.transpose(1, 0, 2).reshape(rows, self.n_all * columns)

    def sum_small(self, value):
        rows, columns = value.shape[0], value.shape[1] // self.n_all
        blocks = value.reshape(rows, self.n_all, columns).transpose(1, 0, 2)
        if not self.ring:
            return lax.psum_scatter(blocks.reshape(self.n_all, -1), ALL, scatter_dimension=0).reshape(rows, columns)
        blocks = blocks.reshape(self.n_exp, self.n_fsdp, rows * columns)
        four = self.sum_rows(blocks, F32)
        parts = [
            lax.dynamic_index_in_dim(four, lax.bitwise_xor(self.my_fsdp, k), 0, keepdims=True) for k in range(4)
        ]
        return self.sum_four(parts, F32).reshape(rows, columns)


def attend_kernel(heads, seq, scale, x_ref, w_ref, bias_ref, cos_ref, sin_ref, place_ref, seg_ref,
                  place_row_ref, seg_row_ref, qkv_ref, out_ref):
    lin = dot_nn(x_ref[...], w_ref[...]) + bias_ref[...]
    cosine, sine = cos_ref[...], sin_ref[...]
    span = heads * HEAD
    for micro in range(x_ref.shape[0] // seq):
        low, high = micro * seq, (micro + 1) * seq
        visible = (place_row_ref[...] <= place_ref[...]) & (seg_row_ref[micro : micro + 1, :] == seg_ref[low:high, :])
        for head in range(heads):
            at = head * HEAD
            query = lin[low:high, at : at + HEAD]
            key = lin[low:high, span + at : span + at + HEAD]
            value = lin[low:high, 2 * span + at : 2 * span + at + HEAD].astype(BF)
            query = (query * cosine + pltpu.roll(query, HEAD // 2, 1) * sine).astype(BF)
            key = (key * cosine + pltpu.roll(key, HEAD // 2, 1) * sine).astype(BF)
            scores = jnp.where(visible, dot_nt(query, key) * scale, MASKED)
            exps = jnp.exp(scores - jnp.max(scores, axis=1, keepdims=True))
            probs = exps / jnp.sum(exps, axis=1, keepdims=True)
            out_ref[low:high, at : at + HEAD] = dot_nn(probs.astype(BF), value).astype(BF)
            qkv_ref[low:high, at : at + HEAD] = query
            qkv_ref[low:high, span + at : span + at + HEAD] = key
            qkv_ref[low:high, 2 * span + at : 2 * span + at + HEAD] = value


def attend_back_kernel(heads, seq, scale, grad_ref, wo_ref, qkv_ref, cos_ref, sin_ref, place_ref, seg_ref,
                       place_row_ref, seg_row_ref, lin_ref):
    grad_out = dot_nt(grad_ref[...], wo_ref[...]).astype(BF)
    cosine, sine = cos_ref[...], sin_ref[...]
    span = heads * HEAD
    for micro in range(grad_ref.shape[0] // seq):
        low, high = micro * seq, (micro + 1) * seq
        visible = (place_row_ref[...] <= place_ref[...]) & (seg_row_ref[micro : micro + 1, :] == seg_ref[low:high, :])
        for head in range(heads):
            at = head * HEAD
            query = qkv_ref[low:high, at : at + HEAD]
            key = qkv_ref[low:high, span + at : span + at + HEAD]
            value = qkv_ref[low:high, 2 * span + at : 2 * span + at + HEAD]
            grad = grad_out[low:high, at : at + HEAD]
            scores = jnp.where(visible, dot_nt(query, key) * scale, MASKED)
            exps = jnp.exp(scores - jnp.max(scores, axis=1, keepdims=True))
            probs = exps / jnp.sum(exps, axis=1, keepdims=True)
            grad_probs = dot_nt(grad, value)
            grad_value = dot_tn(probs.astype(BF), grad)
            grad_scores = probs * (grad_probs - jnp.sum(probs * grad_probs, axis=1, keepdims=True))
            grad_scores = grad_scores.astype(BF)
            grad_query = dot_nn(grad_scores, key) * scale
            grad_key = dot_tn(grad_scores, query) * scale
            grad_query = grad_query * cosine - pltpu.roll(grad_query, HEAD // 2, 1) * sine
            grad_key = grad_key * cosine - pltpu.roll(grad_key, HEAD // 2, 1) * sine
            lin_ref[low:high, at : at + HEAD] = grad_query.astype(BF)
            lin_ref[low:high, span + at : span + at + HEAD] = grad_key.astype(BF)
            lin_ref[low:high, 2 * span + at : 2 * span + at + HEAD] = grad_value.astype(BF)


def whole(shape):
    return pl.BlockSpec(shape, lambda *_: (0,) * len(shape))


def attend(normed, wqkv, bias, tables, seq, back=None):
    cosine, sine, place, seg, place_row, seg_row = tables
    rows = normed.shape[0]
    pairs = 2
    wide3 = wqkv.shape[1]
    heads = wide3 // 3 // HEAD // pairs
    span = heads * HEAD
    scale = HEAD ** (-0.5)
    common = (cosine, sine, place, seg, place_row, seg_row)
    common_specs = [whole(item.shape) for item in common]
    params = pltpu.CompilerParams(vmem_limit_bytes=40 * 2**20)
    if back is None:
        return pl.pallas_call(
            functools.partial(attend_kernel, heads, seq, scale),
            grid=(pairs,),
            in_specs=[
                whole(normed.shape),
                pl.BlockSpec((wqkv.shape[0], 3 * span), lambda p: (0, p)),
                pl.BlockSpec((1, 3 * span), lambda p: (0, p)),
            ] + common_specs,
            out_specs=[
                pl.BlockSpec((rows, 3 * span), lambda p: (0, p)),
                pl.BlockSpec((rows, span), lambda p: (0, p)),
            ],
            out_shape=[
                jax.ShapeDtypeStruct((rows, wide3), BF),
                jax.ShapeDtypeStruct((rows, wide3 // 3), BF),
            ],
            compiler_params=params,
            cost_estimate=pl.CostEstimate(flops=5 * 10**9, bytes_accessed=10**7, transcendentals=10**6),
            name="attend",
        )(normed, wqkv, bias, *common)
    grad, wo, qkv = back
    return pl.pallas_call(
        functools.partial(attend_back_kernel, heads, seq, scale),
        grid=(pairs,),
        in_specs=[
            whole(grad.shape),
            pl.BlockSpec((span, wo.shape[1]), lambda p: (p, 0)),
            pl.BlockSpec((rows, 3 * span), lambda p: (0, p)),
        ] + common_specs,
        out_specs=pl.BlockSpec((rows, 3 * span), lambda p: (0, p)),
        out_shape=jax.ShapeDtypeStruct((rows, wide3), BF),
        compiler_params=params,
        cost_estimate=pl.CostEstimate(flops=5 * 10**9, bytes_accessed=10**7, transcendentals=10**6),
        name="attend_back",
    )(grad, wo, qkv, *common)


def feed_kernel(experts, shared, n_tiles, slots_ref, *refs):
    x_refs, g_refs = refs[:4], refs[4:8]
    wg_ref, wu_ref, wd_ref, router_ref = refs[8:12]
    hs_ref, dg_ref, du_ref = refs[12:15]
    gn_refs, out_refs = refs[15:19], refs[19:23]
    scale_shared, scale_expert, named, dot_shared, dot_expert, acc_out, acc_gn = refs[23:]
    width = x_refs[0].shape[-1]
    own = x_refs[0].shape[0]
    rows = 4 * own
    step = pl.program_id(0)
    x = jnp.concatenate([ref[...] for ref in x_refs], axis=0)
    g = jnp.concatenate([ref[0, :, :width] for ref in g_refs], axis=0)
    expert = slots_ref[2]

    @pl.when(step == 0)
    def _():
        logits = dot_nt(x, router_ref[...])
        lane = lax.broadcasted_iota(jnp.int32, logits.shape, 1)
        scores = jnp.where(lane < experts, logits, MASKED)
        exps = jnp.where(lane < experts, jnp.exp(scores - jnp.max(scores, axis=1, keepdims=True)), 0.0)
        probs = exps / jnp.sum(exps, axis=1, keepdims=True)
        mine = jnp.sum(jnp.where(lane == expert, probs, 0.0), axis=1, keepdims=True)
        gate = jnp.sum(jnp.where(lane == experts, logits, 0.0), axis=1, keepdims=True)
        names = jnp.concatenate([ref[0, :, width:] for ref in g_refs], axis=0).astype(F32)
        lane = lax.broadcasted_iota(jnp.int32, names.shape, 1)
        hit = jnp.where((lane < 4) & (names == expert.astype(F32)), 1.0, 0.0)
        hit = jnp.sum(hit, axis=1, keepdims=True)
        scale_shared[...] = jnp.broadcast_to(1.0 / (1.0 + jnp.exp(-gate)), scale_shared.shape)
        scale_expert[...] = jnp.broadcast_to(mine * hit, scale_expert.shape)
        named[...] = jnp.broadcast_to(hit, named.shape)
        dot_shared[...] = jnp.zeros_like(dot_shared)
        dot_expert[...] = jnp.zeros_like(dot_expert)

    wg, wu, wd = wg_ref[...], wu_ref[...], wd_ref[...]
    act, slope = silu_parts(dot_nt(x, wg))
    up = dot_nt(x, wu)
    grad = dot_nt(g, wd)
    unit = lax.broadcasted_iota(jnp.int32, (rows, TILE), 1) + step * TILE
    in_shared = unit < shared
    row_scale = jnp.where(in_shared, scale_shared[:, :1], scale_expert[:, :1])
    hidden = act * up
    dots = hidden * grad
    dot_shared[...] += jnp.sum(jnp.where(in_shared, dots, 0.0), axis=1, keepdims=True)
    dot_expert[...] += jnp.sum(jnp.where(in_shared, 0.0, dots), axis=1, keepdims=True)
    hs = (hidden * row_scale).astype(BF)
    grad = grad * row_scale
    dg = (grad * up * slope).astype(BF)
    du = (grad * act).astype(BF)
    hs_ref[...] = hs
    dg_ref[...] = dg
    du_ref[...] = du
    out_part = dot_nn(hs, wd)
    gn_part = dot_nn(dg, wg) + dot_nn(du, wu)

    @pl.when(step == 0)
    def _():
        acc_out[...] = out_part
        acc_gn[...] = gn_part

    @pl.when((step > 0) & (step < n_tiles - 1))
    def _():
        acc_out[...] += out_part
        acc_gn[...] += gn_part

    @pl.when(step == n_tiles - 1)
    def _():
        lane = lax.broadcasted_iota(jnp.int32, (rows, LANES), 1)
        extra = jnp.where(lane == expert, dot_expert[...] * named[...], 0.0)
        extra = extra + jnp.where(lane == experts, dot_shared[...], 0.0)
        for k in range(4):
            low, high = k * own, (k + 1) * own
            gn_refs[k][:, :width] = (acc_gn[low:high, :] + gn_part[low:high, :]).astype(BF)
            gn_refs[k][:, width:] = extra[low:high, :].astype(BF)
            out_refs[k][...] = (acc_out[low:high, :] + out_part[low:high, :]).astype(BF)


def feed(slots, blocks, near, far, wg, wu, wd, router, experts, shared):
    own, width = blocks[0].shape
    n_tiles = wg.shape[0] // TILE
    rows = 4 * own
    wide = near.shape[2]
    near_spec = [pl.BlockSpec((1, own, wide), lambda i, s, k=k: (s[k], 0, 0)) for k in range(2)]
    tile_rows = pl.BlockSpec((TILE, width), lambda i, s: (i, 0))
    tile_cols = pl.BlockSpec((rows, TILE), lambda i, s: (0, i))
    units = jax.ShapeDtypeStruct((rows, wg.shape[0]), BF)
    return pl.pallas_call(
        functools.partial(feed_kernel, experts, shared, n_tiles),
        grid_spec=pltpu.PrefetchScalarGridSpec(
            num_scalar_prefetch=1,
            grid=(n_tiles,),
            in_specs=[whole((own, width))] * 4 + near_spec + near_spec + [tile_rows] * 3 + [whole(router.shape)],
            out_specs=[tile_cols] * 3 + [whole((own, wide))] * 4 + [whole((own, width))] * 4,
            scratch_shapes=[pltpu.VMEM((rows, LANES), F32)] * 5 + [pltpu.VMEM((rows, width), F32)] * 2,
        ),
        out_shape=[units] * 3
        + [jax.ShapeDtypeStruct((own, wide), BF)] * 4
        + [jax.ShapeDtypeStruct((own, width), BF)] * 4,
        compiler_params=pltpu.CompilerParams(vmem_limit_bytes=56 * 2**20),
        cost_estimate=pl.CostEstimate(flops=16 * 10**9, bytes_accessed=3 * 10**7, transcendentals=10**6),
        name="feed",
    )(slots, *blocks, near, near, far, far, wg, wu, wd, router)


def weights_kernel(slots_ref, *refs):
    x_refs = [refs[4 * k : 4 * k + 4] for k in range(4)]
    near_ref, far_ref = refs[16:18]
    hs_refs, dg_refs, du_refs = refs[18:22], refs[22:26], refs[26:30]
    wg_ref, wu_ref, wd_ref = refs[30:33]
    width = x_refs[0][0].shape[-1]
    for k in range(4):
        x = jnp.concatenate([ref[...] for ref in x_refs[k]], axis=0)
        first, second = slots_ref[2 * k], slots_ref[2 * k + 1]
        g = jnp.concatenate(
            [ref[slot, :, :width] for ref in (near_ref, far_ref) for slot in (first, second)], axis=0
        )
        parts = dot_tn(dg_refs[k][...], x), dot_tn(du_refs[k][...], x), dot_tn(hs_refs[k][...], g)
        for ref, part in zip((wg_ref, wu_ref, wd_ref), parts):
            if k == 0:
                ref[...] = part
            else:
                ref[...] += part


def weight_grads(slots, blocks, near, far, hs, dg, du):
    own, width = blocks[0].shape
    rows, units = hs[0].shape
    n_tiles = units // TILE
    once = pl.Buffered(1)

    def fixed(shape):
        return pl.BlockSpec(shape, lambda *_: (0,) * len(shape), pipeline_mode=once)

    tile_cols = pl.BlockSpec((rows, TILE), lambda i, s: (0, i))
    return pl.pallas_call(
        weights_kernel,
        grid_spec=pltpu.PrefetchScalarGridSpec(
            num_scalar_prefetch=1,
            grid=(n_tiles,),
            in_specs=[fixed((own, width))] * 16 + [fixed(near.shape)] * 2 + [tile_cols] * 12,
            out_specs=[pl.BlockSpec((TILE, width), lambda i, s: (i, 0))] * 3,
        ),
        out_shape=[jax.ShapeDtypeStruct((units, width), F32)] * 3,
        compiler_params=pltpu.CompilerParams(vmem_limit_bytes=56 * 2**20),
        cost_estimate=pl.CostEstimate(flops=32 * 10**9, bytes_accessed=6 * 10**7, transcendentals=0),
        name="weight_grads",
    )(slots, *blocks, near, far, *hs, *dg, *du)


def feed_plain(normed, grad, named, expert, wg, wu, wd, router, experts, shared):
    logits = contract("td,cd->tc", normed, router)
    router_probs = jax.nn.softmax(logits[:, :experts], axis=-1)
    shared_scale = jax.nn.sigmoid(logits[:, experts : experts + 1])
    hot = (jnp.arange(experts) == expert).astype(F32)
    gate_here = jnp.sum(router_probs * hot, axis=1, keepdims=True) * named[:, None]
    is_shared = (jnp.arange(wg.shape[0]) < shared)[None]
    row_scale = jnp.where(is_shared, shared_scale, gate_here)
    act, slope = silu_parts(contract("td,cd->tc", normed, wg))
    up = contract("td,cd->tc", normed, wu)
    hidden = act * up
    hidden_scaled = (hidden * row_scale).astype(BF)
    grad_hidden = contract("td,fd->tf", grad, wd)
    dots = hidden * grad_hidden
    dot_shared = jnp.sum(jnp.where(is_shared, dots, 0.0), axis=1, keepdims=True)
    dot_expert = jnp.sum(jnp.where(is_shared, 0.0, dots), axis=1, keepdims=True) * named[:, None]
    grad_pre = grad_hidden * row_scale
    grad_gate = (grad_pre * up * slope).astype(BF)
    grad_up = (grad_pre * act).astype(BF)
    grad_normed = contract("tc,cd->td", grad_gate, wg) + contract("tc,cd->td", grad_up, wu)
    extra = jnp.concatenate([dot_expert * hot, dot_shared], axis=1)
    extra = jnp.pad(extra, ((0, 0), (0, LANES - extra.shape[1])))
    out = contract("tf,fd->td", hidden_scaled, wd)
    return (
        jnp.concatenate([grad_normed, extra], axis=1),
        out,
        contract("tc,td->cd", grad_gate, normed),
        contract("tc,td->cd", grad_up, normed),
        contract("tf,td->fd", hidden_scaled, grad),
    )


def on_device(
    hidden_in, seg_ids, routes, out_grad, norm_gain1, w_query, w_key, w_value, b_qkv, w_out,
    norm_gain2, w_router, shared_gate, sh_gate, sh_up, sh_down, ex_gate, ex_up, ex_down,
):
    links = Links()
    micro, tok, width = hidden_in.shape
    experts = w_router.shape[1]
    rows_w = w_query.shape[0]
    n_exp, n_fsdp, n_all = links.n_exp, links.n_fsdp, links.n_all
    my_exp, my_fsdp = links.my_exp, links.my_fsdp
    half_f, core_f = my_fsdp // 2, lax.rem(my_fsdp, 2)
    heads_dev = HEADS // n_fsdp
    wide = heads_dev * HEAD
    seq = tok * n_fsdp
    own = micro * tok
    sh_cols = SHARED_FF // n_all
    ex_cols = ex_gate.shape[2]

    def by_fsdp(three):
        rows = three.shape[0]
        split = three.reshape(rows, 3, 2, 2, heads_dev // 2, 2, HEAD)
        return split.transpose(5, 2, 0, 3, 1, 4, 6).reshape(n_fsdp, rows, 3 * wide)

    def from_fsdp(blocks):
        rows = blocks.shape[1]
        split = blocks.reshape(2, 2, rows, 2, 3, heads_dev // 2, HEAD)
        return split.transpose(4, 2, 1, 3, 5, 0, 6).reshape(3, rows, width)

    small = jnp.concatenate([w_router.T, shared_gate[None], norm_gain1[None], norm_gain2[None], b_qkv], axis=0)
    n_small = small.shape[0]
    small = links.gather_small(small)
    router_rows = small[: experts + 1]
    gain_one = small[experts + 1].astype(F32)
    gain_two = small[experts + 2].astype(F32)
    bias = by_fsdp(small[experts + 3 :].astype(F32)[None])
    bias = lax.dynamic_index_in_dim(bias, my_fsdp, 0, keepdims=False)

    x = hidden_in.reshape(own, width).astype(F32)
    scaled_one, inverse_one = normalize(x)
    normed_one = (scaled_one * gain_one).astype(BF)
    normed_seq = links.gather_seq(normed_one.reshape(micro, tok, width)).reshape(micro * seq, width)

    qkv = by_fsdp(jnp.stack([w_query, w_key, w_value], axis=1))
    qkv = links.swap_fsdp(qkv).reshape(n_fsdp * rows_w, 3 * wide)
    wqkv = links.gather_rows(qkv).reshape(width, 3 * wide)
    if links.ring:
        wo_rows = links.gather_rows(after(w_out, wqkv))
        keep = lax.dynamic_slice_in_dim(wo_rows, 4 * core_f, 4, 0)
        give = lax.dynamic_slice_in_dim(wo_rows, 4 * (1 - core_f), 4, 0)
        got = links.partner(give, 1)
        wo = jnp.where(core_f == 0, jnp.stack([keep, got], axis=1), jnp.stack([got, keep], axis=1))
        wo = wo.reshape(wide, width)
    else:
        wo = lax.all_gather(w_out, ALL, axis=0, tiled=True).reshape(2, heads_dev, 2, HEAD, width)
        wo = lax.dynamic_index_in_dim(wo, core_f, 0, keepdims=False)
        wo = lax.dynamic_index_in_dim(wo, half_f, 1, keepdims=False).reshape(wide, width)

    tile_cols = sh_cols // LANES * LANES
    rest_cols = sh_cols - tile_cols

    def by_owner(weight):
        full = weight[:, : n_all * tile_cols].reshape(rows_w, n_all, tile_cols).transpose(1, 0, 2)
        rest = weight[:, n_all * tile_cols :].reshape(rows_w, n_all, rest_cols).transpose(1, 0, 2)
        return full, rest

    def from_owner(full, rest):
        return jnp.concatenate(
            [full.transpose(1, 0, 2).reshape(rows_w, -1), rest.transpose(1, 0, 2).reshape(rows_w, -1)], axis=1
        )

    pieces = [by_owner(weight) for weight in (sh_gate, sh_up, sh_down)]
    shared_w = jnp.concatenate([piece[0] for piece in pieces] + [piece[1] for piece in pieces], axis=2)
    shared_w = lax.all_to_all(shared_w, ALL, split_axis=0, concat_axis=0, tiled=True)
    shared_w = shared_w.reshape(width, 3 * sh_cols).T

    def three(rows):
        return [
            jnp.concatenate(
                [rows[k * tile_cols : (k + 1) * tile_cols],
                 rows[3 * tile_cols + k * rest_cols : 3 * tile_cols + (k + 1) * rest_cols]], axis=0)
            for k in range(3)
        ]

    shared_other = links.partner(shared_w, 2)
    routed_own = [ex_gate[0].T, ex_up[0].T, ex_down[0]]
    routed_other = [links.partner(after(weight, normed_seq), 2) for weight in routed_own]
    units = 2 * (sh_cols + ex_cols)
    pad = jnp.zeros((-units % TILE, width), BF)
    wg, wu, wd = [
        jnp.concatenate([mine, other, routed, routed_far, pad], axis=0)
        for mine, other, routed, routed_far in zip(three(shared_w), three(shared_other), routed_own, routed_other)
    ]
    shared_units = 2 * sh_cols
    router_pad = jnp.pad(router_rows, ((0, -(experts + 1) % 16), (0, 0)))

    grad_own = out_grad.reshape(own, width)
    names = jnp.pad(routes.reshape(own, -1).astype(BF), ((0, 0), (0, LANES - routes.shape[2])))
    grad_near = lax.all_gather(after(jnp.concatenate([grad_own, names], axis=1), wqkv), "expert", axis=0)
    grad_far = links.partner(grad_near, 1)

    order = lax.bitwise_xor(my_fsdp, jnp.arange(n_fsdp))
    places = (order[:, None] * tok + jnp.arange(tok)[None]).reshape(seq)
    seg_seq = links.gather_seq(seg_ids)
    cosine, sine = angle_tables(places)
    tables = (cosine, sine, places[:, None], seg_seq.reshape(micro * seq, 1), places[None], seg_seq)
    qkv_seq, attended = attend(normed_seq, wqkv, bias, tables, seq)
    attn_part = contract("tc,cd->td", attended, wo).reshape(micro, n_fsdp, tok, width)
    attn_sum = links.sum_four([attn_part[:, k] for k in range(4)]).reshape(own, width)
    after_attn = x + attn_sum
    scaled_two, inverse_two = normalize(after_attn)
    normed_two = (scaled_two * gain_two).astype(BF)

    if links.ring:
        gathered = links.ring_gather(normed_two)
        fed, blocks, slots = {}, {}, {}
        for step in (1, 2, 3, 0):
            blocks[step] = gathered[step] + [links.partner(block, 1) for block in gathered[step]]
            slots[step] = [links.slot(step, other) for other in range(2)]
            fed[step] = feed(
                jnp.stack(slots[step] + [my_exp]), blocks[step], grad_near, grad_far,
                wg, wu, wd, router_pad, experts, shared_units,
            )

        def summed(first):
            def parts(step):
                found = fed[step][first : first + 4]
                return [found[k].astype(F32) + links.partner(found[2 + k], 1).astype(F32) for k in range(2)]

            return links.ring_sum(parts)

        grad_sum = summed(3)
        out_sum = summed(7)
        wg_grad, wu_grad, wd_grad = weight_grads(
            jnp.stack([slot for step in range(4) for slot in slots[step]]),
            [block for step in range(4) for block in blocks[step]],
            grad_near, grad_far, *[[fed[step][item] for step in range(4)] for item in range(3)],
        )
    else:
        near = lax.all_gather(normed_two, "expert", axis=0, tiled=True)
        normed_all = jnp.concatenate([near, links.partner(near, 1)], axis=0)
        grad_all = jnp.concatenate([grad_near, grad_far], axis=0).reshape(2 * n_exp * own, -1)
        named = jnp.sum((grad_all[:, width : width + routes.shape[2]] == my_exp.astype(BF)).astype(F32), axis=1)
        grad_part, out_part, wg_grad, wu_grad, wd_grad = feed_plain(
            normed_all, grad_all[:, :width], named, my_exp, wg, wu, wd, router_pad, experts, shared_units
        )

        def summed(part):
            count = n_exp * own
            total = part[:count] + links.partner(part[count:].astype(BF), 1).astype(F32)
            return links.sum_rows(total.reshape(n_exp, own, -1))

        grad_sum, out_sum = summed(grad_part), summed(out_part)
    hidden_out = (after_attn + out_sum).astype(BF)

    own_logits = contract("td,cd->tc", normed_two, router_rows)
    own_probs = jax.nn.softmax(own_logits[:, :experts], axis=-1)
    own_scale = jax.nn.sigmoid(own_logits[:, experts])
    grad_probs = grad_sum[:, width : width + experts]
    grad_router = own_probs * (grad_probs - jnp.sum(own_probs * grad_probs, axis=-1, keepdims=True))
    grad_gate = grad_sum[:, width + experts] * own_scale * (1.0 - own_scale)
    grad_logits = jnp.concatenate([grad_router, grad_gate[:, None]], axis=1).astype(BF)
    grad_normed_two = grad_sum[:, :width] + contract("tc,cd->td", grad_logits, router_rows)
    router_part = contract("tc,td->cd", grad_logits, normed_two)

    grad_after = grad_own.astype(F32) + norm_back(grad_normed_two, scaled_two, inverse_two, gain_two)
    gain_two_part = jnp.sum(grad_normed_two * scaled_two, axis=0)

    grad_attn = links.gather_seq(grad_after.astype(BF).reshape(micro, tok, width)).reshape(micro * seq, width)
    grad_lin = attend(normed_seq, wqkv, bias, tables, seq, (grad_attn, wo, qkv_seq))
    grad_normed_one = contract("tc,dc->td", grad_lin, wqkv).reshape(micro, n_fsdp, tok, width)
    grad_normed_one = links.sum_four([grad_normed_one[:, k] for k in range(4)]).reshape(own, width)
    in_grad = grad_after + norm_back(grad_normed_one, scaled_one, inverse_one, gain_one)
    gain_one_part = jnp.sum(grad_normed_one * scaled_one, axis=0)
    out_grad_part = contract("tc,td->cd", attended, grad_attn).astype(BF)
    qkv_part = contract("td,tc->dc", normed_seq, grad_lin).astype(BF)
    bias_part = jnp.sum(grad_lin.astype(F32), axis=0)

    qkv_sum = links.sum_rows(qkv_part.reshape(n_exp, n_fsdp * rows_w, 3 * wide)).astype(BF)
    qkv_own = from_fsdp(links.swap_fsdp(qkv_sum.reshape(n_fsdp, rows_w, 3 * wide))).astype(F32)
    if links.ring:
        halves = out_grad_part.reshape(heads_dev, 2, HEAD // 2, width)
        keep = lax.dynamic_index_in_dim(halves, core_f, 1, keepdims=False)
        got = links.partner(lax.dynamic_index_in_dim(halves, 1 - core_f, 1, keepdims=False), 1)
        rows = jnp.where(core_f == 0, jnp.concatenate([keep, got]), jnp.concatenate([got, keep]))
        out_own = links.sum_rows(rows)
    else:
        out_place = jnp.zeros((2, heads_dev, 2, HEAD, width), BF)
        out_place = lax.dynamic_update_slice(
            out_place, out_grad_part.reshape(1, heads_dev, 1, HEAD, width), (core_f, 0, half_f, 0, 0)
        )
        out_own = lax.psum_scatter(
            out_place.reshape(width, width), ALL, scatter_dimension=0, tiled=True
        ).astype(F32)
    bias_place = jnp.zeros((n_fsdp, 1, 3 * wide), F32)
    bias_place = from_fsdp(lax.dynamic_update_index_in_dim(bias_place, bias_part[None], my_fsdp, 0))[:, 0]
    small_part = jnp.concatenate([router_part, gain_one_part[None], gain_two_part[None], bias_place], axis=0)
    small_own = links.sum_small(small_part)

    grads = (wg_grad, wu_grad, wd_grad)
    shared_mine = jnp.concatenate(
        [grad[:tile_cols] for grad in grads] + [grad[tile_cols:sh_cols] for grad in grads], axis=0)
    shared_give = jnp.concatenate(
        [grad[sh_cols : sh_cols + tile_cols] for grad in grads]
        + [grad[sh_cols + tile_cols : 2 * sh_cols] for grad in grads], axis=0).astype(BF)
    shared_grads = (shared_mine + links.partner(shared_give, 2).astype(F32)).astype(BF)
    shared_own = lax.all_to_all(
        shared_grads.T.reshape(n_all, rows_w, 3 * sh_cols), ALL, split_axis=0, concat_axis=0, tiled=True
    )
    cut = 3 * tile_cols
    shared_own = [
        from_owner(
            shared_own[:, :, k * tile_cols : (k + 1) * tile_cols],
            shared_own[:, :, cut + k * rest_cols : cut + (k + 1) * rest_cols],
        ).astype(F32)
        for k in range(3)
    ]
    routed_grads = [
        grad[shared_units : shared_units + ex_cols]
        + links.partner(grad[shared_units + ex_cols : units].astype(BF), 2).astype(F32)
        for grad in grads
    ]
    return (
        hidden_out.reshape(micro, tok, width),
        in_grad.reshape(micro, tok, width),
        small_own[experts + 1],
        qkv_own[0],
        qkv_own[1],
        qkv_own[2],
        small_own[experts + 3 :],
        out_own,
        small_own[experts + 2],
        small_own[:experts].T,
        small_own[experts],
        shared_own[0],
        shared_own[1],
        shared_own[2],
        routed_grads[0].T[None],
        routed_grads[1].T[None],
        routed_grads[2][None],
    )


def solution(mesh):
    rows = P(ALL, None)
    tokens = P(None, ALL, None)
    in_specs = (
        tokens, P(None, ALL), tokens, tokens, P(ALL), rows, rows, rows, P(None, ALL), rows,
        P(ALL), rows, P(ALL), rows, rows, rows,
        P("expert", None, "fsdp"), P("expert", None, "fsdp"), P("expert", "fsdp", None),
    )
    out_specs = (
        tokens, tokens, P(ALL), rows, rows, rows, P(None, ALL), rows, P(ALL), rows, P(ALL),
        rows, rows, rows,
        P("expert", None, "fsdp"), P("expert", None, "fsdp"), P("expert", "fsdp", None),
    )
    return jax.shard_map(on_device, mesh=mesh, in_specs=in_specs, out_specs=out_specs, check_vma=False)
```

```python
import functools

import jax
import jax.numpy as jnp
from jax import lax
from jax.experimental import pallas as pl
from jax.experimental.pallas import tpu as pltpu
from jax.sharding import PartitionSpec as P

HEADS = 16
HEAD = 128
SHARED_FF = 5632
EPSILON = 1e-06
ROPE_BASE = 1000000.0
MASKED = -1e30
ALL = ("expert", "fsdp")
BF = jnp.bfloat16
F32 = jnp.float32
LANES = 128
COLS = 1024
GRAD_TILE = 384


def normalize(values):
    inverse = lax.rsqrt(jnp.mean(values * values, axis=-1, keepdims=True) + EPSILON)
    return (values * inverse, inverse)


def norm_back(grad_normed, scaled, inverse, gain_vec):
    grad_scaled = grad_normed * gain_vec
    return inverse * (grad_scaled - scaled * jnp.mean(grad_scaled * scaled, axis=-1, keepdims=True))


def angle_tables(places):
    inverse = 1.0 / ROPE_BASE ** (jnp.arange(0, HEAD, 2).astype(F32) / HEAD)
    angles = places.astype(F32)[:, None] * inverse[None, :]
    cosine, sine = jnp.cos(angles), jnp.sin(angles)
    return jnp.concatenate([cosine, cosine], axis=1), jnp.concatenate([-sine, sine], axis=1)


def silu_parts(pre_act):
    logistic = 1.0 / (1.0 + jnp.exp(-pre_act))
    return (pre_act * logistic, logistic * (1.0 + pre_act * (1.0 - logistic)))


def contract(pattern, left_op, right_op):
    return jnp.einsum(pattern, left_op, right_op, preferred_element_type=F32)


def dot_nt(left_op, right_op):
    return lax.dot_general(left_op, right_op, (((1,), (1,)), ((), ())), preferred_element_type=F32)


def dot_nn(left_op, right_op):
    return lax.dot_general(left_op, right_op, (((1,), (0,)), ((), ())), preferred_element_type=F32)


def dot_tn(left_op, right_op):
    return lax.dot_general(left_op, right_op, (((0,), (0,)), ((), ())), preferred_element_type=F32)


def after(value, *earlier):
    return lax.optimization_barrier((value, earlier))[0]


class Links:
    def __init__(self):
        self.n_exp = lax.axis_size("expert")
        self.n_fsdp = lax.axis_size("fsdp")
        self.my_exp = lax.axis_index("expert")
        self.my_fsdp = lax.axis_index("fsdp")
        self.n_all = self.n_exp * self.n_fsdp

    def partner(self, value, bit):
        pairs = [
            (e * self.n_fsdp + f, e * self.n_fsdp + (f ^ bit)) for e in range(self.n_exp) for f in range(self.n_fsdp)
        ]
        return lax.ppermute(value, ALL, pairs)

    def gather_rows(self, value):
        return lax.all_gather(value, "expert", axis=0)

    def sum_rows(self, value):
        return lax.psum_scatter(value.astype(BF), "expert", scatter_dimension=0).astype(F32)

    def swap_fsdp(self, value):
        result = value
        for bit in range(1, self.n_fsdp):
            other = lax.bitwise_xor(self.my_fsdp, bit)
            block = lax.dynamic_index_in_dim(value, other, 0, keepdims=False)
            result = lax.dynamic_update_index_in_dim(result, self.partner(block, bit), other, 0)
        return result

    def gather_four(self, value):
        far = self.partner(value, 2)
        return [value, self.partner(value, 1), far, self.partner(far, 1)]

    def gather_seq(self, value):
        return jnp.concatenate(self.gather_four(value), axis=1)

    def sum_four(self, parts):
        far = (parts[2].astype(F32) + self.partner(parts[3].astype(BF), 1).astype(F32)).astype(BF)
        near = parts[0].astype(F32) + self.partner(parts[1].astype(BF), 1).astype(F32)
        return near + self.partner(far, 2).astype(F32)


def attend_kernel(heads, seq, scale, x_ref, w_ref, bias_ref, cos_ref, sin_ref, place_ref, seg_ref,
                  place_row_ref, seg_row_ref, qkv_ref, out_ref):
    lin = dot_nn(x_ref[...], w_ref[...]) + bias_ref[...]
    cosine, sine = cos_ref[...], sin_ref[...]
    span = heads * HEAD
    for micro in range(x_ref.shape[0] // seq):
        low, high = micro * seq, (micro + 1) * seq
        visible = (place_row_ref[...] <= place_ref[...]) & (seg_row_ref[micro : micro + 1, :] == seg_ref[low:high, :])
        for head in range(heads):
            at = head * HEAD
            query = lin[low:high, at : at + HEAD]
            key = lin[low:high, span + at : span + at + HEAD]
            value = lin[low:high, 2 * span + at : 2 * span + at + HEAD].astype(BF)
            query = (query * cosine + pltpu.roll(query, HEAD // 2, 1) * sine).astype(BF)
            key = (key * cosine + pltpu.roll(key, HEAD // 2, 1) * sine).astype(BF)
            scores = jnp.where(visible, dot_nt(query, key) * scale, MASKED)
            exps = jnp.exp(scores - jnp.max(scores, axis=1, keepdims=True))
            probs = exps / jnp.sum(exps, axis=1, keepdims=True)
            out_ref[low:high, at : at + HEAD] = dot_nn(probs.astype(BF), value).astype(BF)
            qkv_ref[low:high, at : at + HEAD] = query
            qkv_ref[low:high, span + at : span + at + HEAD] = key
            qkv_ref[low:high, 2 * span + at : 2 * span + at + HEAD] = value


def attend_back_kernel(heads, seq, scale, grad_ref, wo_ref, qkv_ref, cos_ref, sin_ref, place_ref, seg_ref,
                       place_row_ref, seg_row_ref, w_ref, lin_ref, normed_ref):
    grad_out = dot_nt(grad_ref[...], wo_ref[...]).astype(BF)
    cosine, sine = cos_ref[...], sin_ref[...]
    span = heads * HEAD
    for micro in range(grad_ref.shape[0] // seq):
        low, high = micro * seq, (micro + 1) * seq
        visible = (place_row_ref[...] <= place_ref[...]) & (seg_row_ref[micro : micro + 1, :] == seg_ref[low:high, :])
        for head in range(heads):
            at = head * HEAD
            query = qkv_ref[low:high, at : at + HEAD]
            key = qkv_ref[low:high, span + at : span + at + HEAD]
            value = qkv_ref[low:high, 2 * span + at : 2 * span + at + HEAD]
            grad = grad_out[low:high, at : at + HEAD]
            scores = jnp.where(visible, dot_nt(query, key) * scale, MASKED)
            exps = jnp.exp(scores - jnp.max(scores, axis=1, keepdims=True))
            probs = exps / jnp.sum(exps, axis=1, keepdims=True)
            grad_probs = dot_nt(grad, value)
            grad_value = dot_tn(probs.astype(BF), grad)
            grad_scores = probs * (grad_probs - jnp.sum(probs * grad_probs, axis=1, keepdims=True))
            grad_scores = grad_scores.astype(BF)
            grad_query = dot_nn(grad_scores, key) * scale
            grad_key = dot_tn(grad_scores, query) * scale
            grad_query = grad_query * cosine - pltpu.roll(grad_query, HEAD // 2, 1) * sine
            grad_key = grad_key * cosine - pltpu.roll(grad_key, HEAD // 2, 1) * sine
            lin_ref[low:high, at : at + HEAD] = grad_query.astype(BF)
            lin_ref[low:high, span + at : span + at + HEAD] = grad_key.astype(BF)
            lin_ref[low:high, 2 * span + at : 2 * span + at + HEAD] = grad_value.astype(BF)
    part = dot_nt(lin_ref[...], w_ref[...])

    @pl.when(pl.program_id(0) == 0)
    def _():
        normed_ref[...] = part

    @pl.when(pl.program_id(0) > 0)
    def _():
        normed_ref[...] += part


def whole(shape):
    return pl.BlockSpec(shape, lambda *_: (0,) * len(shape))


def attend(normed, wqkv, bias, tables, seq, back=None):
    cosine, sine, place, seg, place_row, seg_row = tables
    rows = normed.shape[0]
    pairs = 2
    wide3 = bias.shape[1]
    heads = wide3 // 3 // HEAD // pairs
    span = heads * HEAD
    scale = HEAD ** (-0.5)
    common = (cosine, sine, place, seg, place_row, seg_row)
    common_specs = [whole(item.shape) for item in common]
    params = pltpu.CompilerParams(vmem_limit_bytes=40 * 2**20)
    if back is None:
        return pl.pallas_call(
            functools.partial(attend_kernel, heads, seq, scale),
            grid=(pairs,),
            in_specs=[
                whole(normed.shape),
                pl.BlockSpec((wqkv.shape[0], 3 * span), lambda p: (0, p)),
                pl.BlockSpec((1, 3 * span), lambda p: (0, p)),
            ] + common_specs,
            out_specs=[
                pl.BlockSpec((rows, 3 * span), lambda p: (0, p)),
                pl.BlockSpec((rows, span), lambda p: (0, p)),
            ],
            out_shape=[
                jax.ShapeDtypeStruct((rows, wide3), BF),
                jax.ShapeDtypeStruct((rows, wide3 // 3), BF),
            ],
            compiler_params=params,
            cost_estimate=pl.CostEstimate(flops=5 * 10**9, bytes_accessed=10**7, transcendentals=10**6),
            name="attend",
        )(normed, wqkv, bias, *common)
    grad, wo, qkv = back
    return pl.pallas_call(
        functools.partial(attend_back_kernel, heads, seq, scale),
        grid=(pairs,),
        in_specs=[
            whole(grad.shape),
            pl.BlockSpec((span, wo.shape[1]), lambda p: (p, 0)),
            pl.BlockSpec((rows, 3 * span), lambda p: (0, p)),
        ] + common_specs + [pl.BlockSpec((wqkv.shape[0], 3 * span), lambda p: (0, p))],
        out_specs=[pl.BlockSpec((rows, 3 * span), lambda p: (0, p)), whole((rows, wqkv.shape[0]))],
        out_shape=[jax.ShapeDtypeStruct((rows, wide3), BF), jax.ShapeDtypeStruct((rows, wqkv.shape[0]), F32)],
        compiler_params=params,
        cost_estimate=pl.CostEstimate(flops=5 * 10**9, bytes_accessed=10**7, transcendentals=10**6),
        name="attend_back",
    )(grad, wo, qkv, *common, wqkv)


def feed_kernel(experts, shared, expert_ref, *refs):
    x_refs, g_refs = refs[:4], refs[4:8]
    weights = (refs[8:11], refs[11:14])
    unit_refs, gn_refs, out_refs = refs[14:20], refs[20:24], refs[24:28]
    x_all, g_all = refs[28:30]
    units = (refs[30:33], refs[33:36])
    gn, out, sems = refs[36:]
    own, width = x_refs[0].shape
    rows = 4 * own
    expert = expert_ref[0]

    def block(k):
        return pl.ds(k * own, own)

    def start(number, source, target):
        copy = pltpu.make_async_copy(source, target, sems.at[number])
        copy.start()
        return copy

    x_copies = [start(k, x_refs[k], x_all.at[block(k), :]) for k in range(4)]
    g_copies = [start(4 + k, g_refs[k], g_all.at[block(k), :]) for k in range(4)]
    for copy in x_copies:
        copy.wait()
    gates = [dot_nt(x_all[...], weights[k][0][...]) for k in range(2)]
    for copy in g_copies:
        copy.wait()
    names = g_all[:, width:].astype(F32)
    lane = lax.broadcasted_iota(jnp.int32, names.shape, 1)
    hit = jnp.where((lane < 4) & (names == expert.astype(F32)), 1.0, 0.0)
    hit = jnp.sum(hit, axis=1, keepdims=True)
    first = shared // LANES * LANES
    logits = gates[0][:, first : first + LANES]
    lane = lane - (shared - first)
    is_expert = (lane >= 0) & (lane < experts)
    scores = jnp.where(is_expert, logits, MASKED)
    exps = jnp.where(is_expert, jnp.exp(scores - jnp.max(scores, axis=1, keepdims=True)), 0.0)
    mine = jnp.sum(jnp.where(lane == expert, exps, 0.0), axis=1, keepdims=True)
    mine = mine / jnp.sum(exps, axis=1, keepdims=True)
    last = jnp.sum(jnp.where(lane == experts, logits, 0.0), axis=1, keepdims=True)
    scales = (1.0 / (1.0 + jnp.exp(-last)), mine * hit)
    dots, copies = [], []
    for k in range(2):
        hs, dg, du = units[k]
        act, slope = silu_parts(gates[k])
        up = dot_nt(x_all[...], weights[k][1][...])
        grad = dot_nt(g_all[:, :width], weights[k][2][...])
        hidden = act * up
        dots.append(jnp.sum(hidden * grad, axis=1, keepdims=True))
        grad = grad * scales[k]
        hs[...] = (hidden * scales[k]).astype(BF)
        dg[...] = (grad * up * slope).astype(BF)
        du[...] = (grad * act).astype(BF)
        copies += [
            start(3 * k + j, source, target) for j, (source, target) in enumerate(zip((hs, dg, du), unit_refs[3 * k :]))
        ]
    lane = lax.broadcasted_iota(jnp.int32, (rows, LANES), 1)
    extra = jnp.where(lane == expert, dots[1] * hit, 0.0) + jnp.where(lane == experts, dots[0], 0.0)
    gn[:, width:] = extra.astype(BF)
    total = dot_nn(units[0][1][...], weights[0][0][...]) + dot_nn(units[0][2][...], weights[0][1][...])
    total += dot_nn(units[1][1][...], weights[1][0][...]) + dot_nn(units[1][2][...], weights[1][1][...])
    gn[:, :width] = total.astype(BF)
    copies += [start(6 + k, gn.at[block(k), :], gn_refs[k]) for k in range(4)]
    total = dot_nn(units[0][0][...], weights[0][2][...]) + dot_nn(units[1][0][...], weights[1][2][...])
    out[...] = total.astype(BF)
    copies += [start(10 + k, out.at[block(k), :], out_refs[k]) for k in range(4)]
    for copy in copies:
        copy.wait()


def feed(expert, x_blocks, g_blocks, shared_w, routed_w, experts, shared):
    own, width = x_blocks[0].shape
    rows = 4 * own
    wide = g_blocks[0].shape[1]
    counts = (shared_w[0].shape[0], routed_w[0].shape[0])
    anywhere = pl.BlockSpec(memory_space=pl.ANY)
    weights = [pltpu.with_memory_space_constraint(weight, pltpu.VMEM) for weight in (*shared_w, *routed_w)]
    found = pl.pallas_call(
        functools.partial(feed_kernel, experts, shared),
        in_specs=[pl.BlockSpec(memory_space=pltpu.SMEM)]
        + [anywhere] * 8
        + [pl.BlockSpec(memory_space=pltpu.VMEM)] * 6,
        out_specs=[anywhere] * 14,
        scratch_shapes=[pltpu.VMEM((rows, width), BF), pltpu.VMEM((rows, wide), BF)]
        + [pltpu.VMEM((rows, count), BF) for count in counts for _ in range(3)]
        + [pltpu.VMEM((rows, wide), BF), pltpu.VMEM((rows, width), BF), pltpu.SemaphoreType.DMA((14,))],
        out_shape=[jax.ShapeDtypeStruct((rows, count), BF) for count in counts for _ in range(3)]
        + [jax.ShapeDtypeStruct((own, wide), BF)] * 4
        + [jax.ShapeDtypeStruct((own, width), BF)] * 4,
        compiler_params=pltpu.CompilerParams(vmem_limit_bytes=42 * 2**20),
        cost_estimate=pl.CostEstimate(flops=16 * 10**9, bytes_accessed=3 * 10**7, transcendentals=10**6),
        name="feed",
    )(expert, *x_blocks, *g_blocks, *weights)
    return found[:3], found[3:6], found[6:10], found[10:14]


def join_kernel(cuts, y_ref, mine_ref, low_ref, high_ref, behind_ref, *out_refs):
    half = low_ref.shape[0]
    for k, pieces in enumerate(cuts):
        at = 0
        for low, count in pieces:
            for block in range(mine_ref.shape[1] // LANES):
                columns = slice(block * LANES, (block + 1) * LANES)
                target = pl.ds(pl.multiple_of((2 * block + y_ref[0]) * LANES, LANES), LANES)
                out_refs[k][at : at + count, target] = mine_ref[low : low + count, columns]
                target = pl.ds(pl.multiple_of((2 * block + 1 - y_ref[0]) * LANES, LANES), LANES)
                middle = min(max(half - low, 0), count)
                if middle:
                    out_refs[k][at : at + middle, target] = low_ref[low : low + middle, columns]
                if middle < count:
                    begin = low + middle - half
                    out_refs[k][at + middle : at + count, target] = high_ref[begin : begin + count - middle, columns]
            at += count
        rest = out_refs[k].shape[0] - at
        out_refs[k][at:, :] = behind_ref[...] if k == 0 else jnp.zeros((rest, out_refs[k].shape[1]), BF)


def join_shared(y, mine, low, high, behind, cuts):
    rows = sum(count for _, count in cuts[0]) + behind.shape[0]
    vmem = pl.BlockSpec(memory_space=pltpu.VMEM)
    return pl.pallas_call(
        functools.partial(join_kernel, cuts),
        in_specs=[pl.BlockSpec(memory_space=pltpu.SMEM)] + [vmem] * 4,
        out_specs=[vmem] * 3,
        out_shape=[jax.ShapeDtypeStruct((rows, 2 * mine.shape[1]), BF)] * 3,
        compiler_params=pltpu.CompilerParams(vmem_limit_bytes=24 * 2**20),
        cost_estimate=pl.CostEstimate(flops=0, bytes_accessed=10**7, transcendentals=0),
        name="join_shared",
    )(y, mine, low, high, behind)


def weights_kernel(n_sets, split, y_ref, *refs):
    sources, lhs_refs = refs[:16], refs[16 : 16 + 4 * n_sets]
    out_refs, (held, sems) = refs[16 + 4 * n_sets : -2], refs[-2:]
    rows, width = held.shape
    own = rows // 16

    @pl.when(pl.program_id(0) == 0)
    def _():
        copies = [
            pltpu.make_async_copy(
                sources[k].at[:, pl.ds(0, width)], held.at[pl.ds(k * own, own), :], sems.at[k])
            for k in range(16)
        ]
        for copy in copies:
            copy.start()
        for copy in copies:
            copy.wait()

    for k in range(n_sets):
        lhs = jnp.concatenate([ref[...] for ref in lhs_refs[4 * k : 4 * k + 4]], axis=0)
        total = dot_tn(lhs, held[...])
        if not split:
            out_refs[k][...] = total.astype(BF)
            continue
        for block in range(width // LANES // 2):
            even = total[:, 2 * block * LANES : (2 * block + 1) * LANES]
            odd = total[:, (2 * block + 1) * LANES : (2 * block + 2) * LANES]
            columns = slice(block * LANES, (block + 1) * LANES)
            out_refs[2 * k][:, columns] = jnp.where(y_ref[0] == 0, even, odd).astype(BF)
            out_refs[2 * k + 1][:, columns] = jnp.where(y_ref[0] == 0, odd, even).astype(BF)


def weight_grads(y, sources, lhs_sets, width, split=False):
    rows, units = lhs_sets[0][0].shape
    n_sets = len(lhs_sets)
    n_tiles = units // GRAD_TILE
    columns = width // 2 if split else width
    n_outs = 2 * n_sets if split else n_sets
    return pl.pallas_call(
        functools.partial(weights_kernel, n_sets, split),
        grid=(n_tiles,),
        in_specs=[pl.BlockSpec(memory_space=pltpu.SMEM)]
        + [pl.BlockSpec(memory_space=pl.ANY)] * 16
        + [pl.BlockSpec((rows, GRAD_TILE), lambda i: (0, i))] * (4 * n_sets),
        out_specs=[pl.BlockSpec((GRAD_TILE, columns), lambda i: (i, 0))] * n_outs,
        scratch_shapes=[pltpu.VMEM((4 * rows, width), BF), pltpu.SemaphoreType.DMA((16,))],
        out_shape=[jax.ShapeDtypeStruct((units, columns), BF)] * n_outs,
        compiler_params=pltpu.CompilerParams(vmem_limit_bytes=36 * 2**20),
        cost_estimate=pl.CostEstimate(
            flops=4 * 10**9 * n_sets * n_tiles, bytes_accessed=2 * 10**7, transcendentals=0),
        name="weight_grads",
    )(y, *sources, *[item for lhs in lhs_sets for item in lhs])


def feed_plain(normed, grad, named, expert, wg, wu, wd, router, experts, shared):
    logits = contract("td,cd->tc", normed, router)
    router_probs = jax.nn.softmax(logits[:, :experts], axis=-1)
    shared_scale = jax.nn.sigmoid(logits[:, experts : experts + 1])
    hot = (jnp.arange(experts) == expert).astype(F32)
    gate_here = jnp.sum(router_probs * hot, axis=1, keepdims=True) * named[:, None]
    is_shared = (jnp.arange(wg.shape[0]) < shared)[None]
    row_scale = jnp.where(is_shared, shared_scale, gate_here)
    act, slope = silu_parts(contract("td,cd->tc", normed, wg))
    up = contract("td,cd->tc", normed, wu)
    hidden = act * up
    hidden_scaled = (hidden * row_scale).astype(BF)
    grad_hidden = contract("td,fd->tf", grad, wd)
    dots = hidden * grad_hidden
    dot_shared = jnp.sum(jnp.where(is_shared, dots, 0.0), axis=1, keepdims=True)
    dot_expert = jnp.sum(jnp.where(is_shared, 0.0, dots), axis=1, keepdims=True) * named[:, None]
    grad_pre = grad_hidden * row_scale
    grad_gate = (grad_pre * up * slope).astype(BF)
    grad_up = (grad_pre * act).astype(BF)
    grad_normed = contract("tc,cd->td", grad_gate, wg) + contract("tc,cd->td", grad_up, wu)
    extra = jnp.concatenate([dot_expert * hot, dot_shared], axis=1)
    extra = jnp.pad(extra, ((0, 0), (0, LANES - extra.shape[1])))
    out = contract("tf,fd->td", hidden_scaled, wd)
    return (
        jnp.concatenate([grad_normed, extra], axis=1),
        out,
        contract("tc,td->cd", grad_gate, normed),
        contract("tc,td->cd", grad_up, normed),
        contract("tf,td->fd", hidden_scaled, grad),
    )


def ring_perm(move):
    pairs = []
    for me in range(32):
        z, x, y, c = me // 8, me // 4 % 2, me // 2 % 2, me % 2
        z, x, y, c = move(z, x, y, c)
        pairs.append((me, ((z * 2 + x) * 2 + y) * 2 + c))
    return pairs


MOVES = {
    "core": lambda z, x, y, c: (z, x, y, 1 - c),
    "y": lambda z, x, y, c: (z, x, 1 - y, c),
    "yc": lambda z, x, y, c: (z, x, 1 - y, 1 - c),
    "x": lambda z, x, y, c: (z, 1 - x, y, c),
    "z1": lambda z, x, y, c: ((z + 1) % 4, x, y, c),
    "z2": lambda z, x, y, c: ((z + 2) % 4, x, y, c),
    "z3": lambda z, x, y, c: ((z + 3) % 4, x, y, c),
}


def send(value, link):
    return lax.ppermute(value, ALL, ring_perm(MOVES[link]))


def sync(*values):
    return lax.optimization_barrier(values)


def pick(value, place, axis=0):
    return lax.dynamic_index_in_dim(value, place, axis, keepdims=False)


def put(value, block, place, axis=0):
    return lax.dynamic_update_index_in_dim(value, block, place, axis)


def in_order(mine, other, bit, axis):
    return jnp.where(bit == 0, jnp.stack([mine, other], axis=axis), jnp.stack([other, mine], axis=axis))


def on_device_ring(
    hidden_in, seg_ids, routes, out_grad, norm_gain1, w_query, w_key, w_value, b_qkv, w_out,
    norm_gain2, w_router, shared_gate, sh_gate, sh_up, sh_down, ex_gate, ex_up, ex_down,
):
    micro, tok, width = hidden_in.shape
    experts = w_router.shape[1]
    rows_w = w_query.shape[0]
    top_count = routes.shape[2]
    my_exp, my_fsdp = lax.axis_index("expert"), lax.axis_index("fsdp")
    z, x, y, c = my_exp // 2, lax.rem(my_exp, 2), my_fsdp // 2, lax.rem(my_fsdp, 2)
    n_exp, n_fsdp, n_all = 8, 4, 32
    heads_dev = HEADS // n_fsdp
    wide = heads_dev * HEAD
    seq, own = tok * n_fsdp, micro * tok
    ex_cols = ex_gate.shape[2]
    sh_cols = SHARED_FF // 16
    full_cols = sh_cols // LANES * LANES
    rest_cols = sh_cols - full_cols
    unit_cols = 3 * sh_cols

    def slot(step, other):
        return lax.rem(z + 4 - step, 4) * 2 + (1 - x if other else x)

    def by_fsdp(three):
        rows = three.shape[0]
        split = three.reshape(rows, 3, 2, 2, heads_dev // 2, 2, HEAD)
        return split.transpose(5, 2, 0, 3, 1, 4, 6).reshape(n_fsdp, rows, 3 * wide)

    def from_fsdp(blocks):
        rows = blocks.shape[1]
        split = blocks.reshape(2, 2, rows, 2, 3, heads_dev // 2, HEAD)
        return split.transpose(4, 2, 1, 3, 5, 0, 6).reshape(3, rows, width)

    small = jnp.concatenate([w_router.T, shared_gate[None], norm_gain1[None], norm_gain2[None], b_qkv], axis=0)
    n_small = small.shape[0]
    small = [small.reshape(1, n_small * rows_w)]
    for _ in range(3):
        small.append(send(small[-1], "z1"))
    small = jnp.concatenate(small)
    qkv = by_fsdp(jnp.stack([w_query, w_key, w_value], axis=1))
    arrived = [send(pick(qkv, lax.bitwise_xor(my_fsdp, k)), link) for k, link in ((1, "core"), (2, "y"), (3, "yc"))]
    seg_near, seg_far = send(seg_ids, "core"), send(seg_ids, "y")
    grad_own = out_grad.reshape(own, width)
    names = jnp.pad(routes.reshape(own, top_count).astype(BF), ((0, 0), (0, LANES - top_count)))
    g_own = [jnp.concatenate([grad_own, names], axis=1)]
    g_pair = []
    routed_mine = jnp.concatenate([ex_gate[0].T, ex_up[0].T, ex_down[0]], axis=0)
    small, arrived, g_own[0], seg_near, seg_far, routed_mine = sync(
        small, arrived, g_own[0], seg_near, seg_far, routed_mine)
    for k in range(3):
        qkv = put(qkv, arrived[k], lax.bitwise_xor(my_fsdp, k + 1))
    block = jnp.concatenate(
        [qkv.reshape(n_fsdp * rows_w, 3 * wide), w_out.reshape(rows_w, n_fsdp, wide).reshape(-1, wide)], axis=1)

    following = send(block, "z1")
    small = jnp.concatenate([small, send(small, "x")])
    at_pair = send(sync(block, small)[0], "x")
    small = jnp.concatenate([small, send(small, "y")])
    small = jnp.concatenate([small, send(small, "core")])
    places = jnp.stack(
        [slot(step, other) * 4 + lax.bitwise_xor(my_fsdp, k) for k in (0, 2, 1, 3) for other in range(2) for step in range(4)])
    choice = (jnp.arange(n_all)[:, None] == places[None]).astype(BF)
    small = dot_nn(choice, small).astype(BF).reshape(n_all, n_small, rows_w).transpose(1, 0, 2).reshape(n_small, width)
    router_rows = small[: experts + 1]
    gain_one = small[experts + 1].astype(F32)
    gain_two = small[experts + 2].astype(F32)
    bias = pick(by_fsdp(small[experts + 3 :].astype(F32)[None]), my_fsdp)
    hidden = hidden_in.reshape(own, width).astype(F32)
    scaled_one, inverse_one = normalize(hidden)
    normed_one = (scaled_one * gain_one).astype(BF).reshape(micro, tok, width)
    seq_far, seq_near = send(normed_one, "y"), send(normed_one, "core")
    seg_last = send(seg_far, "core")
    weights = jnp.zeros((n_exp,) + block.shape, BF)
    weights = put(weights, block, slot(0, 0))

    def ring_put(weights, step, mine, other):
        return put(put(weights, mine, slot(step, 0)), other, slot(step, 1))

    a_blocks = [routed_mine[k * 264 : (k + 1) * 264] for k in range(4)]
    got_blocks = []
    current = following
    (current, at_pair, seq_far, seq_near, seg_last, normed_one, a_blocks, bias, router_rows) = sync(
        current, at_pair, seq_far, seq_near, seg_last, normed_one, a_blocks, bias, router_rows)
    weights = put(weights, at_pair, slot(0, 1))
    seq_last = send(seq_far, "core")

    def by_owner(weight):
        full = weight[:, : 16 * full_cols].reshape(rows_w, 16, full_cols).transpose(1, 0, 2)
        rest = weight[:, 16 * full_cols :].reshape(rows_w, 16, rest_cols).transpose(1, 0, 2)
        return full, rest

    pieces = [by_owner(weight) for weight in (sh_gate, sh_up, sh_down)]
    shared_w = jnp.concatenate([piece[0] for piece in pieces] + [piece[1] for piece in pieces], axis=2)
    shared_w = shared_w.reshape(4, 2, 2, rows_w, unit_cols)

    def swap_core(blocks):
        mine, give = pick(blocks, c, 2), pick(blocks, 1 - c, 2)
        return in_order(mine, send(give, "core"), c, 2)

    def swap_z(blocks, k):
        return send(pick(blocks, lax.rem(z + k, 4)), f"z{k}")

    def swap_x(blocks):
        mine, give = pick(blocks, x, 1), pick(blocks, 1 - x, 1)
        return in_order(mine, send(give, "x"), x, 1)

    for step in (1, 2):
        at_pair = send(current, "x")
        following = send(current, "z1")
        got = send(a_blocks[step - 1], "y")
        if step == 2:
            shared_w = swap_core(shared_w)
        mine = current
        current, at_pair, got, mine, a_blocks, shared_w, seq_last = sync(
            following, at_pair, got, mine, a_blocks, shared_w, seq_last)
        got_blocks.append(got)
        weights = ring_put(weights, step, mine, at_pair)

    at_pair = send(current, "x")
    got = send(a_blocks[2], "y")
    shared_z = {1: swap_z(shared_w, 1), 3: swap_z(shared_w, 3)}
    current, at_pair, got, shared_z, shared_w, a_blocks, weights = sync(
        current, at_pair, got, shared_z, shared_w, a_blocks, weights)
    got_blocks.append(got)
    weights = ring_put(weights, 3, current, at_pair)

    got = send(a_blocks[3], "y")
    shared_z[2] = swap_z(shared_w, 2)
    wo_rows = weights[:, :, 3 * wide :].reshape(n_exp, rows_w, width)
    keep = lax.dynamic_slice_in_dim(wo_rows, 4 * c, 4, 0)
    arrived = send(lax.dynamic_slice_in_dim(wo_rows, 4 * (1 - c), 4, 0), "core")
    wo = in_order(keep, arrived, c, 1).reshape(wide, width)
    weights = weights.reshape(width, 4 * wide)
    order = lax.bitwise_xor(my_fsdp, jnp.arange(n_fsdp))
    places = (order[:, None] * tok + jnp.arange(tok)[None]).reshape(seq)
    seg_seq = jnp.concatenate([seg_ids, seg_near, seg_far, seg_last], axis=1)
    normed_seq = jnp.concatenate([normed_one, seq_near, seq_far, seq_last], axis=1).reshape(micro * seq, width)
    cosine, sine = angle_tables(places)
    tables = (cosine, sine, places[:, None], seg_seq.reshape(micro * seq, 1), places[None], seg_seq)
    weights, wo, tables, normed_seq, got, shared_z, shared_w, g_own[0] = sync(
        weights, wo, tables, normed_seq, got, shared_z, shared_w, g_own[0])
    got_blocks.append(got)
    for k in (1, 2, 3):
        shared_w = put(shared_w, shared_z[k], lax.rem(z + 4 - k, 4))
    shared_w = swap_x(shared_w)
    g_own.append(send(g_own[0], "z1"))
    qkv_seq, attended = attend(normed_seq, weights, bias, tables, seq)
    attn_part = contract("tc,cd->td", attended, wo).reshape(micro, n_fsdp, tok, width)
    last = (attn_part[:, 2] + send(attn_part[:, 3].astype(BF), "core").astype(F32)).astype(BF)
    near = attn_part[:, 0] + send(attn_part[:, 1].astype(BF), "core").astype(F32)
    last, near, shared_w, g_own, got_blocks = sync(last, near, shared_w, g_own, got_blocks)

    last = send(last, "y")
    g_pair.append(send(g_own[0], "x"))
    g_own.append(send(g_own[1], "z1"))
    shared_w = shared_w.reshape(16 * rows_w, unit_cols).T
    after_attn = hidden + near.reshape(own, width) + last.astype(F32).reshape(own, width)
    scaled_two, inverse_two = normalize(after_attn)
    normed_two = (scaled_two * gain_two).astype(BF)
    x_own, x_pair = [normed_two], []
    shared_w, x_own, after_attn, scaled_two, g_own, g_pair, got_blocks = sync(
        shared_w, x_own, after_attn, scaled_two, g_own, g_pair, got_blocks)

    half = unit_cols // 2
    arrived = [send(shared_w[:half], "y")]
    x_pair.append(send(x_own[0], "x"))
    g_pair.append(send(g_own[1], "x"))
    x_own.append(send(x_own[0], "z1"))
    g_own.append(send(g_own[2], "z1"))
    routed_other = jnp.concatenate(got_blocks, axis=0)
    pad = jnp.zeros((2 * GRAD_TILE - 2 * ex_cols, width), BF)
    routed_w = [
        jnp.concatenate(
            [routed_mine[k * ex_cols : (k + 1) * ex_cols], routed_other[k * ex_cols : (k + 1) * ex_cols], pad], axis=0)
        for k in range(3)
    ]

    def four(mine, other):
        return [mine, other, send(mine, "core"), send(other, "core")]

    arrived, shared_w, x_own, g_own, x_pair, g_pair, routed_w = sync(
        arrived, shared_w, x_own, g_own, x_pair, g_pair, routed_w)
    arrived.append(send(shared_w[half:], "y"))
    x_pair.append(send(x_own[1], "x"))
    g_pair.append(send(g_own[2], "x"))
    x_own.append(send(x_own[1], "z1"))
    x_four, g_four = [four(x_own[0], x_pair[0])], [four(g_own[k], g_pair[k]) for k in range(2)]
    behind = jnp.pad(router_rows, ((0, GRAD_TILE - sh_cols - experts - 1), (0, 0)))
    arrived, shared_w, x_four, g_four, x_own, g_own, x_pair, g_pair, routed_w, behind = sync(
        arrived, shared_w, x_four, g_four, x_own, g_own, x_pair, g_pair, routed_w, behind)
    rest_at = 3 * full_cols
    cuts = [
        [(k * full_cols, full_cols), (rest_at + k * rest_cols, rest_cols)] for k in range(3)
    ]
    y_place = y.reshape(1)
    shared_w = join_shared(y_place, shared_w, arrived[0], arrived[1], behind, cuts)
    g_pair.append(send(g_own[3], "x"))
    x_four.append(four(x_own[1], x_pair[1]))
    g_four.append(four(g_own[2], g_pair[2]))

    expert = my_exp.reshape(1)
    fed, near_sums, sums = [], [], []

    def core_sums(found):
        return [found[k].astype(F32) + send(found[2 + k], "core").astype(F32) for k in range(2)]

    def pair_sums(parts):
        return parts[0] + send(parts[1].astype(BF), "x").astype(F32)

    for step in range(4):
        shared_w, routed_w, x_four, g_four, x_own, x_pair, g_pair, near_sums, sums, fed = sync(
            shared_w, routed_w, x_four, g_four, x_own, x_pair, g_pair, near_sums, sums, fed)
        if step == 0:
            x_pair.append(send(x_own[2], "x"))
            x_own.append(send(x_own[2], "z1"))
            g_four.append(four(g_own[3], g_pair[3]))
        if step == 1:
            x_pair.append(send(x_own[3], "x"))
            x_four.append(four(x_own[2], x_pair[2]))
        if step == 2:
            x_four.append(four(x_own[3], x_pair[3]))
        if step >= 1:
            near_sums.append(core_sums(fed[step - 1][2]))
        if step >= 2:
            sums.append(pair_sums(near_sums[step - 2]))
        fed.append(feed(expert, x_four[step], g_four[step], shared_w, routed_w, experts, sh_cols))
    near_sums, sums, fed, x_four, g_four = sync(near_sums, sums, fed, x_four, g_four)

    x_blocks = [item for four_of in x_four for item in four_of]
    g_blocks = [item for four_of in g_four for item in four_of]
    shared_sets = [[fed[step][0][item] for step in range(4)] for item in range(3)]
    routed_sets = [[fed[step][1][item] for step in range(4)] for item in range(3)]
    flying = send(sums[1].astype(BF), "z1")
    sums.append(pair_sums(near_sums[2]))
    near_sums.append(core_sums(fed[3][2]))
    sg_mine, sg_give, su_mine, su_give = weight_grads(y_place, x_blocks, [shared_sets[1], shared_sets[2]], width, True)
    sums, near_sums, flying, sg_mine, sg_give, su_mine, su_give, x_blocks, g_blocks, shared_sets, routed_sets = sync(
        sums, near_sums, flying, sg_mine, sg_give, su_mine, su_give, x_blocks, g_blocks, shared_sets, routed_sets)
    sums.append(pair_sums(near_sums[3]))
    flying = send((sums[2] + flying.astype(F32)).astype(BF), "z1")
    sg_got = send(sg_give, "y")
    sd_mine, sd_give = weight_grads(y_place, g_blocks, [shared_sets[0]], width, True)
    (ed_grad,) = weight_grads(y_place, g_blocks, [routed_sets[0]], width)
    sums, flying, sg_got, su_give, sd_mine, sd_give, ed_grad, x_blocks, routed_sets, fed = sync(
        sums, flying, sg_got, su_give, sd_mine, sd_give, ed_grad, x_blocks, routed_sets, fed)
    flying = send((sums[3] + flying.astype(F32)).astype(BF), "z1")
    su_got = send(su_give, "y")
    out_near = [core_sums(fed[step][3]) for step in range(4)]
    grad_sum, out_near, su_got, sd_give, x_blocks, routed_sets, ed_grad = sync(
        sums[0] + flying.astype(F32), out_near, su_got, sd_give, x_blocks, routed_sets, ed_grad)

    own_logits = contract("td,cd->tc", normed_two, router_rows)
    own_probs = jax.nn.softmax(own_logits[:, :experts], axis=-1)
    own_scale = jax.nn.sigmoid(own_logits[:, experts])
    grad_probs = grad_sum[:, width : width + experts]
    grad_router = own_probs * (grad_probs - jnp.sum(own_probs * grad_probs, axis=-1, keepdims=True))
    grad_gate = grad_sum[:, width + experts] * own_scale * (1.0 - own_scale)
    grad_logits = jnp.concatenate([grad_router, grad_gate[:, None]], axis=1).astype(BF)
    grad_normed_two = grad_sum[:, :width] + contract("tc,cd->td", grad_logits, router_rows)
    router_part = contract("tc,td->cd", grad_logits, normed_two)
    grad_after = grad_own.astype(F32) + norm_back(grad_normed_two, scaled_two, inverse_two, gain_two)
    gain_two_part = jnp.sum(grad_normed_two * scaled_two, axis=0)
    low = grad_after.astype(BF).reshape(micro, tok, width)
    sd_got = send(sd_give, "y")
    out_sums = [pair_sums(out_near[0])]
    low, grad_after, out_sums, out_near, sd_got, x_blocks, routed_sets, ed_grad = sync(
        low, grad_after, out_sums, out_near, sd_got, x_blocks, routed_sets, ed_grad)
    far, near = send(low, "y"), send(low, "core")
    out_sums.append(pair_sums(out_near[1]))
    eg_grad, eu_grad = weight_grads(y_place, x_blocks, [routed_sets[1], routed_sets[2]], width)
    shared_grads = [
        (mine.astype(F32) + got.astype(F32)).astype(BF)
        for mine, got in ((sg_mine, sg_got), (su_mine, su_got), (sd_mine, sd_got))
    ]
    shared_grads = jnp.concatenate(
        [grad[:full_cols] for grad in shared_grads] + [grad[full_cols:sh_cols] for grad in shared_grads], axis=0)
    shared_grads = shared_grads.T.reshape(4, 2, 2, rows_w, unit_cols)
    far, near, low, grad_after, out_sums, out_near, eg_grad, eu_grad, ed_grad, shared_grads = sync(
        far, near, low, grad_after, out_sums, out_near, eg_grad, eu_grad, ed_grad, shared_grads)

    e_grads = (eg_grad, eu_grad, ed_grad)
    e_give = jnp.concatenate([grad[ex_cols : 2 * ex_cols] for grad in e_grads], axis=0)
    e_got = []
    shared_grads = swap_core(shared_grads)
    grad_attn = jnp.concatenate([low, near, far, send(far, "core")], axis=1).reshape(micro * seq, width)
    grad_lin, grad_normed_one = attend(normed_seq, weights, bias, tables, seq, (grad_attn, wo, qkv_seq))
    gain_one_part = jnp.sum(grad_normed_one * normed_seq.astype(F32), axis=0) / gain_one
    parts = grad_normed_one.reshape(micro, n_fsdp, tok, width)
    last = (parts[:, 2] + send(parts[:, 3].astype(BF), "core").astype(F32)).astype(BF)
    near = parts[:, 0] + send(parts[:, 1].astype(BF), "core").astype(F32)
    out_sums.append(pair_sums(out_near[2]))
    flying = send(out_sums[1].astype(BF), "z1")
    out_grad_part = contract("tc,td->cd", attended, grad_attn).astype(BF)
    split = out_grad_part.reshape(heads_dev, 2, HEAD // 2, width)
    keep = pick(split, c, 1)
    arrived = send(pick(split, 1 - c, 1), "core")
    wo_part = jnp.where(c == 0, jnp.concatenate([keep, arrived]), jnp.concatenate([arrived, keep]))
    grad_lin, gain_one_part, last, near, out_sums, out_near, flying, shared_grads, e_give, wo_part = sync(
        grad_lin, gain_one_part, last, near, out_sums, out_near, flying, shared_grads, e_give, wo_part)

    def panel_sum(panel, step):
        return pick(panel, slot(step, 0)).astype(F32) + send(pick(panel, slot(step, 1)), "x").astype(F32)

    far = send(last, "y")
    shared_z = {1: swap_z(shared_grads, 1), 3: swap_z(shared_grads, 3)}
    out_sums.append(pair_sums(out_near[3]))
    wo_sums = {step: panel_sum(wo_part, step) for step in (1, 2)}
    qkv_part = contract("td,tc->dc", normed_seq, grad_lin).astype(BF)
    bias_place = put(jnp.zeros((n_fsdp, 1, 3 * wide), F32), jnp.sum(grad_lin.astype(F32), axis=0)[None], my_fsdp)
    bias_place = from_fsdp(bias_place)[:, 0]
    small_part = jnp.concatenate([router_part, gain_one_part[None], gain_two_part[None], bias_place], axis=0)
    small_part = small_part.astype(BF).reshape(n_small, n_exp, n_fsdp, rows_w).transpose(1, 2, 0, 3)
    small_part = small_part.reshape(n_exp, n_fsdp * n_small * rows_w)
    behind_rows = 8
    small_part = jnp.pad(small_part, ((0, 0), (0, behind_rows * 3 * wide - small_part.shape[1])))
    panel = qkv_part.reshape(n_exp, n_fsdp * rows_w, 3 * wide)
    panel = jnp.concatenate([panel, small_part.reshape(n_exp, behind_rows, 3 * wide)], axis=1)
    far, out_sums, flying, panel, near, shared_z, shared_grads, wo_sums, wo_part, e_give = sync(
        far, out_sums, flying, panel, near, shared_z, shared_grads, wo_sums, wo_part, e_give)
    grad_normed_one = (near + far.astype(F32)).reshape(own, width)
    in_grad = grad_after + norm_back(grad_normed_one, scaled_one, inverse_one, gain_one)

    sums = {}
    for turn, step in enumerate((1, 2, 3, 0)):
        sums[step] = panel_sum(panel, step)
        e_got.append(send(e_give[turn * 264 : (turn + 1) * 264], "y"))
        if turn == 0:
            shared_z[2] = swap_z(shared_grads, 2)
            flying_out = send((out_sums[2] + flying.astype(F32)).astype(BF), "z1")
        elif turn == 1:
            for k in (1, 2, 3):
                shared_grads = put(shared_grads, shared_z[k], lax.rem(z + 4 - k, 4))
            flying = send(sums[1].astype(BF), "z1")
            flying_out = send((out_sums[3] + flying_out.astype(F32)).astype(BF), "z1")
            flying_wo = send(wo_sums[1].astype(BF), "z1")
            wo_sums[3] = panel_sum(wo_part, 3)
            shared_x = [send(pick(shared_grads, 1 - x, 1)[:2], "x")]
        elif turn == 2:
            flying = send((sums[2] + flying.astype(F32)).astype(BF), "z1")
            flying_wo = send((wo_sums[2] + flying_wo.astype(F32)).astype(BF), "z1")
            wo_sums[0] = panel_sum(wo_part, 0)
            shared_x.append(send(pick(shared_grads, 1 - x, 1)[2:], "x"))
        else:
            flying = send((sums[3] + flying.astype(F32)).astype(BF), "z1")
            flying_wo = send((wo_sums[3] + flying_wo.astype(F32)).astype(BF), "z1")
            shared_grads = in_order(pick(shared_grads, x, 1), jnp.concatenate(shared_x), x, 1)
        if turn == 0:
            sums, e_got, shared_z, shared_grads, e_give, panel, flying_out, wo_part = sync(
                sums, e_got, shared_z, shared_grads, e_give, panel, flying_out, wo_part)
        elif turn < 3:
            sums, e_got, shared_x, shared_grads, flying, e_give, panel, flying_out, flying_wo, wo_sums, wo_part = sync(
                sums, e_got, shared_x, shared_grads, flying, e_give, panel, flying_out, flying_wo, wo_sums, wo_part)
    hidden_out = (after_attn + out_sums[0] + flying_out.astype(F32)).astype(BF)
    out_own = wo_sums[0] + flying_wo.astype(F32)
    total = (sums[0] + flying.astype(F32)).astype(BF)

    total, shared_grads, e_got = sync(total, shared_grads, e_got)
    count = n_fsdp * rows_w
    small_sum = total[count:].reshape(-1)[: n_fsdp * n_small * rows_w].reshape(n_fsdp, n_small * rows_w)
    small_sum = jnp.pad(small_sum, ((0, 0), (0, 3 * wide - n_small * rows_w)))
    blocks = jnp.concatenate([total[:count, : 3 * wide].reshape(n_fsdp, rows_w, 3 * wide), small_sum[:, None]], axis=1)
    qkv_own = blocks
    for k, link in ((1, "core"), (2, "y"), (3, "yc")):
        place = lax.bitwise_xor(my_fsdp, k)
        qkv_own = put(qkv_own, send(pick(blocks, place), link), place)
    small_own = jnp.sum(qkv_own[:, rows_w, : n_small * rows_w].astype(F32), axis=0).reshape(n_small, rows_w)
    qkv_own = from_fsdp(qkv_own[:, :rows_w]).astype(F32)
    shared_grads = shared_grads.reshape(16, rows_w, unit_cols)

    def from_owner(k):
        full = shared_grads[:, :, k * full_cols : (k + 1) * full_cols]
        rest = shared_grads[:, :, rest_at + k * rest_cols : rest_at + (k + 1) * rest_cols]
        return jnp.concatenate(
            [full.transpose(1, 0, 2).reshape(rows_w, -1), rest.transpose(1, 0, 2).reshape(rows_w, -1)], axis=1
        ).astype(F32)

    e_got = jnp.concatenate(e_got, axis=0)
    routed_grads = [
        grad[:ex_cols].astype(F32) + e_got[k * ex_cols : (k + 1) * ex_cols].astype(F32)
        for k, grad in enumerate(e_grads)
    ]
    return (
        hidden_out.reshape(micro, tok, width),
        in_grad.reshape(micro, tok, width),
        small_own[experts + 1],
        qkv_own[0],
        qkv_own[1],
        qkv_own[2],
        small_own[experts + 3 :],
        out_own,
        small_own[experts + 2],
        small_own[:experts].T,
        small_own[experts],
        from_owner(0),
        from_owner(1),
        from_owner(2),
        routed_grads[0].T[None],
        routed_grads[1].T[None],
        routed_grads[2][None],
    )


def on_device_any(
    hidden_in, seg_ids, routes, out_grad, norm_gain1, w_query, w_key, w_value, b_qkv, w_out,
    norm_gain2, w_router, shared_gate, sh_gate, sh_up, sh_down, ex_gate, ex_up, ex_down,
):
    links = Links()
    micro, tok, width = hidden_in.shape
    experts = w_router.shape[1]
    rows_w = w_query.shape[0]
    n_exp, n_fsdp, n_all = links.n_exp, links.n_fsdp, links.n_all
    my_exp, my_fsdp = links.my_exp, links.my_fsdp
    half_f, core_f = my_fsdp // 2, lax.rem(my_fsdp, 2)
    heads_dev = HEADS // n_fsdp
    wide = heads_dev * HEAD
    seq = tok * n_fsdp
    own = micro * tok
    sh_cols = SHARED_FF // n_all
    ex_cols = ex_gate.shape[2]

    def by_fsdp(three):
        rows = three.shape[0]
        split = three.reshape(rows, 3, 2, 2, heads_dev // 2, 2, HEAD)
        return split.transpose(5, 2, 0, 3, 1, 4, 6).reshape(n_fsdp, rows, 3 * wide)

    def from_fsdp(blocks):
        rows = blocks.shape[1]
        split = blocks.reshape(2, 2, rows, 2, 3, heads_dev // 2, HEAD)
        return split.transpose(4, 2, 1, 3, 5, 0, 6).reshape(3, rows, width)

    small = jnp.concatenate([w_router.T, shared_gate[None], norm_gain1[None], norm_gain2[None], b_qkv], axis=0)
    n_small = small.shape[0]
    small = lax.all_gather(small, ALL, axis=1, tiled=True)
    router_rows = small[: experts + 1]
    gain_one = small[experts + 1].astype(F32)
    gain_two = small[experts + 2].astype(F32)
    bias = by_fsdp(small[experts + 3 :].astype(F32)[None])
    bias = lax.dynamic_index_in_dim(bias, my_fsdp, 0, keepdims=False)

    x = hidden_in.reshape(own, width).astype(F32)
    scaled_one, inverse_one = normalize(x)
    normed_one = (scaled_one * gain_one).astype(BF)
    normed_seq = links.gather_seq(normed_one.reshape(micro, tok, width)).reshape(micro * seq, width)

    qkv = by_fsdp(jnp.stack([w_query, w_key, w_value], axis=1))
    qkv = links.swap_fsdp(qkv).reshape(n_fsdp * rows_w, 3 * wide)
    wqkv = links.gather_rows(qkv).reshape(width, 3 * wide)
    wo = lax.all_gather(w_out, ALL, axis=0, tiled=True).reshape(2, heads_dev, 2, HEAD, width)
    wo = lax.dynamic_index_in_dim(wo, core_f, 0, keepdims=False)
    wo = lax.dynamic_index_in_dim(wo, half_f, 1, keepdims=False).reshape(wide, width)

    tile_cols = sh_cols // LANES * LANES
    rest_cols = sh_cols - tile_cols

    def by_owner(weight):
        full = weight[:, : n_all * tile_cols].reshape(rows_w, n_all, tile_cols).transpose(1, 0, 2)
        rest = weight[:, n_all * tile_cols :].reshape(rows_w, n_all, rest_cols).transpose(1, 0, 2)
        return full, rest

    def from_owner(full, rest):
        return jnp.concatenate(
            [full.transpose(1, 0, 2).reshape(rows_w, -1), rest.transpose(1, 0, 2).reshape(rows_w, -1)], axis=1
        )

    pieces = [by_owner(weight) for weight in (sh_gate, sh_up, sh_down)]
    shared_w = jnp.concatenate([piece[0] for piece in pieces] + [piece[1] for piece in pieces], axis=2)
    shared_w = lax.all_to_all(shared_w, ALL, split_axis=0, concat_axis=0, tiled=True)
    shared_w = shared_w.reshape(width, 3 * sh_cols).T

    def three(rows):
        return [
            jnp.concatenate(
                [rows[k * tile_cols : (k + 1) * tile_cols],
                 rows[3 * tile_cols + k * rest_cols : 3 * tile_cols + (k + 1) * rest_cols]], axis=0)
            for k in range(3)
        ]

    shared_other = links.partner(shared_w, 2)
    routed_w = jnp.concatenate([ex_gate[0].T, ex_up[0].T, ex_down[0]], axis=0)
    halves = [[0, 2], [1, 3]]
    routed_w = lax.all_gather(routed_w, "fsdp", axis=0, axis_index_groups=halves)
    routed_w = [routed_w[:, k * ex_cols : (k + 1) * ex_cols].reshape(2 * ex_cols, width) for k in range(3)]
    units = 2 * (sh_cols + ex_cols)
    pad_rows = -(units + experts + 1) % LANES
    pad = jnp.zeros((pad_rows + experts + 1, width), BF)
    behind = (jnp.pad(router_rows, ((0, pad_rows), (0, 0))), pad, pad)
    wg, wu, wd = [
        jnp.concatenate(pieces, axis=0)
        for pieces in zip(three(shared_w), three(shared_other), routed_w, behind)
    ]
    shared_units = 2 * sh_cols

    grad_own = out_grad.reshape(own, width)
    names = jnp.pad(routes.reshape(own, -1).astype(BF), ((0, 0), (0, LANES - routes.shape[2])))
    grad_near = lax.all_gather(jnp.concatenate([grad_own, names], axis=1), "expert", axis=0)
    grad_far = links.partner(grad_near, 1)

    order = lax.bitwise_xor(my_fsdp, jnp.arange(n_fsdp))
    places = (order[:, None] * tok + jnp.arange(tok)[None]).reshape(seq)
    seg_seq = links.gather_seq(seg_ids)
    cosine, sine = angle_tables(places)
    tables = (cosine, sine, places[:, None], seg_seq.reshape(micro * seq, 1), places[None], seg_seq)
    qkv_seq, attended = attend(normed_seq, wqkv, bias, tables, seq)
    attn_part = contract("tc,cd->td", attended, wo).reshape(micro, n_fsdp, tok, width)
    attn_sum = links.sum_four([attn_part[:, k] for k in range(4)]).reshape(own, width)
    after_attn = x + attn_sum
    scaled_two, inverse_two = normalize(after_attn)
    normed_two = (scaled_two * gain_two).astype(BF)

    near = lax.all_gather(normed_two, "expert", axis=0, tiled=True)
    normed_all = jnp.concatenate([near, links.partner(near, 1)], axis=0)
    grad_all = jnp.concatenate([grad_near, grad_far], axis=0).reshape(2 * n_exp * own, -1)
    named = jnp.sum((grad_all[:, width : width + routes.shape[2]] == my_exp.astype(BF)).astype(F32), axis=1)
    grad_part, out_part, wg_grad, wu_grad, wd_grad = feed_plain(
        normed_all, grad_all[:, :width], named, my_exp, wg, wu, wd, router_rows, experts, shared_units
    )

    def summed(part):
        count = n_exp * own
        total = part[:count] + links.partner(part[count:].astype(BF), 1).astype(F32)
        return links.sum_rows(total.reshape(n_exp, own, -1))

    grad_sum, out_sum = summed(grad_part), summed(out_part)
    wg_grad, wu_grad, wd_grad = [item.astype(BF) for item in (wg_grad, wu_grad, wd_grad)]
    hidden_out = (after_attn + out_sum).astype(BF)

    own_logits = contract("td,cd->tc", normed_two, router_rows)
    own_probs = jax.nn.softmax(own_logits[:, :experts], axis=-1)
    own_scale = jax.nn.sigmoid(own_logits[:, experts])
    grad_probs = grad_sum[:, width : width + experts]
    grad_router = own_probs * (grad_probs - jnp.sum(own_probs * grad_probs, axis=-1, keepdims=True))
    grad_gate = grad_sum[:, width + experts] * own_scale * (1.0 - own_scale)
    grad_logits = jnp.concatenate([grad_router, grad_gate[:, None]], axis=1).astype(BF)
    grad_normed_two = grad_sum[:, :width] + contract("tc,cd->td", grad_logits, router_rows)
    router_part = contract("tc,td->cd", grad_logits, normed_two)

    grad_after = grad_own.astype(F32) + norm_back(grad_normed_two, scaled_two, inverse_two, gain_two)
    gain_two_part = jnp.sum(grad_normed_two * scaled_two, axis=0)

    grad_attn = links.gather_seq(grad_after.astype(BF).reshape(micro, tok, width)).reshape(micro * seq, width)
    grad_lin, grad_normed_one = attend(normed_seq, wqkv, bias, tables, seq, (grad_attn, wo, qkv_seq))
    gain_one_part = jnp.sum(grad_normed_one * normed_seq.astype(F32), axis=0) / gain_one
    grad_normed_one = grad_normed_one.reshape(micro, n_fsdp, tok, width)
    grad_normed_one = links.sum_four([grad_normed_one[:, k] for k in range(4)]).reshape(own, width)
    in_grad = grad_after + norm_back(grad_normed_one, scaled_one, inverse_one, gain_one)
    out_grad_part = contract("tc,td->cd", attended, grad_attn).astype(BF)
    qkv_part = contract("td,tc->dc", normed_seq, grad_lin).astype(BF)
    bias_part = jnp.sum(grad_lin.astype(F32), axis=0)

    out_place = jnp.zeros((2, heads_dev, 2, HEAD, width), BF)
    out_place = lax.dynamic_update_slice(
        out_place, out_grad_part.reshape(1, heads_dev, 1, HEAD, width), (core_f, 0, half_f, 0, 0)
    )
    out_own = lax.psum_scatter(
        out_place.reshape(width, width), ALL, scatter_dimension=0, tiled=True
    ).astype(F32)
    bias_place = jnp.zeros((n_fsdp, 1, 3 * wide), F32)
    bias_place = from_fsdp(lax.dynamic_update_index_in_dim(bias_place, bias_part[None], my_fsdp, 0))[:, 0]
    small_part = jnp.concatenate([router_part, gain_one_part[None], gain_two_part[None], bias_place], axis=0)
    small_part = small_part.astype(BF).reshape(n_small, n_exp, n_fsdp, rows_w).transpose(1, 2, 0, 3)
    behind_rows = -(-n_fsdp * n_small * rows_w // (3 * wide) // 8) * 8
    room = behind_rows * 3 * wide
    small_part = small_part.reshape(n_exp, n_fsdp * n_small * rows_w)
    small_part = jnp.pad(small_part, ((0, 0), (0, room - small_part.shape[1])))
    qkv_part = jnp.concatenate(
        [qkv_part.reshape(n_exp, n_fsdp * rows_w, 3 * wide), small_part.reshape(n_exp, behind_rows, 3 * wide)], axis=1
    )
    qkv_sum = links.sum_rows(qkv_part).astype(BF)
    small_sum = qkv_sum[n_fsdp * rows_w :].reshape(-1)[: n_fsdp * n_small * rows_w].reshape(n_fsdp, n_small * rows_w)
    small_sum = jnp.pad(small_sum, ((0, 0), (0, 3 * wide - n_small * rows_w)))
    qkv_sum = qkv_sum[: n_fsdp * rows_w].reshape(n_fsdp, rows_w, 3 * wide)
    qkv_own = links.swap_fsdp(jnp.concatenate([qkv_sum, small_sum[:, None]], axis=1))
    small_own = jnp.sum(qkv_own[:, rows_w, : n_small * rows_w].astype(F32), axis=0).reshape(n_small, rows_w)
    qkv_own = from_fsdp(qkv_own[:, :rows_w]).astype(F32)

    grads = (wg_grad, wu_grad, wd_grad)
    shared_mine = jnp.concatenate(
        [grad[:tile_cols] for grad in grads] + [grad[tile_cols:sh_cols] for grad in grads], axis=0)
    shared_give = jnp.concatenate(
        [grad[sh_cols : sh_cols + tile_cols] for grad in grads]
        + [grad[sh_cols + tile_cols : 2 * sh_cols] for grad in grads], axis=0)
    shared_got = links.partner(shared_give, 2)
    shared_grads = (shared_mine.astype(F32) + shared_got.astype(F32)).astype(BF)
    shared_own = lax.all_to_all(
        shared_grads.T.reshape(n_all, rows_w, 3 * sh_cols), ALL, split_axis=0, concat_axis=0, tiled=True
    )
    cut = 3 * tile_cols
    shared_own = [
        from_owner(
            shared_own[:, :, k * tile_cols : (k + 1) * tile_cols],
            shared_own[:, :, cut + k * rest_cols : cut + (k + 1) * rest_cols],
        ).astype(F32)
        for k in range(3)
    ]
    routed_grads = jnp.stack(
        [
            jnp.concatenate([grad[low : low + ex_cols] for grad in grads], axis=0)
            for low in (shared_units, shared_units + ex_cols)
        ]
    )
    routed_grads = lax.psum_scatter(routed_grads, "fsdp", scatter_dimension=0, axis_index_groups=halves).astype(F32)
    routed_grads = [routed_grads[k * ex_cols : (k + 1) * ex_cols] for k in range(3)]
    return (
        hidden_out.reshape(micro, tok, width),
        in_grad.reshape(micro, tok, width),
        small_own[experts + 1],
        qkv_own[0],
        qkv_own[1],
        qkv_own[2],
        small_own[experts + 3 :],
        out_own,
        small_own[experts + 2],
        small_own[:experts].T,
        small_own[experts],
        shared_own[0],
        shared_own[1],
        shared_own[2],
        routed_grads[0].T[None],
        routed_grads[1].T[None],
        routed_grads[2][None],
    )


def solution(mesh):
    rows = P(ALL, None)
    tokens = P(None, ALL, None)
    in_specs = (
        tokens, P(None, ALL), tokens, tokens, P(ALL), rows, rows, rows, P(None, ALL), rows,
        P(ALL), rows, P(ALL), rows, rows, rows,
        P("expert", None, "fsdp"), P("expert", None, "fsdp"), P("expert", "fsdp", None),
    )
    out_specs = (
        tokens, tokens, P(ALL), rows, rows, rows, P(None, ALL), rows, P(ALL), rows, P(ALL),
        rows, rows, rows,
        P("expert", None, "fsdp"), P("expert", None, "fsdp"), P("expert", "fsdp", None),
    )
    on_device = on_device_ring if mesh.shape["expert"] == 8 and mesh.shape["fsdp"] == 4 else on_device_any
    return jax.shard_map(on_device, mesh=mesh, in_specs=in_specs, out_specs=out_specs, check_vma=False)
```

```python
import functools

import jax
import jax.numpy as jnp
from jax import lax
from jax.experimental import pallas as pl
from jax.experimental.pallas import tpu as pltpu
from jax.sharding import PartitionSpec as P

HEADS = 16
HEAD = 128
SHARED_FF = 5632
EPSILON = 1e-06
ROPE_BASE = 1000000.0
MASKED = -1e30
ALL = ("expert", "fsdp")
BF = jnp.bfloat16
F32 = jnp.float32
LANES = 128
COLS = 1024
GRAD_TILE = 384


def normalize(values):
    inverse = lax.rsqrt(jnp.mean(values * values, axis=-1, keepdims=True) + EPSILON)
    return (values * inverse, inverse)


def norm_back(grad_normed, scaled, inverse, gain_vec):
    grad_scaled = grad_normed * gain_vec
    return inverse * (grad_scaled - scaled * jnp.mean(grad_scaled * scaled, axis=-1, keepdims=True))


def angle_tables(places):
    inverse = 1.0 / ROPE_BASE ** (jnp.arange(0, HEAD, 2).astype(F32) / HEAD)
    angles = places.astype(F32)[:, None] * inverse[None, :]
    cosine, sine = jnp.cos(angles), jnp.sin(angles)
    return jnp.concatenate([cosine, cosine], axis=1), jnp.concatenate([-sine, sine], axis=1)


def silu_parts(pre_act):
    logistic = 1.0 / (1.0 + jnp.exp(-pre_act))
    return (pre_act * logistic, logistic * (1.0 + pre_act * (1.0 - logistic)))


def contract(pattern, left_op, right_op):
    return jnp.einsum(pattern, left_op, right_op, preferred_element_type=F32)


def dot_nt(left_op, right_op):
    return lax.dot_general(left_op, right_op, (((1,), (1,)), ((), ())), preferred_element_type=F32)


def dot_nn(left_op, right_op):
    return lax.dot_general(left_op, right_op, (((1,), (0,)), ((), ())), preferred_element_type=F32)


def dot_tn(left_op, right_op):
    return lax.dot_general(left_op, right_op, (((0,), (0,)), ((), ())), preferred_element_type=F32)


def after(value, *earlier):
    return lax.optimization_barrier((value, earlier))[0]


class Links:
    def __init__(self):
        self.n_exp = lax.axis_size("expert")
        self.n_fsdp = lax.axis_size("fsdp")
        self.my_exp = lax.axis_index("expert")
        self.my_fsdp = lax.axis_index("fsdp")
        self.n_all = self.n_exp * self.n_fsdp

    def partner(self, value, bit):
        pairs = [
            (e * self.n_fsdp + f, e * self.n_fsdp + (f ^ bit)) for e in range(self.n_exp) for f in range(self.n_fsdp)
        ]
        return lax.ppermute(value, ALL, pairs)

    def gather_rows(self, value):
        return lax.all_gather(value, "expert", axis=0)

    def sum_rows(self, value):
        return lax.psum_scatter(value.astype(BF), "expert", scatter_dimension=0).astype(F32)

    def swap_fsdp(self, value):
        result = value
        for bit in range(1, self.n_fsdp):
            other = lax.bitwise_xor(self.my_fsdp, bit)
            block = lax.dynamic_index_in_dim(value, other, 0, keepdims=False)
            result = lax.dynamic_update_index_in_dim(result, self.partner(block, bit), other, 0)
        return result

    def gather_four(self, value):
        far = self.partner(value, 2)
        return [value, self.partner(value, 1), far, self.partner(far, 1)]

    def gather_seq(self, value):
        return jnp.concatenate(self.gather_four(value), axis=1)

    def sum_four(self, parts):
        far = (parts[2].astype(F32) + self.partner(parts[3].astype(BF), 1).astype(F32)).astype(BF)
        near = parts[0].astype(F32) + self.partner(parts[1].astype(BF), 1).astype(F32)
        return near + self.partner(far, 2).astype(F32)


def attend_kernel(heads, seq, scale, split, x_ref, w_ref, bias_ref, cos_ref, sin_ref, place_ref, seg_ref,
                  place_row_ref, seg_row_ref, core_ref, qkv_ref, *out_refs):
    lin = dot_nn(x_ref[...], w_ref[...]) + bias_ref[...]
    cosine, sine = cos_ref[...], sin_ref[...]
    span = heads * HEAD
    for micro in range(x_ref.shape[0] // seq):
        low, high = micro * seq, (micro + 1) * seq
        visible = (place_row_ref[...] <= place_ref[...]) & (seg_row_ref[micro : micro + 1, :] == seg_ref[low:high, :])
        found = []
        for head in range(heads):
            at = head * HEAD
            query = lin[low:high, at : at + HEAD]
            key = lin[low:high, span + at : span + at + HEAD]
            value = lin[low:high, 2 * span + at : 2 * span + at + HEAD].astype(BF)
            query = (query * cosine + pltpu.roll(query, HEAD // 2, 1) * sine).astype(BF)
            key = (key * cosine + pltpu.roll(key, HEAD // 2, 1) * sine).astype(BF)
            scores = jnp.where(visible, dot_nt(query, key) * scale, MASKED)
            exps = jnp.exp(scores - jnp.max(scores, axis=1, keepdims=True))
            probs = exps / jnp.sum(exps, axis=1, keepdims=True)
            found.append(dot_nn(probs.astype(BF), value))
            qkv_ref[low:high, at : at + HEAD] = query
            qkv_ref[low:high, span + at : span + at + HEAD] = key
            qkv_ref[low:high, 2 * span + at : 2 * span + at + HEAD] = value
        if not split:
            out_refs[0][low:high, :] = jnp.concatenate(found, axis=1).astype(BF)
            continue
        first = jnp.concatenate([item[:, : HEAD // 2] for item in found], axis=1)
        second = jnp.concatenate([item[:, HEAD // 2 :] for item in found], axis=1)
        out_refs[0][low:high, :] = jnp.where(core_ref[0] == 0, first, second).astype(BF)
        out_refs[1][low:high, :] = jnp.where(core_ref[0] == 0, second, first).astype(BF)


def attend_back_kernel(heads, seq, scale, split, grad_ref, other_ref, qkv_ref, cos_ref, sin_ref, place_ref, seg_ref,
                       place_row_ref, seg_row_ref, core_ref, w_ref, x_ref, lin_ref, normed_ref, *panel_refs):
    cosine, sine = cos_ref[...], sin_ref[...]
    span = heads * HEAD
    if split:
        first = jnp.where(core_ref[0] == 0, grad_ref[...], other_ref[...])
        second = jnp.where(core_ref[0] == 0, other_ref[...], grad_ref[...])
        half = HEAD // 2
        grad_out = jnp.concatenate(
            [part[:, k * half : (k + 1) * half] for k in range(heads) for part in (first, second)], axis=1)
    else:
        grad_out = dot_nt(grad_ref[...], other_ref[...]).astype(BF)
    for micro in range(grad_ref.shape[0] // seq):
        low, high = micro * seq, (micro + 1) * seq
        visible = (place_row_ref[...] <= place_ref[...]) & (seg_row_ref[micro : micro + 1, :] == seg_ref[low:high, :])
        for head in range(heads):
            at = head * HEAD
            query = qkv_ref[low:high, at : at + HEAD]
            key = qkv_ref[low:high, span + at : span + at + HEAD]
            value = qkv_ref[low:high, 2 * span + at : 2 * span + at + HEAD]
            grad = grad_out[low:high, at : at + HEAD]
            scores = jnp.where(visible, dot_nt(query, key) * scale, MASKED)
            exps = jnp.exp(scores - jnp.max(scores, axis=1, keepdims=True))
            probs = exps / jnp.sum(exps, axis=1, keepdims=True)
            grad_probs = dot_nt(grad, value)
            grad_value = dot_tn(probs.astype(BF), grad)
            grad_scores = probs * (grad_probs - jnp.sum(probs * grad_probs, axis=1, keepdims=True))
            grad_scores = grad_scores.astype(BF)
            grad_query = dot_nn(grad_scores, key) * scale
            grad_key = dot_tn(grad_scores, query) * scale
            grad_query = grad_query * cosine - pltpu.roll(grad_query, HEAD // 2, 1) * sine
            grad_key = grad_key * cosine - pltpu.roll(grad_key, HEAD // 2, 1) * sine
            lin_ref[low:high, at : at + HEAD] = grad_query.astype(BF)
            lin_ref[low:high, span + at : span + at + HEAD] = grad_key.astype(BF)
            lin_ref[low:high, 2 * span + at : 2 * span + at + HEAD] = grad_value.astype(BF)
    if split:
        panel_ref = panel_refs[0]
        count, rows = panel_ref.shape[0], x_ref.shape[1] // panel_ref.shape[0]
        grad_w = dot_tn(x_ref[...], lin_ref[...]).astype(BF)
        for k in range(count):
            panel_ref[k, :rows, :] = grad_w[k * rows : (k + 1) * rows, :]
        behind = panel_ref.shape[1] - rows
        panel_ref[:, rows:, :] = jnp.zeros((count, behind, panel_ref.shape[2]), BF)
    part = dot_nt(lin_ref[...], w_ref[...])

    @pl.when(pl.program_id(0) == 0)
    def _():
        normed_ref[...] = part

    @pl.when(pl.program_id(0) > 0)
    def _():
        normed_ref[...] += part


def whole(shape):
    return pl.BlockSpec(shape, lambda *_: (0,) * len(shape))


def attend(normed, wqkv, bias, tables, seq, back=None, core=None, panel=None):
    cosine, sine, place, seg, place_row, seg_row = tables
    rows = normed.shape[0]
    pairs = 2
    wide3 = bias.shape[1]
    heads = wide3 // 3 // HEAD // pairs
    span = heads * HEAD
    scale = HEAD ** (-0.5)
    split = core is not None
    common = (cosine, sine, place, seg, place_row, seg_row, core if split else jnp.zeros((1,), jnp.int32))
    common_specs = [whole(item.shape) for item in common[:-1]] + [pl.BlockSpec(memory_space=pltpu.SMEM)]
    params = pltpu.CompilerParams(vmem_limit_bytes=48 * 2**20)
    cost = pl.CostEstimate(flops=10**8, bytes_accessed=10**6, transcendentals=10**5)
    columns, count = (span // 2, 2) if split else (span, 1)
    kept = pl.BlockSpec((rows, columns), lambda p: (0, p))
    if back is None:
        return pl.pallas_call(
            functools.partial(attend_kernel, heads, seq, scale, split),
            grid=(pairs,),
            in_specs=[
                whole(normed.shape),
                pl.BlockSpec((wqkv.shape[0], 3 * span), lambda p: (0, p)),
                pl.BlockSpec((1, 3 * span), lambda p: (0, p)),
            ] + common_specs,
            out_specs=[pl.BlockSpec((rows, 3 * span), lambda p: (0, p))] + [kept] * count,
            out_shape=[jax.ShapeDtypeStruct((rows, wide3), BF)]
            + [jax.ShapeDtypeStruct((rows, pairs * columns), BF)] * count,
            compiler_params=params,
            cost_estimate=cost,
            name="attend",
        )(normed, wqkv, bias, *common)
    grad, other, qkv = back
    return pl.pallas_call(
        functools.partial(attend_back_kernel, heads, seq, scale, split),
        grid=(pairs,),
        in_specs=([kept, kept] if split else [whole(grad.shape), pl.BlockSpec((span, other.shape[1]), lambda p: (p, 0))])
        + [pl.BlockSpec((rows, 3 * span), lambda p: (0, p))]
        + common_specs
        + [pl.BlockSpec((wqkv.shape[0], 3 * span), lambda p: (0, p)), whole(normed.shape)],
        out_specs=[pl.BlockSpec((rows, 3 * span), lambda p: (0, p)), whole((rows, wqkv.shape[0]))]
        + ([pl.BlockSpec(panel[:2] + (3 * span,), lambda p: (0, 0, p))] if split else []),
        out_shape=[jax.ShapeDtypeStruct((rows, wide3), BF), jax.ShapeDtypeStruct((rows, wqkv.shape[0]), F32)]
        + ([jax.ShapeDtypeStruct(panel, BF)] if split else []),
        compiler_params=params,
        cost_estimate=cost,
        name="attend_back",
    )(grad, other, qkv, *common, wqkv, normed)


def feed_kernel(experts, shared, expert_ref, *refs):
    x_refs, g_refs = refs[:3], refs[3:6]
    weights = (refs[6:9], refs[9:12])
    unit_refs, gn_refs, out_refs = refs[12:18], refs[18:21], refs[21:24]
    x_all, g_all = refs[24:26]
    units = (refs[26:29], refs[29:32])
    gn, out, sems = refs[32:]
    own, width = x_refs[0].shape
    rows = 4 * own
    expert = expert_ref[0]

    def block(k):
        return pl.ds(k * own, 2 * own if k == 2 else own)

    def start(number, source, target):
        copy = pltpu.make_async_copy(source, target, sems.at[number])
        copy.start()
        return copy

    x_copies = [start(k, x_refs[k], x_all.at[block(k), :]) for k in range(3)]
    g_copies = [start(3 + k, g_refs[k], g_all.at[block(k), :]) for k in range(3)]
    for copy in x_copies:
        copy.wait()
    gates = [dot_nt(x_all[...], weights[k][0][...]) for k in range(2)]
    for copy in g_copies:
        copy.wait()
    names = g_all[:, width:].astype(F32)
    lane = lax.broadcasted_iota(jnp.int32, names.shape, 1)
    hit = jnp.where((lane < 4) & (names == expert.astype(F32)), 1.0, 0.0)
    hit = jnp.sum(hit, axis=1, keepdims=True)
    first = shared // LANES * LANES
    logits = gates[0][:, first : first + LANES]
    lane = lane - (shared - first)
    is_expert = (lane >= 0) & (lane < experts)
    scores = jnp.where(is_expert, logits, MASKED)
    exps = jnp.where(is_expert, jnp.exp(scores - jnp.max(scores, axis=1, keepdims=True)), 0.0)
    mine = jnp.sum(jnp.where(lane == expert, exps, 0.0), axis=1, keepdims=True)
    mine = mine / jnp.sum(exps, axis=1, keepdims=True)
    last = jnp.sum(jnp.where(lane == experts, logits, 0.0), axis=1, keepdims=True)
    scales = (1.0 / (1.0 + jnp.exp(-last)), mine * hit)
    dots, copies = [], []
    for k in range(2):
        hs, dg, du = units[k]
        act, slope = silu_parts(gates[k])
        up = dot_nt(x_all[...], weights[k][1][...])
        grad = dot_nt(g_all[:, :width], weights[k][2][...])
        hidden = act * up
        dots.append(jnp.sum(hidden * grad, axis=1, keepdims=True))
        grad = grad * scales[k]
        hs[...] = (hidden * scales[k]).astype(BF)
        dg[...] = (grad * up * slope).astype(BF)
        du[...] = (grad * act).astype(BF)
        copies += [
            start(3 * k + j, source, target) for j, (source, target) in enumerate(zip((hs, dg, du), unit_refs[3 * k :]))
        ]
    lane = lax.broadcasted_iota(jnp.int32, (rows, LANES), 1)
    extra = jnp.where(lane == expert, dots[1] * hit, 0.0) + jnp.where(lane == experts, dots[0], 0.0)
    gn[:, width:] = extra.astype(BF)
    total = dot_nn(units[0][1][...], weights[0][0][...]) + dot_nn(units[0][2][...], weights[0][1][...])
    total += dot_nn(units[1][1][...], weights[1][0][...]) + dot_nn(units[1][2][...], weights[1][1][...])
    gn[:, :width] = total.astype(BF)
    copies += [start(6 + k, gn.at[block(k), :], gn_refs[k]) for k in range(3)]
    total = dot_nn(units[0][0][...], weights[0][2][...]) + dot_nn(units[1][0][...], weights[1][2][...])
    out[...] = total.astype(BF)
    copies += [start(9 + k, out.at[block(k), :], out_refs[k]) for k in range(3)]
    for copy in copies:
        copy.wait()


def feed(expert, x_blocks, g_blocks, shared_w, routed_w, experts, shared):
    own, width = x_blocks[0].shape
    rows = 4 * own
    wide = g_blocks[0].shape[1]
    counts = (shared_w[0].shape[0], routed_w[0].shape[0])
    anywhere = pl.BlockSpec(memory_space=pl.ANY)
    weights = [pltpu.with_memory_space_constraint(weight, pltpu.VMEM) for weight in (*shared_w, *routed_w)]
    found = pl.pallas_call(
        functools.partial(feed_kernel, experts, shared),
        in_specs=[pl.BlockSpec(memory_space=pltpu.SMEM)]
        + [anywhere] * 6
        + [pl.BlockSpec(memory_space=pltpu.VMEM)] * 6,
        out_specs=[anywhere] * 12,
        scratch_shapes=[pltpu.VMEM((rows, width), BF), pltpu.VMEM((rows, wide), BF)]
        + [pltpu.VMEM((rows, count), BF) for count in counts for _ in range(3)]
        + [pltpu.VMEM((rows, wide), BF), pltpu.VMEM((rows, width), BF), pltpu.SemaphoreType.DMA((12,))],
        out_shape=[jax.ShapeDtypeStruct((rows, count), BF) for count in counts for _ in range(3)]
        + [jax.ShapeDtypeStruct((count, columns), BF) for columns in (wide, width) for count in (own, own, 2 * own)],
        compiler_params=pltpu.CompilerParams(vmem_limit_bytes=42 * 2**20),
        cost_estimate=pl.CostEstimate(flops=16 * 10**9, bytes_accessed=3 * 10**7, transcendentals=10**6),
        name="feed",
    )(expert, *x_blocks, *g_blocks, *weights)
    return found[:3], found[3:6], found[6:9], found[9:12]


SMALL_COST = pl.CostEstimate(flops=0, bytes_accessed=10**6, transcendentals=0)


def pack_kernel(full, rest, gate_ref, up_ref, down_ref, out_ref):
    count = out_ref.shape[0]
    refs = (gate_ref, up_ref, down_ref)
    for j in range(count):
        for k in range(3):
            out_ref[j, :, k * full : (k + 1) * full] = refs[k][:, j * full : (j + 1) * full]
        low = count * full + j * rest
        out_ref[j, :, 3 * full :] = jnp.concatenate([ref[:, low : low + rest] for ref in refs], axis=1)


def pack_shared(gate, up, down, count, full, rest):
    vmem = pl.BlockSpec(memory_space=pltpu.VMEM)
    return pl.pallas_call(
        functools.partial(pack_kernel, full, rest),
        in_specs=[vmem] * 3,
        out_specs=vmem,
        out_shape=jax.ShapeDtypeStruct((count, gate.shape[0], 3 * (full + rest)), BF),
        compiler_params=pltpu.CompilerParams(vmem_limit_bytes=16 * 2**20),
        cost_estimate=SMALL_COST,
        name="pack_shared",
    )(gate, up, down)


def unpack_kernel(full, rest, in_ref, *out_refs):
    count = in_ref.shape[0]
    for k in range(3):
        for j in range(count):
            out_refs[k][:, j * full : (j + 1) * full] = in_ref[j, :, k * full : (k + 1) * full].astype(F32)
        low = 3 * full + k * rest
        for j in range(0, count, 4):
            at = count * full + j * rest
            piece = jnp.concatenate([in_ref[j + i, :, low : low + rest] for i in range(4)], axis=1)
            out_refs[k][:, at : at + 4 * rest] = piece.astype(F32)


def unpack_shared(blocks, full, rest):
    count, rows, _ = blocks.shape
    vmem = pl.BlockSpec(memory_space=pltpu.VMEM)
    return pl.pallas_call(
        functools.partial(unpack_kernel, full, rest),
        in_specs=[vmem],
        out_specs=[vmem] * 3,
        out_shape=[jax.ShapeDtypeStruct((rows, count * (full + rest)), F32)] * 3,
        compiler_params=pltpu.CompilerParams(vmem_limit_bytes=16 * 2**20),
        cost_estimate=SMALL_COST,
        name="unpack_shared",
    )(blocks)


def fold_kernel(full, rest, *refs):
    out_ref, rests = refs[6], []
    for k in range(3):
        total = refs[2 * k][...].astype(F32) + refs[2 * k + 1][...].astype(F32)
        total = total.T.astype(BF)
        out_ref[:, k * full : (k + 1) * full] = total[:, :full]
        rests.append(total[:, full : full + rest])
    out_ref[:, 3 * full :] = jnp.concatenate(rests, axis=1)


def fold_shared(pairs, full, rest):
    vmem = pl.BlockSpec(memory_space=pltpu.VMEM)
    return pl.pallas_call(
        functools.partial(fold_kernel, full, rest),
        in_specs=[vmem] * 6,
        out_specs=vmem,
        out_shape=jax.ShapeDtypeStruct((pairs[0][0].shape[1], 3 * (full + rest)), BF),
        compiler_params=pltpu.CompilerParams(vmem_limit_bytes=24 * 2**20),
        cost_estimate=SMALL_COST,
        name="fold_shared",
    )(*[item for pair in pairs for item in pair])


def join_kernel(cuts, y_ref, mine_ref, low_ref, high_ref, behind_ref, *out_refs):
    half = low_ref.shape[0]
    for k, pieces in enumerate(cuts):
        at = 0
        for low, count in pieces:
            for block in range(mine_ref.shape[1] // LANES):
                columns = slice(block * LANES, (block + 1) * LANES)
                target = pl.ds(pl.multiple_of((2 * block + y_ref[0]) * LANES, LANES), LANES)
                out_refs[k][at : at + count, target] = mine_ref[low : low + count, columns]
                target = pl.ds(pl.multiple_of((2 * block + 1 - y_ref[0]) * LANES, LANES), LANES)
                middle = min(max(half - low, 0), count)
                if middle:
                    out_refs[k][at : at + middle, target] = low_ref[low : low + middle, columns]
                if middle < count:
                    begin = low + middle - half
                    out_refs[k][at + middle : at + count, target] = high_ref[begin : begin + count - middle, columns]
            at += count
        rest = out_refs[k].shape[0] - at
        out_refs[k][at:, :] = behind_ref[...] if k == 0 else jnp.zeros((rest, out_refs[k].shape[1]), BF)


def join_shared(y, mine, low, high, behind, cuts):
    rows = sum(count for _, count in cuts[0]) + behind.shape[0]
    vmem = pl.BlockSpec(memory_space=pltpu.VMEM)
    return pl.pallas_call(
        functools.partial(join_kernel, cuts),
        in_specs=[pl.BlockSpec(memory_space=pltpu.SMEM)] + [vmem] * 4,
        out_specs=[vmem] * 3,
        out_shape=[jax.ShapeDtypeStruct((rows, 2 * mine.shape[1]), BF)] * 3,
        compiler_params=pltpu.CompilerParams(vmem_limit_bytes=24 * 2**20),
        cost_estimate=pl.CostEstimate(flops=0, bytes_accessed=10**7, transcendentals=0),
        name="join_shared",
    )(y, mine, low, high, behind)


def weights_kernel(n_sets, split, y_ref, *refs):
    sources, lhs_refs = refs[:12], refs[12 : 12 + 4 * n_sets]
    out_refs, (held, sems) = refs[12 + 4 * n_sets : -2], refs[-2:]
    rows, width = held.shape
    own = rows // 16

    @pl.when(pl.program_id(0) == 0)
    def _():
        copies = []
        for k in range(12):
            at, count = (k // 3 * 4 + k % 3) * own, 2 * own if k % 3 == 2 else own
            copies.append(
                pltpu.make_async_copy(sources[k].at[:, pl.ds(0, width)], held.at[pl.ds(at, count), :], sems.at[k]))
        for copy in copies:
            copy.start()
        for copy in copies:
            copy.wait()

    for k in range(n_sets):
        lhs = jnp.concatenate([ref[...] for ref in lhs_refs[4 * k : 4 * k + 4]], axis=0)
        total = dot_tn(lhs, held[...])
        if not split:
            for tile in range(2):
                at = 0
                for out_ref in out_refs:
                    low, high = max(at, tile * GRAD_TILE), min(at + out_ref.shape[0], (tile + 1) * GRAD_TILE)
                    if low < high:

                        @pl.when(pl.program_id(0) == tile)
                        def _(out_ref=out_ref, low=low, high=high, at=at, tile=tile):
                            out_ref[low - at : high - at, :] = total[
                                low - tile * GRAD_TILE : high - tile * GRAD_TILE, :].astype(BF)

                    at += out_ref.shape[0]
            continue
        for block in range(width // LANES // 2):
            even = total[:, 2 * block * LANES : (2 * block + 1) * LANES]
            odd = total[:, (2 * block + 1) * LANES : (2 * block + 2) * LANES]
            columns = slice(block * LANES, (block + 1) * LANES)
            out_refs[2 * k][:, columns] = jnp.where(y_ref[0] == 0, even, odd).astype(BF)
            out_refs[2 * k + 1][:, columns] = jnp.where(y_ref[0] == 0, odd, even).astype(BF)


def weight_grads(y, sources, lhs_sets, width, parts=None):
    rows, units = lhs_sets[0][0].shape
    n_sets = len(lhs_sets)
    n_tiles = units // GRAD_TILE
    split = parts is None
    if split:
        shapes = [(GRAD_TILE, width // 2)] * (2 * n_sets)
    else:
        shapes = [(count, width) for count in parts]
    return pl.pallas_call(
        functools.partial(weights_kernel, n_sets, split),
        grid=(n_tiles,),
        in_specs=[pl.BlockSpec(memory_space=pltpu.SMEM)]
        + [pl.BlockSpec(memory_space=pl.ANY)] * 12
        + [pl.BlockSpec((rows, GRAD_TILE), lambda i: (0, i))] * (4 * n_sets),
        out_specs=[whole(shape) for shape in shapes],
        scratch_shapes=[pltpu.VMEM((4 * rows, width), BF), pltpu.SemaphoreType.DMA((12,))],
        out_shape=[jax.ShapeDtypeStruct(shape, BF) for shape in shapes],
        compiler_params=pltpu.CompilerParams(vmem_limit_bytes=36 * 2**20),
        cost_estimate=pl.CostEstimate(
            flops=4 * 10**9 * n_sets * n_tiles, bytes_accessed=2 * 10**7, transcendentals=0),
        name="weight_grads",
    )(y, *sources, *[item for lhs in lhs_sets for item in lhs])


def feed_plain(normed, grad, named, expert, wg, wu, wd, router, experts, shared):
    logits = contract("td,cd->tc", normed, router)
    router_probs = jax.nn.softmax(logits[:, :experts], axis=-1)
    shared_scale = jax.nn.sigmoid(logits[:, experts : experts + 1])
    hot = (jnp.arange(experts) == expert).astype(F32)
    gate_here = jnp.sum(router_probs * hot, axis=1, keepdims=True) * named[:, None]
    is_shared = (jnp.arange(wg.shape[0]) < shared)[None]
    row_scale = jnp.where(is_shared, shared_scale, gate_here)
    act, slope = silu_parts(contract("td,cd->tc", normed, wg))
    up = contract("td,cd->tc", normed, wu)
    hidden = act * up
    hidden_scaled = (hidden * row_scale).astype(BF)
    grad_hidden = contract("td,fd->tf", grad, wd)
    dots = hidden * grad_hidden
    dot_shared = jnp.sum(jnp.where(is_shared, dots, 0.0), axis=1, keepdims=True)
    dot_expert = jnp.sum(jnp.where(is_shared, 0.0, dots), axis=1, keepdims=True) * named[:, None]
    grad_pre = grad_hidden * row_scale
    grad_gate = (grad_pre * up * slope).astype(BF)
    grad_up = (grad_pre * act).astype(BF)
    grad_normed = contract("tc,cd->td", grad_gate, wg) + contract("tc,cd->td", grad_up, wu)
    extra = jnp.concatenate([dot_expert * hot, dot_shared], axis=1)
    extra = jnp.pad(extra, ((0, 0), (0, LANES - extra.shape[1])))
    out = contract("tf,fd->td", hidden_scaled, wd)
    return (
        jnp.concatenate([grad_normed, extra], axis=1),
        out,
        contract("tc,td->cd", grad_gate, normed),
        contract("tc,td->cd", grad_up, normed),
        contract("tf,td->fd", hidden_scaled, grad),
    )


def ring_perm(move):
    pairs = []
    for me in range(32):
        z, x, y, c = me // 8, me // 4 % 2, me // 2 % 2, me % 2
        z, x, y, c = move(z, x, y, c)
        pairs.append((me, ((z * 2 + x) * 2 + y) * 2 + c))
    return pairs


MOVES = {
    "core": lambda z, x, y, c: (z, x, y, 1 - c),
    "y": lambda z, x, y, c: (z, x, 1 - y, c),
    "yc": lambda z, x, y, c: (z, x, 1 - y, 1 - c),
    "x": lambda z, x, y, c: (z, 1 - x, y, c),
    "z1": lambda z, x, y, c: ((z + 1) % 4, x, y, c),
    "z2": lambda z, x, y, c: ((z + 2) % 4, x, y, c),
    "z3": lambda z, x, y, c: ((z + 3) % 4, x, y, c),
}


def send(value, link):
    return lax.ppermute(value, ALL, ring_perm(MOVES[link]))


def sync(*values):
    return lax.optimization_barrier(values)


def pick(value, place, axis=0):
    return lax.dynamic_index_in_dim(value, place, axis, keepdims=False)


def put(value, block, place, axis=0):
    return lax.dynamic_update_index_in_dim(value, block, place, axis)


def in_order(mine, other, bit, axis):
    return jnp.where(bit == 0, jnp.stack([mine, other], axis=axis), jnp.stack([other, mine], axis=axis))


def on_device_ring(
    hidden_in, seg_ids, routes, out_grad, norm_gain1, w_query, w_key, w_value, b_qkv, w_out,
    norm_gain2, w_router, shared_gate, sh_gate, sh_up, sh_down, ex_gate, ex_up, ex_down,
):
    micro, tok, width = hidden_in.shape
    experts = w_router.shape[1]
    rows_w = w_query.shape[0]
    top_count = routes.shape[2]
    my_exp, my_fsdp = lax.axis_index("expert"), lax.axis_index("fsdp")
    z, x, y, c = my_exp // 2, lax.rem(my_exp, 2), my_fsdp // 2, lax.rem(my_fsdp, 2)
    n_exp, n_fsdp, n_all = 8, 4, 32
    heads_dev = HEADS // n_fsdp
    wide = heads_dev * HEAD
    seq, own = tok * n_fsdp, micro * tok
    ex_cols = ex_gate.shape[2]
    sh_cols = SHARED_FF // 16
    full_cols = sh_cols // LANES * LANES
    rest_cols = sh_cols - full_cols
    unit_cols = 3 * sh_cols

    def slot(step, other):
        return lax.rem(z + 4 - step, 4) * 2 + (1 - x if other else x)

    def by_fsdp(three):
        rows = three.shape[0]
        split = three.reshape(rows, 3, 2, 2, heads_dev // 2, 2, HEAD)
        return split.transpose(5, 2, 0, 3, 1, 4, 6).reshape(n_fsdp, rows, 3 * wide)

    def from_fsdp(blocks):
        rows = blocks.shape[1]
        split = blocks.reshape(2, 2, rows, 2, 3, heads_dev // 2, HEAD)
        return split.transpose(4, 2, 1, 3, 5, 0, 6).reshape(3, rows, width)

    def swap_core(blocks):
        mine, give = pick(blocks, c, 2), pick(blocks, 1 - c, 2)
        return in_order(mine, send(give, "core"), c, 2)

    def swap_z(blocks, k):
        return send(pick(blocks, lax.rem(z + k, 4)), f"z{k}")

    def swap_x(blocks):
        mine, give = pick(blocks, x, 1), pick(blocks, 1 - x, 1)
        return in_order(mine, send(give, "x"), x, 1)

    small = jnp.concatenate(
        [w_router.T, shared_gate[None], norm_gain1[None], norm_gain2[None], b_qkv, seg_ids.astype(BF)], axis=0)
    n_small = experts + 6
    small = [small.reshape(1, (n_small + micro) * rows_w)]
    for _ in range(3):
        small.append(send(small[-1], "z1"))
    small = jnp.concatenate(small)
    qkv = by_fsdp(jnp.stack([w_query, w_key, w_value], axis=1))
    arrived = [send(pick(qkv, lax.bitwise_xor(my_fsdp, k)), link) for k, link in ((1, "core"), (2, "y"), (3, "yc"))]
    grad_own = out_grad.reshape(own, width)
    names = jnp.pad(routes.reshape(own, top_count).astype(BF), ((0, 0), (0, LANES - top_count)))
    g_own = [jnp.concatenate([grad_own, names], axis=1)]
    g_pair = []
    routed_mine = jnp.concatenate([ex_gate[0].T, ex_up[0].T, ex_down[0]], axis=0)
    small, arrived, g_own[0], routed_mine = sync(small, arrived, g_own[0], routed_mine)
    for k in range(3):
        qkv = put(qkv, arrived[k], lax.bitwise_xor(my_fsdp, k + 1))
    block = jnp.concatenate([w_out[:, k * wide : (k + 1) * wide] for k in range(n_fsdp)], axis=0)
    block = jnp.concatenate([qkv.reshape(n_fsdp * rows_w, 3 * wide), block], axis=1)
    following = send(block, "z1")
    small = jnp.concatenate([small, send(small, "x")])
    at_pair = send(sync(block, small)[0], "x")
    small = jnp.concatenate([small, send(small, "y")])
    got = send(sync(routed_mine[:264], small)[0], "y")
    small = jnp.concatenate([small, send(small, "core")])
    block, following, at_pair, small, got, routed_mine, sh_gate, sh_up, sh_down, hidden_in = sync(
        block, following, at_pair, small, got, routed_mine, sh_gate, sh_up, sh_down, hidden_in)
    a_blocks = [routed_mine[k * 264 : (k + 1) * 264] for k in range(4)]
    got_blocks = [got]
    weights = jnp.zeros((n_exp,) + block.shape, BF)

    def ring_put(weights, step, mine, other):
        return put(put(weights, mine, slot(step, 0)), other, slot(step, 1))

    first_pair, mine = at_pair, following
    at_pair, following = send(mine, "x"), send(mine, "z1")
    places = jnp.stack(
        [slot(step, other) * 4 + lax.bitwise_xor(my_fsdp, k) for k in (0, 2, 1, 3) for other in range(2) for step in range(4)])
    choice = (jnp.arange(n_all)[:, None] == places[None]).astype(BF)
    small = dot_nn(choice, small).astype(BF).reshape(n_all, n_small + micro, rows_w)
    small = small.transpose(1, 0, 2).reshape(n_small + micro, width)
    router_rows = small[: experts + 1]
    gain_one = small[experts + 1].astype(F32)
    gain_two = small[experts + 2].astype(F32)
    bias = pick(by_fsdp(small[experts + 3 : n_small].astype(F32)[None]), my_fsdp)
    seg_seq = lax.dynamic_slice_in_dim(small[n_small:], my_exp * seq, seq, 1).reshape(micro, n_fsdp, tok)
    hidden = hidden_in.reshape(own, width).astype(F32)
    scaled_one, inverse_one = normalize(hidden)
    normed_one = (scaled_one * gain_one).astype(BF).reshape(micro, tok, width)
    seq_far, seq_near = send(normed_one, "y"), send(normed_one, "core")

    (block, mine, following, at_pair, seq_far, seq_near, normed_one, a_blocks, bias, router_rows, seg_seq,
     sh_gate, sh_up, sh_down) = sync(
        block, mine, following, at_pair, seq_far, seq_near, normed_one, a_blocks, bias, router_rows, seg_seq,
        sh_gate, sh_up, sh_down)

    previous, previous_pair, mine = mine, at_pair, following
    at_pair, following = send(mine, "x"), send(mine, "z1")
    shared_w = pack_shared(sh_gate, sh_up, sh_down, 16, full_cols, rest_cols)
    shared_w = swap_core(shared_w.reshape(4, 2, 2, rows_w, unit_cols))
    weights = ring_put(ring_put(weights, 0, block, first_pair), 1, previous, previous_pair)
    seq_last = send(seq_far, "core")
    got = send(a_blocks[1], "y")
    mine, following, at_pair, got, a_blocks, shared_w, seq_last, weights = sync(
        mine, following, at_pair, got, a_blocks, shared_w, seq_last, weights)
    got_blocks.append(got)

    weights = ring_put(weights, 2, mine, at_pair)
    at_pair = send(following, "x")
    got = send(a_blocks[2], "y")
    shared_z = {1: swap_z(shared_w, 1), 3: swap_z(shared_w, 3)}
    order = lax.bitwise_xor(my_fsdp, jnp.arange(n_fsdp))
    places = (order[:, None] * tok + jnp.arange(tok)[None]).reshape(seq)
    seg_seq = jnp.take(seg_seq, order, axis=1).reshape(micro, seq).astype(jnp.int32)
    normed_seq = jnp.concatenate([normed_one, seq_near, seq_far, seq_last], axis=1).reshape(micro * seq, width)
    cosine, sine = angle_tables(places)
    tables = (cosine, sine, places[:, None], seg_seq.reshape(micro * seq, 1), places[None], seg_seq)
    following, at_pair, got, shared_z, shared_w, a_blocks, weights, tables, normed_seq, g_own[0] = sync(
        following, at_pair, got, shared_z, shared_w, a_blocks, weights, tables, normed_seq, g_own[0])
    got_blocks.append(got)
    weights = ring_put(weights, 3, following, at_pair)
    wqkv = weights.reshape(width, 4 * wide)

    def turned(value):
        value = value.reshape(micro, 2, 2, tok, -1)
        return jnp.concatenate([value[:, :, 1:], value[:, :, :1]], axis=2).reshape(micro * seq, -1)

    core_place = c.reshape(1)
    got = [send(a_blocks[3][:132], "y")]
    far_w = pick(shared_w, lax.rem(z + 2, 4))
    shared_z[2] = [send(far_w[0], "z2")]
    g_pair.append(send(g_own[0], "x"))
    qkv_seq, keep, give = attend(normed_seq, wqkv, bias, tables, seq, core=core_place)
    wo = sync(weights, give)[0]
    wo = [wo[:, k * rows_w : (k + 1) * rows_w, 3 * wide :].reshape(n_exp * rows_w, wide) for k in range(n_fsdp)]
    wo = jnp.concatenate(wo, axis=1)
    got, shared_z, qkv_seq, keep, give, wqkv, wo, far_w, g_pair, a_blocks = sync(
        got, shared_z, qkv_seq, keep, give, wqkv, wo, far_w, g_pair, a_blocks)
    got.append(send(a_blocks[3][132:], "y"))
    shared_z[2].append(send(far_w[1], "z2"))
    arrived = turned(send(give, "core"))
    attended = jnp.where(c == 0, jnp.concatenate([keep, arrived], axis=1), jnp.concatenate([arrived, keep], axis=1))
    attn_part = contract("tc,cd->td", attended, wo).reshape(micro, 2, 2, tok, width)
    attn_part = attn_part[:, :, 0] + send(attn_part[:, :, 1].astype(BF), "core").astype(F32)
    near, last = attn_part[:, 0], attn_part[:, 1].astype(BF)
    last, near, got, shared_z, shared_w, g_own, g_pair = sync(last, near, got, shared_z, shared_w, g_own, g_pair)
    got_blocks += got
    for k in (1, 2, 3):
        arrived = jnp.stack(shared_z[2]) if k == 2 else shared_z[k]
        shared_w = put(shared_w, arrived, lax.rem(z + 4 - k, 4))

    last = send(last, "y")
    shared_w = swap_x(shared_w)
    g_own.append(send(g_own[0], "z1"))

    def blocks_of(mine, other):
        return [mine, other, send(jnp.concatenate([mine, other]), "core")]

    g_four = [blocks_of(g_own[0], g_pair[0])]
    after_attn = hidden + near.reshape(own, width) + last.astype(F32).reshape(own, width)
    scaled_two, inverse_two = normalize(after_attn)
    normed_two = (scaled_two * gain_two).astype(BF)
    x_own, x_pair = [normed_two], []
    shared_w, x_own, after_attn, scaled_two, g_own, g_pair, got_blocks, g_four = sync(
        shared_w, x_own, after_attn, scaled_two, g_own, g_pair, got_blocks, g_four)

    half = unit_cols // 2
    shared_w = shared_w.reshape(16 * rows_w, unit_cols).T
    arrived = [send(shared_w[:half], "y")]
    x_pair.append(send(x_own[0], "x"))
    g_pair.append(send(g_own[1], "x"))
    x_own.append(send(x_own[0], "z1"))
    g_own.append(send(g_own[1], "z1"))
    routed_other = jnp.concatenate(got_blocks, axis=0)
    pad = jnp.zeros((2 * GRAD_TILE - 2 * ex_cols, width), BF)
    routed_w = [
        jnp.concatenate(
            [routed_mine[k * ex_cols : (k + 1) * ex_cols], routed_other[k * ex_cols : (k + 1) * ex_cols], pad], axis=0)
        for k in range(3)
    ]

    arrived, shared_w, x_own, g_own, x_pair, g_pair, routed_w = sync(
        arrived, shared_w, x_own, g_own, x_pair, g_pair, routed_w)
    arrived.append(send(shared_w[half:], "y"))
    x_pair.append(send(x_own[1], "x"))
    g_pair.append(send(g_own[2], "x"))
    x_own.append(send(x_own[1], "z1"))
    x_four = [blocks_of(x_own[0], x_pair[0])]
    behind = jnp.pad(router_rows, ((0, GRAD_TILE - sh_cols - experts - 1), (0, 0)))
    arrived, shared_w, x_four, g_four, x_own, g_own, x_pair, g_pair, routed_w, behind = sync(
        arrived, shared_w, x_four, g_four, x_own, g_own, x_pair, g_pair, routed_w, behind)
    rest_at = 3 * full_cols
    cuts = [
        [(k * full_cols, full_cols), (rest_at + k * rest_cols, rest_cols)] for k in range(3)
    ]
    y_place = y.reshape(1)
    shared_w = join_shared(y_place, shared_w, arrived[0], arrived[1], behind, cuts)

    expert = my_exp.reshape(1)
    fed, near_sums, sums, out_near, out_sums = [], [], [], [], []

    def core_sums(found):
        arrived = send(found[2], "core").astype(F32)
        return [found[0].astype(F32) + arrived[:own], found[1].astype(F32) + arrived[own:]]

    def pair_sums(parts):
        return parts[0] + send(parts[1].astype(BF), "x").astype(F32)

    for step in range(4):
        shared_w, routed_w, x_four, g_four, x_own, g_own, x_pair, g_pair, near_sums, sums, fed, out_near, out_sums = sync(
            shared_w, routed_w, x_four, g_four, x_own, g_own, x_pair, g_pair, near_sums, sums, fed, out_near, out_sums)
        if step == 0:
            x_pair.append(send(x_own[2], "x"))
            x_own.append(send(x_own[2], "z1"))
            g_own.append(send(g_own[2], "z1"))
            x_four.append(blocks_of(x_own[1], x_pair[1]))
            g_four.append(blocks_of(g_own[1], g_pair[1]))
        if step == 1:
            x_pair.append(send(x_own[3], "x"))
            g_pair.append(send(g_own[3], "x"))
            x_four.append(blocks_of(x_own[2], x_pair[2]))
            g_four.append(blocks_of(g_own[2], g_pair[2]))
        if step == 2:
            x_four.append(blocks_of(x_own[3], x_pair[3]))
            g_four.append(blocks_of(g_own[3], g_pair[3]))
        if step >= 1:
            near_sums.append(core_sums(fed[step - 1][2]))
        if step >= 2:
            sums.append(pair_sums(near_sums[step - 2]))
            out_near.append(core_sums(fed[step - 2][3]))
        if step == 3:
            out_sums.append(pair_sums(out_near[0]))
        fed.append(feed(expert, x_four[step], g_four[step], shared_w, routed_w, experts, sh_cols))
    near_sums, sums, fed, x_four, g_four, out_near, out_sums, normed_two = sync(
        near_sums, sums, fed, x_four, g_four, out_near, out_sums, normed_two)

    x_blocks = [item for four_of in x_four for item in four_of]
    g_blocks = [item for four_of in g_four for item in four_of]
    shared_sets = [[fed[step][0][item] for step in range(4)] for item in range(3)]
    routed_sets = [[fed[step][1][item] for step in range(4)] for item in range(3)]
    flying = send(sums[1].astype(BF), "z1")
    sums.append(pair_sums(near_sums[2]))
    near_sums.append(core_sums(fed[3][2]))
    out_near.append(core_sums(fed[2][3]))
    sg_mine, sg_give, su_mine, su_give = weight_grads(y_place, x_blocks, [shared_sets[1], shared_sets[2]], width)
    (sums, near_sums, flying, sg_mine, sg_give, su_mine, su_give, x_blocks, g_blocks, shared_sets, routed_sets,
     out_near, fed) = sync(sums, near_sums, flying, sg_mine, sg_give, su_mine, su_give, x_blocks, g_blocks,
                           shared_sets, routed_sets, out_near, fed)
    sums.append(pair_sums(near_sums[3]))
    flying = send((sums[2] + flying.astype(F32)).astype(BF), "z1")
    sg_got = send(sg_give, "y")
    out_near.append(core_sums(fed[3][3]))
    sd_mine, sd_give = weight_grads(y_place, g_blocks, [shared_sets[0]], width)
    sums, flying, sg_got, su_give, sd_mine, sd_give, x_blocks, g_blocks, routed_sets, out_near, out_sums = sync(
        sums, flying, sg_got, su_give, sd_mine, sd_give, x_blocks, g_blocks, routed_sets, out_near, out_sums)
    flying = send((sums[3] + flying.astype(F32)).astype(BF), "z1")
    su_got = send(su_give, "y")
    out_sums.append(pair_sums(out_near[1]))
    e_parts = (ex_cols, ex_cols // 2, ex_cols // 2)
    ed_grad = weight_grads(y_place, g_blocks, [routed_sets[0]], width, e_parts)
    grad_sum, out_near, out_sums, su_got, sd_give, ed_grad, x_blocks, routed_sets = sync(
        sums[0] + flying.astype(F32), out_near, out_sums, su_got, sd_give, ed_grad, x_blocks, routed_sets)

    own_logits = contract("td,cd->tc", normed_two, router_rows)
    own_probs = jax.nn.softmax(own_logits[:, :experts], axis=-1)
    own_scale = jax.nn.sigmoid(own_logits[:, experts])
    grad_probs = grad_sum[:, width : width + experts]
    grad_router = own_probs * (grad_probs - jnp.sum(own_probs * grad_probs, axis=-1, keepdims=True))
    grad_gate = grad_sum[:, width + experts] * own_scale * (1.0 - own_scale)
    grad_logits = jnp.concatenate([grad_router, grad_gate[:, None]], axis=1).astype(BF)
    grad_normed_two = grad_sum[:, :width] + contract("tc,cd->td", grad_logits, router_rows)
    router_part = contract("tc,td->cd", grad_logits, normed_two)
    grad_after = grad_own.astype(F32) + norm_back(grad_normed_two, scaled_two, inverse_two, gain_two)
    gain_two_part = jnp.sum(grad_normed_two * scaled_two, axis=0)
    low = grad_after.astype(BF).reshape(micro, tok, width)
    sd_got = send(sd_give, "y")
    out_sums.append(pair_sums(out_near[2]))
    flying_out = send(out_sums[1].astype(BF), "z1")
    low, grad_after, out_sums, out_near, sd_got, flying_out, gain_two_part, router_part, x_blocks, routed_sets = sync(
        low, grad_after, out_sums, out_near, sd_got, flying_out, gain_two_part, router_part, x_blocks, routed_sets)
    far, near = send(low, "y"), send(low, "core")
    out_sums.append(pair_sums(out_near[3]))
    flying_out = send((out_sums[2] + flying_out.astype(F32)).astype(BF), "z1")
    shared_grads = fold_shared([(sg_mine, sg_got), (su_mine, su_got), (sd_mine, sd_got)], full_cols, rest_cols)
    shared_grads = shared_grads.reshape(4, 2, 2, rows_w, unit_cols)
    far, near, low, out_sums, flying_out, shared_grads, ed_grad, x_blocks, routed_sets = sync(
        far, near, low, out_sums, flying_out, shared_grads, ed_grad, x_blocks, routed_sets)

    def panel_sum(panel, gives, step):
        return pick(panel, slot(step, 0)).astype(F32) + send(gives[step], "x").astype(F32)

    shared_grads = swap_core(shared_grads)
    flying_out = send((out_sums[3] + flying_out.astype(F32)).astype(BF), "z1")
    grad_attn = jnp.concatenate([low, near, far, send(far, "core")], axis=1).reshape(micro * seq, width)
    grad_attended = contract("td,cd->tc", grad_attn, wo).astype(BF)
    half = wide // 2
    keep = lax.dynamic_slice_in_dim(grad_attended, c * half, half, 1)
    give = lax.dynamic_slice_in_dim(grad_attended, (1 - c) * half, half, 1)
    arrived = turned(send(give, "core"))
    wo_part = contract("tc,td->cd", attended, grad_attn).astype(BF).reshape(n_exp, rows_w, width)
    wo_gives = [pick(wo_part, slot(step, 1)) for step in range(4)]
    shared_far = pick(shared_grads, lax.rem(z + 2, 4))
    shared_grads, shared_far, keep, arrived, flying_out, wo_part, wo_gives, ed_grad, x_blocks, routed_sets = sync(
        shared_grads, shared_far, keep, arrived, flying_out, wo_part, wo_gives, ed_grad, x_blocks, routed_sets)
    hidden_out = (after_attn + out_sums[0] + flying_out.astype(F32)).astype(BF)
    e_got = [send(ed_grad[1], "y")]
    shared_z = {2: send(shared_far, "z2")}
    wo_sums = {step: panel_sum(wo_part, wo_gives, step) for step in (1, 2)}
    behind_rows = 8
    panel_shape = (n_exp, n_fsdp * rows_w + behind_rows, 3 * wide)
    grad_lin, grad_normed_one, panel = attend(
        normed_seq, wqkv, bias, tables, seq, (keep, arrived, qkv_seq), core_place, panel_shape)
    shared_far = {k: pick(shared_grads, lax.rem(z + k, 4)) for k in (1, 3)}
    (grad_lin, grad_normed_one, panel, hidden_out, e_got, shared_z, shared_far, shared_grads, wo_part, wo_gives,
     wo_sums, ed_grad, x_blocks, routed_sets) = sync(
        grad_lin, grad_normed_one, panel, hidden_out, e_got, shared_z, shared_far, shared_grads, wo_part, wo_gives,
        wo_sums, ed_grad, x_blocks, routed_sets)
    parts = grad_normed_one.reshape(micro, 2, 2, tok, width)
    parts = parts[:, :, 0] + send(parts[:, :, 1].astype(BF), "core").astype(F32)
    near, last = parts[:, 0], parts[:, 1].astype(BF)
    e_got.append(send(ed_grad[2], "y"))
    eg_grad = weight_grads(y_place, x_blocks, [routed_sets[1]], width, e_parts)
    for k in (1, 3):
        shared_z[k] = send(shared_far[k], f"z{k}")
    for step in (3, 0):
        wo_sums[step] = panel_sum(wo_part, wo_gives, step)
    gain_one_part = jnp.sum(grad_normed_one * normed_seq.astype(F32), axis=0) / gain_one
    bias_place = put(jnp.zeros((n_fsdp, 1, 3 * wide), F32), jnp.sum(grad_lin.astype(F32), axis=0)[None], my_fsdp)
    bias_place = from_fsdp(bias_place)[:, 0]
    small_part = jnp.concatenate([router_part, gain_one_part[None], gain_two_part[None], bias_place], axis=0)
    small_part = small_part.astype(BF).reshape(n_small, n_exp, n_fsdp, rows_w).transpose(1, 2, 0, 3)
    small_part = small_part.reshape(n_exp, n_fsdp * n_small * rows_w)
    small_part = jnp.pad(small_part, ((0, 0), (0, behind_rows * 3 * wide - small_part.shape[1])))
    panel = lax.dynamic_update_slice_in_dim(
        panel, small_part.reshape(n_exp, behind_rows, 3 * wide), n_fsdp * rows_w, 1)
    gives = [pick(panel, slot(step, 1)) for step in range(4)]
    gives, panel, last, near, e_got, shared_z, shared_grads, wo_sums, eg_grad, x_blocks, routed_sets = sync(
        gives, panel, last, near, e_got, shared_z, shared_grads, wo_sums, eg_grad, x_blocks, routed_sets)

    far = send(last, "y")
    eu_grad = weight_grads(y_place, x_blocks, [routed_sets[2]], width, e_parts)
    e_grads = (eg_grad, eu_grad, ed_grad)
    for k in (1, 2, 3):
        shared_grads = put(shared_grads, shared_z[k], lax.rem(z + 4 - k, 4))
    shared_mine, shared_give = pick(shared_grads, x, 1), pick(shared_grads, 1 - x, 1)
    shared_x, sums = [], {}

    for turn, step in enumerate((1, 2, 3, 0)):
        sums[step] = panel_sum(panel, gives, step)
        shared_x.append(send(shared_give[turn], "x"))
        e_got.append(send(e_grads[turn // 2][1 + turn % 2], "y"))
        if turn == 0:
            flying_wo = send(wo_sums[1].astype(BF), "z1")
            (far, near, sums, e_got, shared_x, shared_give, shared_mine, e_grads, panel, gives, flying_wo,
             wo_sums) = sync(far, near, sums, e_got, shared_x, shared_give, shared_mine, e_grads, panel, gives,
                             flying_wo, wo_sums)
            continue
        if turn == 1:
            routed_grads = {2: ed_grad[0].astype(F32) + jnp.concatenate(e_got[:2]).astype(F32)}
            flying = send(sums[1].astype(BF), "z1")
            grad_normed_one = (near + far.astype(F32)).reshape(own, width)
            in_grad = grad_after + norm_back(grad_normed_one, scaled_one, inverse_one, gain_one)
        else:
            flying = send((sums[turn] + flying.astype(F32)).astype(BF), "z1")
        if turn == 2:
            routed_grads[0] = (eg_grad[0].astype(F32) + jnp.concatenate(e_got[2:4]).astype(F32)).T
        if turn < 3:
            flying_wo = send((wo_sums[turn + 1] + flying_wo.astype(F32)).astype(BF), "z1")
            sums, e_got, shared_x, shared_give, flying, e_grads, panel, gives, flying_wo, in_grad, routed_grads = sync(
                sums, e_got, shared_x, shared_give, flying, e_grads, panel, gives, flying_wo, in_grad, routed_grads)
        else:
            out_own = wo_sums[0] + flying_wo.astype(F32)
            flying, sums, out_own, e_got, shared_x = sync(flying, sums, out_own, e_got, shared_x)
    shared_grads = in_order(shared_mine, jnp.stack(shared_x), x, 1).reshape(16, rows_w, unit_cols)
    shared_own = unpack_shared(shared_grads, full_cols, rest_cols)
    routed_grads[1] = (eu_grad[0].astype(F32) + jnp.concatenate(e_got[4:6]).astype(F32)).T
    total = (sums[0] + flying.astype(F32)).astype(BF)

    count = n_fsdp * rows_w
    small_sum = total[count:].reshape(-1)[: n_fsdp * n_small * rows_w].reshape(n_fsdp, n_small * rows_w)
    small_sum = jnp.pad(small_sum, ((0, 0), (0, 3 * wide - n_small * rows_w)))
    blocks = jnp.concatenate([total[:count, : 3 * wide].reshape(n_fsdp, rows_w, 3 * wide), small_sum[:, None]], axis=1)
    qkv_own = blocks
    for k, link in ((1, "core"), (2, "y"), (3, "yc")):
        place = lax.bitwise_xor(my_fsdp, k)
        qkv_own = put(qkv_own, send(pick(blocks, place), link), place)
    small_own = jnp.sum(qkv_own[:, rows_w, : n_small * rows_w].astype(F32), axis=0).reshape(n_small, rows_w)
    qkv_own = from_fsdp(qkv_own[:, :rows_w]).astype(F32)
    return (
        hidden_out.reshape(micro, tok, width),
        in_grad.reshape(micro, tok, width),
        small_own[experts + 1],
        qkv_own[0],
        qkv_own[1],
        qkv_own[2],
        small_own[experts + 3 :],
        out_own,
        small_own[experts + 2],
        small_own[:experts].T,
        small_own[experts],
        shared_own[0],
        shared_own[1],
        shared_own[2],
        routed_grads[0][None],
        routed_grads[1][None],
        routed_grads[2][None],
    )


def on_device_any(
    hidden_in, seg_ids, routes, out_grad, norm_gain1, w_query, w_key, w_value, b_qkv, w_out,
    norm_gain2, w_router, shared_gate, sh_gate, sh_up, sh_down, ex_gate, ex_up, ex_down,
):
    links = Links()
    micro, tok, width = hidden_in.shape
    experts = w_router.shape[1]
    rows_w = w_query.shape[0]
    n_exp, n_fsdp, n_all = links.n_exp, links.n_fsdp, links.n_all
    my_exp, my_fsdp = links.my_exp, links.my_fsdp
    half_f, core_f = my_fsdp // 2, lax.rem(my_fsdp, 2)
    heads_dev = HEADS // n_fsdp
    wide = heads_dev * HEAD
    seq = tok * n_fsdp
    own = micro * tok
    sh_cols = SHARED_FF // n_all
    ex_cols = ex_gate.shape[2]

    def by_fsdp(three):
        rows = three.shape[0]
        split = three.reshape(rows, 3, 2, 2, heads_dev // 2, 2, HEAD)
        return split.transpose(5, 2, 0, 3, 1, 4, 6).reshape(n_fsdp, rows, 3 * wide)

    def from_fsdp(blocks):
        rows = blocks.shape[1]
        split = blocks.reshape(2, 2, rows, 2, 3, heads_dev // 2, HEAD)
        return split.transpose(4, 2, 1, 3, 5, 0, 6).reshape(3, rows, width)

    small = jnp.concatenate([w_router.T, shared_gate[None], norm_gain1[None], norm_gain2[None], b_qkv], axis=0)
    n_small = small.shape[0]
    small = lax.all_gather(small, ALL, axis=1, tiled=True)
    router_rows = small[: experts + 1]
    gain_one = small[experts + 1].astype(F32)
    gain_two = small[experts + 2].astype(F32)
    bias = by_fsdp(small[experts + 3 :].astype(F32)[None])
    bias = lax.dynamic_index_in_dim(bias, my_fsdp, 0, keepdims=False)

    x = hidden_in.reshape(own, width).astype(F32)
    scaled_one, inverse_one = normalize(x)
    normed_one = (scaled_one * gain_one).astype(BF)
    normed_seq = links.gather_seq(normed_one.reshape(micro, tok, width)).reshape(micro * seq, width)

    qkv = by_fsdp(jnp.stack([w_query, w_key, w_value], axis=1))
    qkv = links.swap_fsdp(qkv).reshape(n_fsdp * rows_w, 3 * wide)
    wqkv = links.gather_rows(qkv).reshape(width, 3 * wide)
    wo = lax.all_gather(w_out, ALL, axis=0, tiled=True).reshape(2, heads_dev, 2, HEAD, width)
    wo = lax.dynamic_index_in_dim(wo, core_f, 0, keepdims=False)
    wo = lax.dynamic_index_in_dim(wo, half_f, 1, keepdims=False).reshape(wide, width)

    tile_cols = sh_cols // LANES * LANES
    rest_cols = sh_cols - tile_cols

    def by_owner(weight):
        full = weight[:, : n_all * tile_cols].reshape(rows_w, n_all, tile_cols).transpose(1, 0, 2)
        rest = weight[:, n_all * tile_cols :].reshape(rows_w, n_all, rest_cols).transpose(1, 0, 2)
        return full, rest

    def from_owner(full, rest):
        return jnp.concatenate(
            [full.transpose(1, 0, 2).reshape(rows_w, -1), rest.transpose(1, 0, 2).reshape(rows_w, -1)], axis=1
        )

    pieces = [by_owner(weight) for weight in (sh_gate, sh_up, sh_down)]
    shared_w = jnp.concatenate([piece[0] for piece in pieces] + [piece[1] for piece in pieces], axis=2)
    shared_w = lax.all_to_all(shared_w, ALL, split_axis=0, concat_axis=0, tiled=True)
    shared_w = shared_w.reshape(width, 3 * sh_cols).T

    def three(rows):
        return [
            jnp.concatenate(
                [rows[k * tile_cols : (k + 1) * tile_cols],
                 rows[3 * tile_cols + k * rest_cols : 3 * tile_cols + (k + 1) * rest_cols]], axis=0)
            for k in range(3)
        ]

    shared_other = links.partner(shared_w, 2)
    routed_w = jnp.concatenate([ex_gate[0].T, ex_up[0].T, ex_down[0]], axis=0)
    halves = [[0, 2], [1, 3]]
    routed_w = lax.all_gather(routed_w, "fsdp", axis=0, axis_index_groups=halves)
    routed_w = [routed_w[:, k * ex_cols : (k + 1) * ex_cols].reshape(2 * ex_cols, width) for k in range(3)]
    units = 2 * (sh_cols + ex_cols)
    pad_rows = -(units + experts + 1) % LANES
    pad = jnp.zeros((pad_rows + experts + 1, width), BF)
    behind = (jnp.pad(router_rows, ((0, pad_rows), (0, 0))), pad, pad)
    wg, wu, wd = [
        jnp.concatenate(pieces, axis=0)
        for pieces in zip(three(shared_w), three(shared_other), routed_w, behind)
    ]
    shared_units = 2 * sh_cols

    grad_own = out_grad.reshape(own, width)
    names = jnp.pad(routes.reshape(own, -1).astype(BF), ((0, 0), (0, LANES - routes.shape[2])))
    grad_near = lax.all_gather(jnp.concatenate([grad_own, names], axis=1), "expert", axis=0)
    grad_far = links.partner(grad_near, 1)

    order = lax.bitwise_xor(my_fsdp, jnp.arange(n_fsdp))
    places = (order[:, None] * tok + jnp.arange(tok)[None]).reshape(seq)
    seg_seq = links.gather_seq(seg_ids)
    cosine, sine = angle_tables(places)
    tables = (cosine, sine, places[:, None], seg_seq.reshape(micro * seq, 1), places[None], seg_seq)
    qkv_seq, attended = attend(normed_seq, wqkv, bias, tables, seq)
    attn_part = contract("tc,cd->td", attended, wo).reshape(micro, n_fsdp, tok, width)
    attn_sum = links.sum_four([attn_part[:, k] for k in range(4)]).reshape(own, width)
    after_attn = x + attn_sum
    scaled_two, inverse_two = normalize(after_attn)
    normed_two = (scaled_two * gain_two).astype(BF)

    near = lax.all_gather(normed_two, "expert", axis=0, tiled=True)
    normed_all = jnp.concatenate([near, links.partner(near, 1)], axis=0)
    grad_all = jnp.concatenate([grad_near, grad_far], axis=0).reshape(2 * n_exp * own, -1)
    named = jnp.sum((grad_all[:, width : width + routes.shape[2]] == my_exp.astype(BF)).astype(F32), axis=1)
    grad_part, out_part, wg_grad, wu_grad, wd_grad = feed_plain(
        normed_all, grad_all[:, :width], named, my_exp, wg, wu, wd, router_rows, experts, shared_units
    )

    def summed(part):
        count = n_exp * own
        total = part[:count] + links.partner(part[count:].astype(BF), 1).astype(F32)
        return links.sum_rows(total.reshape(n_exp, own, -1))

    grad_sum, out_sum = summed(grad_part), summed(out_part)
    wg_grad, wu_grad, wd_grad = [item.astype(BF) for item in (wg_grad, wu_grad, wd_grad)]
    hidden_out = (after_attn + out_sum).astype(BF)

    own_logits = contract("td,cd->tc", normed_two, router_rows)
    own_probs = jax.nn.softmax(own_logits[:, :experts], axis=-1)
    own_scale = jax.nn.sigmoid(own_logits[:, experts])
    grad_probs = grad_sum[:, width : width + experts]
    grad_router = own_probs * (grad_probs - jnp.sum(own_probs * grad_probs, axis=-1, keepdims=True))
    grad_gate = grad_sum[:, width + experts] * own_scale * (1.0 - own_scale)
    grad_logits = jnp.concatenate([grad_router, grad_gate[:, None]], axis=1).astype(BF)
    grad_normed_two = grad_sum[:, :width] + contract("tc,cd->td", grad_logits, router_rows)
    router_part = contract("tc,td->cd", grad_logits, normed_two)

    grad_after = grad_own.astype(F32) + norm_back(grad_normed_two, scaled_two, inverse_two, gain_two)
    gain_two_part = jnp.sum(grad_normed_two * scaled_two, axis=0)

    grad_attn = links.gather_seq(grad_after.astype(BF).reshape(micro, tok, width)).reshape(micro * seq, width)
    grad_lin, grad_normed_one = attend(normed_seq, wqkv, bias, tables, seq, (grad_attn, wo, qkv_seq))
    gain_one_part = jnp.sum(grad_normed_one * normed_seq.astype(F32), axis=0) / gain_one
    grad_normed_one = grad_normed_one.reshape(micro, n_fsdp, tok, width)
    grad_normed_one = links.sum_four([grad_normed_one[:, k] for k in range(4)]).reshape(own, width)
    in_grad = grad_after + norm_back(grad_normed_one, scaled_one, inverse_one, gain_one)
    out_grad_part = contract("tc,td->cd", attended, grad_attn).astype(BF)
    qkv_part = contract("td,tc->dc", normed_seq, grad_lin).astype(BF)
    bias_part = jnp.sum(grad_lin.astype(F32), axis=0)

    out_place = jnp.zeros((2, heads_dev, 2, HEAD, width), BF)
    out_place = lax.dynamic_update_slice(
        out_place, out_grad_part.reshape(1, heads_dev, 1, HEAD, width), (core_f, 0, half_f, 0, 0)
    )
    out_own = lax.psum_scatter(
        out_place.reshape(width, width), ALL, scatter_dimension=0, tiled=True
    ).astype(F32)
    bias_place = jnp.zeros((n_fsdp, 1, 3 * wide), F32)
    bias_place = from_fsdp(lax.dynamic_update_index_in_dim(bias_place, bias_part[None], my_fsdp, 0))[:, 0]
    small_part = jnp.concatenate([router_part, gain_one_part[None], gain_two_part[None], bias_place], axis=0)
    small_part = small_part.astype(BF).reshape(n_small, n_exp, n_fsdp, rows_w).transpose(1, 2, 0, 3)
    behind_rows = -(-n_fsdp * n_small * rows_w // (3 * wide) // 8) * 8
    room = behind_rows * 3 * wide
    small_part = small_part.reshape(n_exp, n_fsdp * n_small * rows_w)
    small_part = jnp.pad(small_part, ((0, 0), (0, room - small_part.shape[1])))
    qkv_part = jnp.concatenate(
        [qkv_part.reshape(n_exp, n_fsdp * rows_w, 3 * wide), small_part.reshape(n_exp, behind_rows, 3 * wide)], axis=1
    )
    qkv_sum = links.sum_rows(qkv_part).astype(BF)
    small_sum = qkv_sum[n_fsdp * rows_w :].reshape(-1)[: n_fsdp * n_small * rows_w].reshape(n_fsdp, n_small * rows_w)
    small_sum = jnp.pad(small_sum, ((0, 0), (0, 3 * wide - n_small * rows_w)))
    qkv_sum = qkv_sum[: n_fsdp * rows_w].reshape(n_fsdp, rows_w, 3 * wide)
    qkv_own = links.swap_fsdp(jnp.concatenate([qkv_sum, small_sum[:, None]], axis=1))
    small_own = jnp.sum(qkv_own[:, rows_w, : n_small * rows_w].astype(F32), axis=0).reshape(n_small, rows_w)
    qkv_own = from_fsdp(qkv_own[:, :rows_w]).astype(F32)

    grads = (wg_grad, wu_grad, wd_grad)
    shared_mine = jnp.concatenate(
        [grad[:tile_cols] for grad in grads] + [grad[tile_cols:sh_cols] for grad in grads], axis=0)
    shared_give = jnp.concatenate(
        [grad[sh_cols : sh_cols + tile_cols] for grad in grads]
        + [grad[sh_cols + tile_cols : 2 * sh_cols] for grad in grads], axis=0)
    shared_got = links.partner(shared_give, 2)
    shared_grads = (shared_mine.astype(F32) + shared_got.astype(F32)).astype(BF)
    shared_own = lax.all_to_all(
        shared_grads.T.reshape(n_all, rows_w, 3 * sh_cols), ALL, split_axis=0, concat_axis=0, tiled=True
    )
    cut = 3 * tile_cols
    shared_own = [
        from_owner(
            shared_own[:, :, k * tile_cols : (k + 1) * tile_cols],
            shared_own[:, :, cut + k * rest_cols : cut + (k + 1) * rest_cols],
        ).astype(F32)
        for k in range(3)
    ]
    routed_grads = jnp.stack(
        [
            jnp.concatenate([grad[low : low + ex_cols] for grad in grads], axis=0)
            for low in (shared_units, shared_units + ex_cols)
        ]
    )
    routed_grads = lax.psum_scatter(routed_grads, "fsdp", scatter_dimension=0, axis_index_groups=halves).astype(F32)
    routed_grads = [routed_grads[k * ex_cols : (k + 1) * ex_cols] for k in range(3)]
    return (
        hidden_out.reshape(micro, tok, width),
        in_grad.reshape(micro, tok, width),
        small_own[experts + 1],
        qkv_own[0],
        qkv_own[1],
        qkv_own[2],
        small_own[experts + 3 :],
        out_own,
        small_own[experts + 2],
        small_own[:experts].T,
        small_own[experts],
        shared_own[0],
        shared_own[1],
        shared_own[2],
        routed_grads[0].T[None],
        routed_grads[1].T[None],
        routed_grads[2][None],
    )


def solution(mesh):
    rows = P(ALL, None)
    tokens = P(None, ALL, None)
    in_specs = (
        tokens, P(None, ALL), tokens, tokens, P(ALL), rows, rows, rows, P(None, ALL), rows,
        P(ALL), rows, P(ALL), rows, rows, rows,
        P("expert", None, "fsdp"), P("expert", None, "fsdp"), P("expert", "fsdp", None),
    )
    out_specs = (
        tokens, tokens, P(ALL), rows, rows, rows, P(None, ALL), rows, P(ALL), rows, P(ALL),
        rows, rows, rows,
        P("expert", None, "fsdp"), P("expert", None, "fsdp"), P("expert", "fsdp", None),
    )
    on_device = on_device_ring if mesh.shape["expert"] == 8 and mesh.shape["fsdp"] == 4 else on_device_any
    return jax.shard_map(on_device, mesh=mesh, in_specs=in_specs, out_specs=out_specs, check_vma=False)
```

```python
import functools

import jax
import jax.numpy as jnp
from jax import lax
from jax.experimental import pallas as pl
from jax.experimental.pallas import tpu as pltpu
from jax.sharding import PartitionSpec as P

HEADS = 16
HEAD = 128
SHARED_FF = 5632
EPSILON = 1e-06
ROPE_BASE = 1000000.0
MASKED = -1e30
ALL = ("expert", "fsdp")
BF = jnp.bfloat16
F32 = jnp.float32
LANES = 128
COLS = 1024
GRAD_TILE = 384


def normalize(values):
    inverse = lax.rsqrt(jnp.mean(values * values, axis=-1, keepdims=True) + EPSILON)
    return (values * inverse, inverse)


def norm_back(grad_normed, scaled, inverse, gain_vec):
    grad_scaled = grad_normed * gain_vec
    return inverse * (grad_scaled - scaled * jnp.mean(grad_scaled * scaled, axis=-1, keepdims=True))


def angle_tables(places):
    inverse = 1.0 / ROPE_BASE ** (jnp.arange(0, HEAD, 2).astype(F32) / HEAD)
    angles = places.astype(F32)[:, None] * inverse[None, :]
    cosine, sine = jnp.cos(angles), jnp.sin(angles)
    return jnp.concatenate([cosine, cosine], axis=1), jnp.concatenate([-sine, sine], axis=1)


def silu_parts(pre_act):
    logistic = 1.0 / (1.0 + jnp.exp(-pre_act))
    return (pre_act * logistic, logistic * (1.0 + pre_act * (1.0 - logistic)))


def contract(pattern, left_op, right_op):
    return jnp.einsum(pattern, left_op, right_op, preferred_element_type=F32)


def dot_nt(left_op, right_op):
    return lax.dot_general(left_op, right_op, (((1,), (1,)), ((), ())), preferred_element_type=F32)


def dot_nn(left_op, right_op):
    return lax.dot_general(left_op, right_op, (((1,), (0,)), ((), ())), preferred_element_type=F32)


def dot_tn(left_op, right_op):
    return lax.dot_general(left_op, right_op, (((0,), (0,)), ((), ())), preferred_element_type=F32)


def after(value, *earlier):
    return lax.optimization_barrier((value, earlier))[0]


class Links:
    def __init__(self):
        self.n_exp = lax.axis_size("expert")
        self.n_fsdp = lax.axis_size("fsdp")
        self.my_exp = lax.axis_index("expert")
        self.my_fsdp = lax.axis_index("fsdp")
        self.n_all = self.n_exp * self.n_fsdp

    def partner(self, value, bit):
        pairs = [
            (e * self.n_fsdp + f, e * self.n_fsdp + (f ^ bit)) for e in range(self.n_exp) for f in range(self.n_fsdp)
        ]
        return lax.ppermute(value, ALL, pairs)

    def gather_rows(self, value):
        return lax.all_gather(value, "expert", axis=0)

    def sum_rows(self, value):
        return lax.psum_scatter(value.astype(BF), "expert", scatter_dimension=0).astype(F32)

    def swap_fsdp(self, value):
        result = value
        for bit in range(1, self.n_fsdp):
            other = lax.bitwise_xor(self.my_fsdp, bit)
            block = lax.dynamic_index_in_dim(value, other, 0, keepdims=False)
            result = lax.dynamic_update_index_in_dim(result, self.partner(block, bit), other, 0)
        return result

    def gather_four(self, value):
        far = self.partner(value, 2)
        return [value, self.partner(value, 1), far, self.partner(far, 1)]

    def gather_seq(self, value):
        return jnp.concatenate(self.gather_four(value), axis=1)

    def sum_four(self, parts):
        far = (parts[2].astype(F32) + self.partner(parts[3].astype(BF), 1).astype(F32)).astype(BF)
        near = parts[0].astype(F32) + self.partner(parts[1].astype(BF), 1).astype(F32)
        return near + self.partner(far, 2).astype(F32)


def attend_kernel(heads, seq, scale, split, x_ref, w_ref, bias_ref, cos_ref, sin_ref, place_ref, seg_ref,
                  place_row_ref, seg_row_ref, core_ref, qkv_ref, *out_refs):
    lin = dot_nn(x_ref[...], w_ref[...]) + bias_ref[...]
    cosine, sine = cos_ref[...], sin_ref[...]
    span = heads * HEAD
    for micro in range(x_ref.shape[0] // seq):
        low, high = micro * seq, (micro + 1) * seq
        visible = (place_row_ref[...] <= place_ref[...]) & (seg_row_ref[micro : micro + 1, :] == seg_ref[low:high, :])
        found = []
        for head in range(heads):
            at = head * HEAD
            query = lin[low:high, at : at + HEAD]
            key = lin[low:high, span + at : span + at + HEAD]
            value = lin[low:high, 2 * span + at : 2 * span + at + HEAD].astype(BF)
            query = (query * cosine + pltpu.roll(query, HEAD // 2, 1) * sine).astype(BF)
            key = (key * cosine + pltpu.roll(key, HEAD // 2, 1) * sine).astype(BF)
            scores = jnp.where(visible, dot_nt(query, key) * scale, MASKED)
            exps = jnp.exp(scores - jnp.max(scores, axis=1, keepdims=True))
            probs = exps / jnp.sum(exps, axis=1, keepdims=True)
            found.append(dot_nn(probs.astype(BF), value))
            qkv_ref[low:high, at : at + HEAD] = query
            qkv_ref[low:high, span + at : span + at + HEAD] = key
            qkv_ref[low:high, 2 * span + at : 2 * span + at + HEAD] = value
        if not split:
            out_refs[0][low:high, :] = jnp.concatenate(found, axis=1).astype(BF)
            continue
        first = jnp.concatenate([item[:, : HEAD // 2] for item in found], axis=1)
        second = jnp.concatenate([item[:, HEAD // 2 :] for item in found], axis=1)
        out_refs[0][low:high, :] = jnp.where(core_ref[0] == 0, first, second).astype(BF)
        out_refs[1][low:high, :] = jnp.where(core_ref[0] == 0, second, first).astype(BF)


def attend_back_kernel(heads, seq, scale, split, grad_ref, other_ref, qkv_ref, cos_ref, sin_ref, place_ref, seg_ref,
                       place_row_ref, seg_row_ref, core_ref, w_ref, x_ref, lin_ref, normed_ref, gain_ref, *panel_refs):
    cosine, sine = cos_ref[...], sin_ref[...]
    span = heads * HEAD
    if split:
        first = jnp.where(core_ref[0] == 0, grad_ref[...], other_ref[...])
        second = jnp.where(core_ref[0] == 0, other_ref[...], grad_ref[...])
        half = HEAD // 2
        grad_out = jnp.concatenate(
            [part[:, k * half : (k + 1) * half] for k in range(heads) for part in (first, second)], axis=1)
    else:
        grad_out = dot_nt(grad_ref[...], other_ref[...]).astype(BF)
    for micro in range(grad_ref.shape[0] // seq):
        low, high = micro * seq, (micro + 1) * seq
        visible = (place_row_ref[...] <= place_ref[...]) & (seg_row_ref[micro : micro + 1, :] == seg_ref[low:high, :])
        for head in range(heads):
            at = head * HEAD
            query = qkv_ref[low:high, at : at + HEAD]
            key = qkv_ref[low:high, span + at : span + at + HEAD]
            value = qkv_ref[low:high, 2 * span + at : 2 * span + at + HEAD]
            grad = grad_out[low:high, at : at + HEAD]
            scores = jnp.where(visible, dot_nt(query, key) * scale, MASKED)
            exps = jnp.exp(scores - jnp.max(scores, axis=1, keepdims=True))
            probs = exps / jnp.sum(exps, axis=1, keepdims=True)
            grad_probs = dot_nt(grad, value)
            grad_value = dot_tn(probs.astype(BF), grad)
            grad_scores = probs * (grad_probs - jnp.sum(probs * grad_probs, axis=1, keepdims=True))
            grad_scores = grad_scores.astype(BF)
            grad_query = dot_nn(grad_scores, key) * scale
            grad_key = dot_tn(grad_scores, query) * scale
            grad_query = grad_query * cosine - pltpu.roll(grad_query, HEAD // 2, 1) * sine
            grad_key = grad_key * cosine - pltpu.roll(grad_key, HEAD // 2, 1) * sine
            lin_ref[low:high, at : at + HEAD] = grad_query.astype(BF)
            lin_ref[low:high, span + at : span + at + HEAD] = grad_key.astype(BF)
            lin_ref[low:high, 2 * span + at : 2 * span + at + HEAD] = grad_value.astype(BF)
    if split:
        panel_ref = panel_refs[0]
        count, rows = panel_ref.shape[0], x_ref.shape[1] // panel_ref.shape[0]
        grad_w = dot_tn(x_ref[...], lin_ref[...]).astype(BF)
        for k in range(count):
            panel_ref[k, :rows, :] = grad_w[k * rows : (k + 1) * rows, :]
        behind = panel_ref.shape[1] - rows
        panel_ref[:, rows:, :] = jnp.zeros((count, behind, panel_ref.shape[2]), BF)
    part = dot_nt(lin_ref[...], w_ref[...])

    @pl.when(pl.program_id(0) == 0)
    def _():
        normed_ref[...] = part

    @pl.when(pl.program_id(0) > 0)
    def _():
        total = normed_ref[...] + part
        normed_ref[...] = total
        gain_ref[...] = jnp.sum(total * x_ref[...].astype(F32), axis=0, keepdims=True)


def whole(shape):
    return pl.BlockSpec(shape, lambda *_: (0,) * len(shape))


def attend(normed, wqkv, bias, tables, seq, back=None, core=None, panel=None):
    cosine, sine, place, seg, place_row, seg_row = tables
    rows = normed.shape[0]
    pairs = 2
    wide3 = bias.shape[1]
    heads = wide3 // 3 // HEAD // pairs
    span = heads * HEAD
    scale = HEAD ** (-0.5)
    split = core is not None
    common = (cosine, sine, place, seg, place_row, seg_row, core if split else jnp.zeros((1,), jnp.int32))
    common_specs = [whole(item.shape) for item in common[:-1]] + [pl.BlockSpec(memory_space=pltpu.SMEM)]
    params = pltpu.CompilerParams(vmem_limit_bytes=48 * 2**20)
    cost = pl.CostEstimate(flops=10**8, bytes_accessed=10**6, transcendentals=10**5)
    columns, count = (span // 2, 2) if split else (span, 1)
    kept = pl.BlockSpec((rows, columns), lambda p: (0, p))
    if back is None:
        return pl.pallas_call(
            functools.partial(attend_kernel, heads, seq, scale, split),
            grid=(pairs,),
            in_specs=[
                whole(normed.shape),
                pl.BlockSpec((wqkv.shape[0], 3 * span), lambda p: (0, p)),
                pl.BlockSpec((1, 3 * span), lambda p: (0, p)),
            ] + common_specs,
            out_specs=[pl.BlockSpec((rows, 3 * span), lambda p: (0, p))] + [kept] * count,
            out_shape=[jax.ShapeDtypeStruct((rows, wide3), BF)]
            + [jax.ShapeDtypeStruct((rows, pairs * columns), BF)] * count,
            compiler_params=params,
            cost_estimate=cost,
            name="attend",
        )(normed, wqkv, bias, *common)
    grad, other, qkv = back
    return pl.pallas_call(
        functools.partial(attend_back_kernel, heads, seq, scale, split),
        grid=(pairs,),
        in_specs=([kept, kept] if split else [whole(grad.shape), pl.BlockSpec((span, other.shape[1]), lambda p: (p, 0))])
        + [pl.BlockSpec((rows, 3 * span), lambda p: (0, p))]
        + common_specs
        + [pl.BlockSpec((wqkv.shape[0], 3 * span), lambda p: (0, p)), whole(normed.shape)],
        out_specs=[
            pl.BlockSpec((rows, 3 * span), lambda p: (0, p)), whole((rows, wqkv.shape[0])), whole((1, wqkv.shape[0]))]
        + ([pl.BlockSpec(panel[:2] + (3 * span,), lambda p: (0, 0, p))] if split else []),
        out_shape=[jax.ShapeDtypeStruct((rows, wide3), BF)]
        + [jax.ShapeDtypeStruct((count, wqkv.shape[0]), F32) for count in (rows, 1)]
        + ([jax.ShapeDtypeStruct(panel, BF)] if split else []),
        compiler_params=params,
        cost_estimate=cost,
        name="attend_back",
    )(grad, other, qkv, *common, wqkv, normed)


def feed_kernel(experts, shared, expert_ref, *refs):
    x_refs, g_refs = refs[:3], refs[3:6]
    weights = (refs[6:9], refs[9:12])
    unit_refs, gn_refs, out_refs = refs[12:18], refs[18:21], refs[21:24]
    x_all, g_all = refs[24:26]
    units = (refs[26:29], refs[29:32])
    gn, out, sems = refs[32:]
    own, width = x_refs[0].shape
    rows = 4 * own
    expert = expert_ref[0]

    def block(k):
        return pl.ds(k * own, 2 * own if k == 2 else own)

    def start(number, source, target):
        copy = pltpu.make_async_copy(source, target, sems.at[number])
        copy.start()
        return copy

    x_copies = [start(k, x_refs[k], x_all.at[block(k), :]) for k in range(3)]
    g_copies = [start(3 + k, g_refs[k], g_all.at[block(k), :]) for k in range(3)]
    for copy in x_copies:
        copy.wait()
    gates = [dot_nt(x_all[...], weights[k][0][...]) for k in range(2)]
    for copy in g_copies:
        copy.wait()
    names = g_all[:, width:].astype(F32)
    lane = lax.broadcasted_iota(jnp.int32, names.shape, 1)
    hit = jnp.where((lane < 4) & (names == expert.astype(F32)), 1.0, 0.0)
    hit = jnp.sum(hit, axis=1, keepdims=True)
    first = shared // LANES * LANES
    logits = gates[0][:, first : first + LANES]
    lane = lane - (shared - first)
    is_expert = (lane >= 0) & (lane < experts)
    scores = jnp.where(is_expert, logits, MASKED)
    exps = jnp.where(is_expert, jnp.exp(scores - jnp.max(scores, axis=1, keepdims=True)), 0.0)
    mine = jnp.sum(jnp.where(lane == expert, exps, 0.0), axis=1, keepdims=True)
    mine = mine / jnp.sum(exps, axis=1, keepdims=True)
    last = jnp.sum(jnp.where(lane == experts, logits, 0.0), axis=1, keepdims=True)
    scales = (1.0 / (1.0 + jnp.exp(-last)), mine * hit)
    dots, copies = [], []
    for k in range(2):
        hs, dg, du = units[k]
        act, slope = silu_parts(gates[k])
        up = dot_nt(x_all[...], weights[k][1][...])
        grad = dot_nt(g_all[:, :width], weights[k][2][...])
        hidden = act * up
        dots.append(jnp.sum(hidden * grad, axis=1, keepdims=True))
        grad = grad * scales[k]
        hs[...] = (hidden * scales[k]).astype(BF)
        dg[...] = (grad * up * slope).astype(BF)
        du[...] = (grad * act).astype(BF)
        copies += [
            start(3 * k + j, source, target) for j, (source, target) in enumerate(zip((hs, dg, du), unit_refs[3 * k :]))
        ]
    lane = lax.broadcasted_iota(jnp.int32, (rows, LANES), 1)
    extra = jnp.where(lane == expert, dots[1] * hit, 0.0) + jnp.where(lane == experts, dots[0], 0.0)
    gn[:, width:] = extra.astype(BF)
    total = dot_nn(units[0][1][...], weights[0][0][...]) + dot_nn(units[0][2][...], weights[0][1][...])
    total += dot_nn(units[1][1][...], weights[1][0][...]) + dot_nn(units[1][2][...], weights[1][1][...])
    gn[:, :width] = total.astype(BF)
    copies += [start(6 + k, gn.at[block(k), :], gn_refs[k]) for k in range(3)]
    total = dot_nn(units[0][0][...], weights[0][2][...]) + dot_nn(units[1][0][...], weights[1][2][...])
    out[...] = total.astype(BF)
    copies += [start(9 + k, out.at[block(k), :], out_refs[k]) for k in range(3)]
    for copy in copies:
        copy.wait()


def feed(expert, x_blocks, g_blocks, shared_w, routed_w, experts, shared):
    own, width = x_blocks[0].shape
    rows = 4 * own
    wide = g_blocks[0].shape[1]
    counts = (shared_w[0].shape[0], routed_w[0].shape[0])
    anywhere = pl.BlockSpec(memory_space=pl.ANY)
    weights = [pltpu.with_memory_space_constraint(weight, pltpu.VMEM) for weight in (*shared_w, *routed_w)]
    found = pl.pallas_call(
        functools.partial(feed_kernel, experts, shared),
        in_specs=[pl.BlockSpec(memory_space=pltpu.SMEM)]
        + [anywhere] * 6
        + [pl.BlockSpec(memory_space=pltpu.VMEM)] * 6,
        out_specs=[anywhere] * 12,
        scratch_shapes=[pltpu.VMEM((rows, width), BF), pltpu.VMEM((rows, wide), BF)]
        + [pltpu.VMEM((rows, count), BF) for count in counts for _ in range(3)]
        + [pltpu.VMEM((rows, wide), BF), pltpu.VMEM((rows, width), BF), pltpu.SemaphoreType.DMA((12,))],
        out_shape=[jax.ShapeDtypeStruct((rows, count), BF) for count in counts for _ in range(3)]
        + [jax.ShapeDtypeStruct((count, columns), BF) for columns in (wide, width) for count in (own, own, 2 * own)],
        compiler_params=pltpu.CompilerParams(vmem_limit_bytes=42 * 2**20),
        cost_estimate=pl.CostEstimate(flops=16 * 10**9, bytes_accessed=3 * 10**7, transcendentals=10**6),
        name="feed",
    )(expert, *x_blocks, *g_blocks, *weights)
    return found[:3], found[3:6], found[6:9], found[9:12]


SMALL_COST = pl.CostEstimate(flops=0, bytes_accessed=10**6, transcendentals=0)


def pack_kernel(full, rest, gate_ref, up_ref, down_ref, out_ref):
    count = out_ref.shape[0]
    refs = (gate_ref, up_ref, down_ref)
    for j in range(count):
        for k in range(3):
            out_ref[j, :, k * full : (k + 1) * full] = refs[k][:, j * full : (j + 1) * full]
        low = count * full + j * rest
        out_ref[j, :, 3 * full :] = jnp.concatenate([ref[:, low : low + rest] for ref in refs], axis=1)


def pack_shared(gate, up, down, count, full, rest):
    vmem = pl.BlockSpec(memory_space=pltpu.VMEM)
    return pl.pallas_call(
        functools.partial(pack_kernel, full, rest),
        in_specs=[vmem] * 3,
        out_specs=vmem,
        out_shape=jax.ShapeDtypeStruct((count, gate.shape[0], 3 * (full + rest)), BF),
        compiler_params=pltpu.CompilerParams(vmem_limit_bytes=16 * 2**20),
        cost_estimate=SMALL_COST,
        name="pack_shared",
    )(gate, up, down)


def unpack_kernel(full, rest, order_ref, in_ref, *out_refs):
    count = in_ref.shape[0]
    for k in range(3):
        for j in range(count):
            out_refs[k][:, j * full : (j + 1) * full] = in_ref[order_ref[j], :, k * full : (k + 1) * full].astype(F32)
        low = 3 * full + k * rest
        for j in range(0, count, 4):
            at = count * full + j * rest
            piece = jnp.concatenate([in_ref[order_ref[j + i], :, low : low + rest] for i in range(4)], axis=1)
            out_refs[k][:, at : at + 4 * rest] = piece.astype(F32)


def unpack_shared(blocks, order, full, rest):
    count, rows, _ = blocks.shape
    vmem = pl.BlockSpec(memory_space=pltpu.VMEM)
    return pl.pallas_call(
        functools.partial(unpack_kernel, full, rest),
        in_specs=[pl.BlockSpec(memory_space=pltpu.SMEM), vmem],
        out_specs=[vmem] * 3,
        out_shape=[jax.ShapeDtypeStruct((rows, count * (full + rest)), F32)] * 3,
        compiler_params=pltpu.CompilerParams(vmem_limit_bytes=16 * 2**20),
        cost_estimate=SMALL_COST,
        name="unpack_shared",
    )(order, blocks)


def fold_kernel(full, rest, *refs):
    out_ref, rests = refs[6], []
    for k in range(3):
        total = refs[2 * k][...].astype(F32) + refs[2 * k + 1][...].astype(F32)
        total = total.T.astype(BF)
        out_ref[:, k * full : (k + 1) * full] = total[:, :full]
        rests.append(total[:, full : full + rest])
    out_ref[:, 3 * full :] = jnp.concatenate(rests, axis=1)


def fold_shared(pairs, full, rest):
    vmem = pl.BlockSpec(memory_space=pltpu.VMEM)
    return pl.pallas_call(
        functools.partial(fold_kernel, full, rest),
        in_specs=[vmem] * 6,
        out_specs=vmem,
        out_shape=jax.ShapeDtypeStruct((pairs[0][0].shape[1], 3 * (full + rest)), BF),
        compiler_params=pltpu.CompilerParams(vmem_limit_bytes=24 * 2**20),
        cost_estimate=SMALL_COST,
        name="fold_shared",
    )(*[item for pair in pairs for item in pair])


def join_kernel(cuts, places_ref, *refs):
    mine_refs, far_refs, behind_ref, out_refs = refs[:2], refs[2:4], refs[4], refs[5:]
    n_blocks = mine_refs[0].shape[1] // LANES
    y = places_ref[2 * n_blocks]
    for k, pieces in enumerate(cuts):
        at = 0
        for low, count in pieces:
            for block in range(2 * n_blocks):
                half, column = block // n_blocks, block % n_blocks * LANES
                for source, side in ((mine_refs[half], y), (far_refs[half], 1 - y)):
                    target = pl.ds(pl.multiple_of((2 * places_ref[block] + side) * LANES, LANES), LANES)
                    out_refs[k][at : at + count, target] = source[low : low + count, column : column + LANES]
            at += count
        rest = out_refs[k].shape[0] - at
        out_refs[k][at:, :] = behind_ref[...] if k == 0 else jnp.zeros((rest, out_refs[k].shape[1]), BF)


def join_shared(places, mine, far, behind, cuts):
    rows = sum(count for _, count in cuts[0]) + behind.shape[0]
    vmem = pl.BlockSpec(memory_space=pltpu.VMEM)
    return pl.pallas_call(
        functools.partial(join_kernel, cuts),
        in_specs=[pl.BlockSpec(memory_space=pltpu.SMEM)] + [vmem] * 5,
        out_specs=[vmem] * 3,
        out_shape=[jax.ShapeDtypeStruct((rows, 4 * mine[0].shape[1]), BF)] * 3,
        compiler_params=pltpu.CompilerParams(vmem_limit_bytes=24 * 2**20),
        cost_estimate=SMALL_COST,
        name="join_shared",
    )(places, *mine, *far, behind)


def weights_kernel(n_sets, split, y_ref, *refs):
    sources, lhs_refs = refs[:12], refs[12 : 12 + 4 * n_sets]
    out_refs, (held, sems) = refs[12 + 4 * n_sets : -2], refs[-2:]
    rows, width = held.shape
    own = rows // 16

    @pl.when(pl.program_id(0) == 0)
    def _():
        copies = []
        for k in range(12):
            at, count = (k // 3 * 4 + k % 3) * own, 2 * own if k % 3 == 2 else own
            copies.append(
                pltpu.make_async_copy(sources[k].at[:, pl.ds(0, width)], held.at[pl.ds(at, count), :], sems.at[k]))
        for copy in copies:
            copy.start()
        for copy in copies:
            copy.wait()

    for k in range(n_sets):
        lhs = jnp.concatenate([ref[...] for ref in lhs_refs[4 * k : 4 * k + 4]], axis=0)
        total = dot_tn(lhs, held[...])
        if not split:
            for tile in range(2):
                at = 0
                for out_ref in out_refs:
                    low, high = max(at, tile * GRAD_TILE), min(at + out_ref.shape[0], (tile + 1) * GRAD_TILE)
                    if low < high:

                        @pl.when(pl.program_id(0) == tile)
                        def _(out_ref=out_ref, low=low, high=high, at=at, tile=tile):
                            out_ref[low - at : high - at, :] = total[
                                low - tile * GRAD_TILE : high - tile * GRAD_TILE, :].astype(BF)

                    at += out_ref.shape[0]
            continue
        for block in range(width // LANES // 2):
            even = total[:, 2 * block * LANES : (2 * block + 1) * LANES]
            odd = total[:, (2 * block + 1) * LANES : (2 * block + 2) * LANES]
            columns = slice(block * LANES, (block + 1) * LANES)
            out_refs[2 * k][:, columns] = jnp.where(y_ref[0] == 0, even, odd).astype(BF)
            out_refs[2 * k + 1][:, columns] = jnp.where(y_ref[0] == 0, odd, even).astype(BF)


def weight_grads(y, sources, lhs_sets, width, parts=None):
    rows, units = lhs_sets[0][0].shape
    n_sets = len(lhs_sets)
    n_tiles = units // GRAD_TILE
    split = parts is None
    if split:
        shapes = [(GRAD_TILE, width // 2)] * (2 * n_sets)
    else:
        shapes = [(count, width) for count in parts]
    return pl.pallas_call(
        functools.partial(weights_kernel, n_sets, split),
        grid=(n_tiles,),
        in_specs=[pl.BlockSpec(memory_space=pltpu.SMEM)]
        + [pl.BlockSpec(memory_space=pl.ANY)] * 12
        + [pl.BlockSpec((rows, GRAD_TILE), lambda i: (0, i))] * (4 * n_sets),
        out_specs=[whole(shape) for shape in shapes],
        scratch_shapes=[pltpu.VMEM((4 * rows, width), BF), pltpu.SemaphoreType.DMA((12,))],
        out_shape=[jax.ShapeDtypeStruct(shape, BF) for shape in shapes],
        compiler_params=pltpu.CompilerParams(vmem_limit_bytes=56 * 2**20),
        cost_estimate=pl.CostEstimate(
            flops=4 * 10**9 * n_sets * n_tiles, bytes_accessed=2 * 10**7, transcendentals=0),
        name="weight_grads",
    )(y, *sources, *[item for lhs in lhs_sets for item in lhs])


def feed_plain(normed, grad, named, expert, wg, wu, wd, router, experts, shared):
    logits = contract("td,cd->tc", normed, router)
    router_probs = jax.nn.softmax(logits[:, :experts], axis=-1)
    shared_scale = jax.nn.sigmoid(logits[:, experts : experts + 1])
    hot = (jnp.arange(experts) == expert).astype(F32)
    gate_here = jnp.sum(router_probs * hot, axis=1, keepdims=True) * named[:, None]
    is_shared = (jnp.arange(wg.shape[0]) < shared)[None]
    row_scale = jnp.where(is_shared, shared_scale, gate_here)
    act, slope = silu_parts(contract("td,cd->tc", normed, wg))
    up = contract("td,cd->tc", normed, wu)
    hidden = act * up
    hidden_scaled = (hidden * row_scale).astype(BF)
    grad_hidden = contract("td,fd->tf", grad, wd)
    dots = hidden * grad_hidden
    dot_shared = jnp.sum(jnp.where(is_shared, dots, 0.0), axis=1, keepdims=True)
    dot_expert = jnp.sum(jnp.where(is_shared, 0.0, dots), axis=1, keepdims=True) * named[:, None]
    grad_pre = grad_hidden * row_scale
    grad_gate = (grad_pre * up * slope).astype(BF)
    grad_up = (grad_pre * act).astype(BF)
    grad_normed = contract("tc,cd->td", grad_gate, wg) + contract("tc,cd->td", grad_up, wu)
    extra = jnp.concatenate([dot_expert * hot, dot_shared], axis=1)
    extra = jnp.pad(extra, ((0, 0), (0, LANES - extra.shape[1])))
    out = contract("tf,fd->td", hidden_scaled, wd)
    return (
        jnp.concatenate([grad_normed, extra], axis=1),
        out,
        contract("tc,td->cd", grad_gate, normed),
        contract("tc,td->cd", grad_up, normed),
        contract("tf,td->fd", hidden_scaled, grad),
    )


def ring_perm(move):
    pairs = []
    for me in range(32):
        z, x, y, c = me // 8, me // 4 % 2, me // 2 % 2, me % 2
        z, x, y, c = move(z, x, y, c)
        pairs.append((me, ((z * 2 + x) * 2 + y) * 2 + c))
    return pairs


MOVES = {
    "core": lambda z, x, y, c: (z, x, y, 1 - c),
    "y": lambda z, x, y, c: (z, x, 1 - y, c),
    "yc": lambda z, x, y, c: (z, x, 1 - y, 1 - c),
    "x": lambda z, x, y, c: (z, 1 - x, y, c),
    "z1": lambda z, x, y, c: ((z + 1) % 4, x, y, c),
    "z2": lambda z, x, y, c: ((z + 2) % 4, x, y, c),
    "z3": lambda z, x, y, c: ((z + 3) % 4, x, y, c),
}


def send(value, link):
    return lax.ppermute(value, ALL, ring_perm(MOVES[link]))


def sync(*values):
    return lax.optimization_barrier(values)


def pick(value, place, axis=0):
    return lax.dynamic_index_in_dim(value, place, axis, keepdims=False)


def put(value, block, place, axis=0):
    return lax.dynamic_update_index_in_dim(value, block, place, axis)


def in_order(mine, other, bit, axis):
    return jnp.where(bit == 0, jnp.stack([mine, other], axis=axis), jnp.stack([other, mine], axis=axis))


def on_device_ring(
    hidden_in, seg_ids, routes, out_grad, norm_gain1, w_query, w_key, w_value, b_qkv, w_out,
    norm_gain2, w_router, shared_gate, sh_gate, sh_up, sh_down, ex_gate, ex_up, ex_down,
):
    micro, tok, width = hidden_in.shape
    experts = w_router.shape[1]
    rows_w = w_query.shape[0]
    top_count = routes.shape[2]
    my_exp, my_fsdp = lax.axis_index("expert"), lax.axis_index("fsdp")
    z, x, y, c = my_exp // 2, lax.rem(my_exp, 2), my_fsdp // 2, lax.rem(my_fsdp, 2)
    n_exp, n_fsdp, n_all = 8, 4, 32
    heads_dev = HEADS // n_fsdp
    wide = heads_dev * HEAD
    seq, own = tok * n_fsdp, micro * tok
    ex_cols = ex_gate.shape[2]
    sh_cols = SHARED_FF // 16
    full_cols = sh_cols // LANES * LANES
    rest_cols = sh_cols - full_cols
    unit_cols = 3 * sh_cols

    def slot(step, other):
        return lax.rem(z + 4 - step, 4) * 2 + (1 - x if other else x)

    def by_fsdp(three):
        rows = three.shape[0]
        split = three.reshape(rows, 3, 2, 2, heads_dev // 2, 2, HEAD)
        return split.transpose(5, 2, 0, 3, 1, 4, 6).reshape(n_fsdp, rows, 3 * wide)

    def from_fsdp(blocks):
        rows = blocks.shape[1]
        split = blocks.reshape(2, 2, rows, 2, 3, heads_dev // 2, HEAD)
        return split.transpose(4, 2, 1, 3, 5, 0, 6).reshape(3, rows, width)

    def swap_core(blocks):
        mine, give = pick(blocks, c, 2), pick(blocks, 1 - c, 2)
        return in_order(mine, send(give, "core"), c, 2)

    def swap_z(blocks, k):
        return send(pick(blocks, lax.rem(z + k, 4)), f"z{k}")

    small = jnp.concatenate(
        [w_router.T, shared_gate[None], norm_gain1[None], norm_gain2[None], b_qkv, seg_ids.astype(BF)], axis=0)
    n_small = experts + 6
    small = [small.reshape(1, (n_small + micro) * rows_w)]
    for _ in range(3):
        small.append(send(small[-1], "z1"))
    small = jnp.concatenate(small)
    qkv = by_fsdp(jnp.stack([w_query, w_key, w_value], axis=1))
    arrived = [send(pick(qkv, lax.bitwise_xor(my_fsdp, k)), link) for k, link in ((1, "core"), (2, "y"), (3, "yc"))]
    grad_own = out_grad.reshape(own, width)
    names = jnp.pad(routes.reshape(own, top_count).astype(BF), ((0, 0), (0, LANES - top_count)))
    g_own = [jnp.concatenate([grad_own, names], axis=1)]
    g_pair = []
    routed_mine = jnp.concatenate([ex_gate[0].T, ex_up[0].T, ex_down[0]], axis=0)
    small, arrived, g_own[0], routed_mine = sync(small, arrived, g_own[0], routed_mine)
    for k in range(3):
        qkv = put(qkv, arrived[k], lax.bitwise_xor(my_fsdp, k + 1))
    block = jnp.concatenate([w_out[:, k * wide : (k + 1) * wide] for k in range(n_fsdp)], axis=0)
    block = jnp.concatenate([qkv.reshape(n_fsdp * rows_w, 3 * wide), block], axis=1)
    following = send(block, "z1")
    small = jnp.concatenate([small, send(small, "x")])
    at_pair = send(sync(block, small)[0], "x")
    small = jnp.concatenate([small, send(small, "y")])
    got = send(sync(routed_mine[:264], small)[0], "y")
    small = jnp.concatenate([small, send(small, "core")])
    block, following, at_pair, small, got, routed_mine, sh_gate, sh_up, sh_down, hidden_in = sync(
        block, following, at_pair, small, got, routed_mine, sh_gate, sh_up, sh_down, hidden_in)
    a_blocks = [routed_mine[k * 264 : (k + 1) * 264] for k in range(4)]
    got_blocks = [got]
    weights = jnp.zeros((n_exp,) + block.shape, BF)

    def ring_put(weights, step, mine, other):
        return put(put(weights, mine, slot(step, 0)), other, slot(step, 1))

    first_pair, mine = at_pair, following
    at_pair, following = send(mine, "x"), send(mine, "z1")
    places = jnp.stack(
        [slot(step, other) * 4 + lax.bitwise_xor(my_fsdp, k) for k in (0, 2, 1, 3) for other in range(2) for step in range(4)])
    choice = (jnp.arange(n_all)[:, None] == places[None]).astype(BF)
    small = dot_nn(choice, small).astype(BF).reshape(n_all, n_small + micro, rows_w)
    small = small.transpose(1, 0, 2).reshape(n_small + micro, width)
    router_rows = small[: experts + 1]
    gain_one = small[experts + 1].astype(F32)
    gain_two = small[experts + 2].astype(F32)
    bias = pick(by_fsdp(small[experts + 3 : n_small].astype(F32)[None]), my_fsdp)
    seg_seq = lax.dynamic_slice_in_dim(small[n_small:], my_exp * seq, seq, 1).reshape(micro, n_fsdp, tok)
    hidden = hidden_in.reshape(own, width).astype(F32)
    scaled_one, inverse_one = normalize(hidden)
    normed_one = (scaled_one * gain_one).astype(BF).reshape(micro, tok, width)
    seq_far, seq_near = send(normed_one, "y"), send(normed_one, "core")

    (block, mine, following, at_pair, seq_far, seq_near, normed_one, a_blocks, bias, router_rows, seg_seq,
     sh_gate, sh_up, sh_down) = sync(
        block, mine, following, at_pair, seq_far, seq_near, normed_one, a_blocks, bias, router_rows, seg_seq,
        sh_gate, sh_up, sh_down)

    previous, previous_pair, mine = mine, at_pair, following
    at_pair, following = send(mine, "x"), send(mine, "z1")
    shared_w = pack_shared(sh_gate, sh_up, sh_down, 16, full_cols, rest_cols)
    shared_w = swap_core(shared_w.reshape(4, 2, 2, rows_w, unit_cols))
    weights = ring_put(ring_put(weights, 0, block, first_pair), 1, previous, previous_pair)
    seq_last = send(seq_far, "core")
    got = send(a_blocks[1], "y")
    mine, following, at_pair, got, a_blocks, shared_w, seq_last, weights = sync(
        mine, following, at_pair, got, a_blocks, shared_w, seq_last, weights)
    got_blocks.append(got)

    weights = ring_put(weights, 2, mine, at_pair)
    at_pair = send(following, "x")
    got = send(a_blocks[2], "y")
    shared_z = {1: swap_z(shared_w, 1), 3: swap_z(shared_w, 3)}
    order = lax.bitwise_xor(my_fsdp, jnp.arange(n_fsdp))
    places = (order[:, None] * tok + jnp.arange(tok)[None]).reshape(seq)
    seg_seq = jnp.take(seg_seq, order, axis=1).reshape(micro, seq).astype(jnp.int32)
    normed_seq = jnp.concatenate([normed_one, seq_near, seq_far, seq_last], axis=1).reshape(micro * seq, width)
    cosine, sine = angle_tables(places)
    tables = (cosine, sine, places[:, None], seg_seq.reshape(micro * seq, 1), places[None], seg_seq)
    following, at_pair, got, shared_z, shared_w, a_blocks, weights, tables, normed_seq, g_own[0] = sync(
        following, at_pair, got, shared_z, shared_w, a_blocks, weights, tables, normed_seq, g_own[0])
    got_blocks.append(got)
    weights = ring_put(weights, 3, following, at_pair)
    wqkv = weights.reshape(width, 4 * wide)

    def turned(value):
        value = value.reshape(micro, 2, 2, tok, -1)
        return jnp.concatenate([value[:, :, 1:], value[:, :, :1]], axis=2).reshape(micro * seq, -1)

    core_place = c.reshape(1)
    got = send(a_blocks[3], "y")
    far_w = pick(shared_w, lax.rem(z + 2, 4))
    shared_z[2] = [send(far_w[0], "z2")]
    shared_z[0] = pick(shared_w, z)
    shared_x = {}

    def swap_x(steps):
        arrived = send(jnp.stack([pick(shared_z[step], 1 - x) for step in steps]), "x")
        return arrived, [pick(shared_z[step], x) for step in steps]

    def as_columns(parts):
        blocks = [
            in_order(mine, arrived[k], x, 0) for arrived, all_mine in parts for k, mine in enumerate(all_mine)
        ]
        return jnp.stack(blocks).reshape(-1, unit_cols).T

    shared_x = [swap_x((0, 1))]
    g_pair.append(send(g_own[0], "x"))
    qkv_seq, keep, give = attend(normed_seq, wqkv, bias, tables, seq, core=core_place)
    wo = sync(weights, give)[0]
    wo = [wo[:, k * rows_w : (k + 1) * rows_w, 3 * wide :].reshape(n_exp * rows_w, wide) for k in range(n_fsdp)]
    wo = jnp.concatenate(wo, axis=1)
    got, shared_z, shared_x, qkv_seq, keep, give, wqkv, wo, far_w, g_pair = sync(
        got, shared_z, shared_x, qkv_seq, keep, give, wqkv, wo, far_w, g_pair)
    got_blocks.append(got)
    shared_w = [as_columns(shared_x)]
    arrived = turned(send(give, "core"))
    shared_z, shared_w, arrived, keep, wo, far_w, g_own, g_pair = sync(
        shared_z, shared_w, arrived, keep, wo, far_w, g_own, g_pair)
    shared_z[2].append(send(far_w[1], "z2"))
    arrived_w = [send(shared_w[0], "y")]
    shared_x = [swap_x((3,))]
    attended = jnp.where(c == 0, jnp.concatenate([keep, arrived], axis=1), jnp.concatenate([arrived, keep], axis=1))
    attn_part = contract("tc,cd->td", attended, wo).reshape(micro, 2, 2, tok, width)
    attn_part = attn_part[:, :, 0] + send(attn_part[:, :, 1].astype(BF), "core").astype(F32)
    near, last = attn_part[:, 0], attn_part[:, 1].astype(BF)
    last, near, shared_z, shared_x, shared_w, arrived_w, g_own, g_pair = sync(
        last, near, shared_z, shared_x, shared_w, arrived_w, g_own, g_pair)
    shared_z[2] = jnp.stack(shared_z[2])

    last = send(last, "y")
    shared_x.append(swap_x((2,)))
    g_own.append(send(g_own[0], "z1"))

    def blocks_of(mine, other):
        return [mine, other, send(jnp.concatenate([mine, other]), "core")]

    g_four = [blocks_of(g_own[0], g_pair[0])]
    after_attn = hidden + near.reshape(own, width) + last.astype(F32).reshape(own, width)
    scaled_two, inverse_two = normalize(after_attn)
    normed_two = (scaled_two * gain_two).astype(BF)
    x_own, x_pair = [normed_two], []
    shared_w.append(as_columns(shared_x))
    shared_w, arrived_w, x_own, after_attn, scaled_two, g_own, g_pair, got_blocks, g_four = sync(
        shared_w, arrived_w, x_own, after_attn, scaled_two, g_own, g_pair, got_blocks, g_four)

    arrived_w.append(send(shared_w[1], "y"))
    x_pair.append(send(x_own[0], "x"))
    g_pair.append(send(g_own[1], "x"))
    x_own.append(send(x_own[0], "z1"))
    g_own.append(send(g_own[1], "z1"))
    routed_other = jnp.concatenate(got_blocks, axis=0)
    pad = jnp.zeros((2 * GRAD_TILE - 2 * ex_cols, width), BF)
    routed_w = [
        jnp.concatenate(
            [routed_mine[k * ex_cols : (k + 1) * ex_cols], routed_other[k * ex_cols : (k + 1) * ex_cols], pad], axis=0)
        for k in range(3)
    ]

    shared_w, arrived_w, x_own, g_own, x_pair, g_pair, routed_w = sync(
        shared_w, arrived_w, x_own, g_own, x_pair, g_pair, routed_w)
    x_pair.append(send(x_own[1], "x"))
    x_own.append(send(x_own[1], "z1"))
    g_four.append(blocks_of(g_own[1], g_pair[1]))
    x_four = [blocks_of(x_own[0], x_pair[0])]
    behind = jnp.pad(router_rows, ((0, GRAD_TILE - sh_cols - experts - 1), (0, 0)))
    rest_at = 3 * full_cols
    cuts = [
        [(k * full_cols, full_cols), (rest_at + k * rest_cols, rest_cols)] for k in range(3)
    ]
    y_place = y.reshape(1)
    places = jnp.stack([lax.rem(z + 4 - step, 4) * 2 + side for step in (0, 1, 3, 2) for side in range(2)] + [y])
    shared_w = join_shared(places, shared_w, arrived_w, behind, cuts)

    expert = my_exp.reshape(1)
    fed, near_sums, sums, out_near, out_sums = [], [], [], [], []

    def core_sums(found):
        arrived = send(found[2], "core")
        return [found[0].astype(F32) + arrived[:own].astype(F32), found[1].astype(F32) + arrived[own:].astype(F32)]

    def pair_sums(parts):
        return parts[0] + send(parts[1].astype(BF), "x").astype(F32)

    for step in range(4):
        shared_w, routed_w, x_four, g_four, x_own, g_own, x_pair, g_pair, near_sums, sums, fed, out_near, out_sums = sync(
            shared_w, routed_w, x_four, g_four, x_own, g_own, x_pair, g_pair, near_sums, sums, fed, out_near, out_sums)
        if step == 0:
            x_pair.append(send(x_own[2], "x"))
            x_own.append(send(x_own[2], "z1"))
            g_own.append(send(g_own[2], "z1"))
            g_pair.append(send(g_own[2], "x"))
            x_four.append(blocks_of(x_own[1], x_pair[1]))
        if step == 1:
            x_pair.append(send(x_own[3], "x"))
            g_pair.append(send(g_own[3], "x"))
            x_four.append(blocks_of(x_own[2], x_pair[2]))
            g_four.append(blocks_of(g_own[2], g_pair[2]))
        if step == 2:
            x_four.append(blocks_of(x_own[3], x_pair[3]))
            g_four.append(blocks_of(g_own[3], g_pair[3]))
        if step >= 1:
            near_sums.append(core_sums(fed[step - 1][2]))
        if step >= 2:
            sums.append(pair_sums(near_sums[step - 2]))
            out_near.append(core_sums(fed[step - 2][3]))
        if step == 3:
            out_sums.append(pair_sums(out_near[0]))
        fed.append(feed(expert, x_four[step], g_four[step], shared_w, routed_w, experts, sh_cols))
    near_sums, sums, fed, x_four, g_four, out_near, out_sums, normed_two = sync(
        near_sums, sums, fed, x_four, g_four, out_near, out_sums, normed_two)

    x_blocks = [item for four_of in x_four for item in four_of]
    g_blocks = [item for four_of in g_four for item in four_of]
    shared_sets = [[fed[step][0][item] for step in range(4)] for item in range(3)]
    routed_sets = [[fed[step][1][item] for step in range(4)] for item in range(3)]
    flying = send(sums[1].astype(BF), "z1")
    sums.append(pair_sums(near_sums[2]))
    near_sums.append(core_sums(fed[3][2]))
    out_near.append(core_sums(fed[2][3]))
    sg_mine, sg_give, su_mine, su_give = weight_grads(y_place, x_blocks, [shared_sets[1], shared_sets[2]], width)
    (sums, near_sums, flying, sg_mine, sg_give, su_mine, su_give, x_blocks, g_blocks, shared_sets, routed_sets,
     out_near, fed) = sync(sums, near_sums, flying, sg_mine, sg_give, su_mine, su_give, x_blocks, g_blocks,
                           shared_sets, routed_sets, out_near, fed)
    sums.append(pair_sums(near_sums[3]))
    flying = send((sums[2] + flying.astype(F32)).astype(BF), "z1")
    sg_got = send(sg_give, "y")
    out_near.append(core_sums(fed[3][3]))
    sd_mine, sd_give = weight_grads(y_place, g_blocks, [shared_sets[0]], width)
    sums, flying, sg_got, su_give, sd_mine, sd_give, x_blocks, g_blocks, routed_sets, out_near, out_sums = sync(
        sums, flying, sg_got, su_give, sd_mine, sd_give, x_blocks, g_blocks, routed_sets, out_near, out_sums)
    flying = send((sums[3] + flying.astype(F32)).astype(BF), "z1")
    su_got = send(su_give, "y")
    out_sums.append(pair_sums(out_near[1]))
    e_parts = (ex_cols, ex_cols // 2, ex_cols // 2)
    ed_grad = weight_grads(y_place, g_blocks, [routed_sets[0]], width, e_parts)
    grad_sum, out_near, out_sums, su_got, sd_give, ed_grad, x_blocks, routed_sets = sync(
        sums[0] + flying.astype(F32), out_near, out_sums, su_got, sd_give, ed_grad, x_blocks, routed_sets)

    own_logits = contract("td,cd->tc", normed_two, router_rows)
    own_probs = jax.nn.softmax(own_logits[:, :experts], axis=-1)
    own_scale = jax.nn.sigmoid(own_logits[:, experts])
    grad_probs = grad_sum[:, width : width + experts]
    grad_router = own_probs * (grad_probs - jnp.sum(own_probs * grad_probs, axis=-1, keepdims=True))
    grad_gate = grad_sum[:, width + experts] * own_scale * (1.0 - own_scale)
    grad_logits = jnp.concatenate([grad_router, grad_gate[:, None]], axis=1).astype(BF)
    grad_normed_two = grad_sum[:, :width] + contract("tc,cd->td", grad_logits, router_rows)
    router_part = contract("tc,td->cd", grad_logits, normed_two)
    grad_after = grad_own.astype(F32) + norm_back(grad_normed_two, scaled_two, inverse_two, gain_two)
    gain_two_part = jnp.sum(grad_normed_two * scaled_two, axis=0)
    low = grad_after.astype(BF).reshape(micro, tok, width)
    sd_got = send(sd_give, "y")
    out_sums.append(pair_sums(out_near[2]))
    flying_out = send(out_sums[1].astype(BF), "z1")
    low, grad_after, out_sums, out_near, sd_got, flying_out, gain_two_part, router_part, x_blocks, routed_sets = sync(
        low, grad_after, out_sums, out_near, sd_got, flying_out, gain_two_part, router_part, x_blocks, routed_sets)
    far, near = send(low, "y"), send(low, "core")
    out_sums.append(pair_sums(out_near[3]))
    flying_out = send((out_sums[2] + flying_out.astype(F32)).astype(BF), "z1")
    shared_grads = fold_shared([(sg_mine, sg_got), (su_mine, su_got), (sd_mine, sd_got)], full_cols, rest_cols)
    shared_grads = shared_grads.reshape(4, 2, 2, rows_w, unit_cols)
    far, near, low, out_sums, flying_out, shared_grads, ed_grad, x_blocks, routed_sets = sync(
        far, near, low, out_sums, flying_out, shared_grads, ed_grad, x_blocks, routed_sets)

    def panel_sum(panel, gives, step):
        return [pick(panel, slot(step, 0)), send(gives[step], "x")]

    def two(parts):
        return parts[0].astype(F32) + parts[1].astype(F32)

    shared_grads = swap_core(shared_grads)
    flying_out = send((out_sums[3] + flying_out.astype(F32)).astype(BF), "z1")
    grad_attn = jnp.concatenate([low, near, far, send(far, "core")], axis=1).reshape(micro * seq, width)
    grad_attended = contract("td,cd->tc", grad_attn, wo).astype(BF)
    half = wide // 2
    keep = lax.dynamic_slice_in_dim(grad_attended, c * half, half, 1)
    give = lax.dynamic_slice_in_dim(grad_attended, (1 - c) * half, half, 1)
    arrived = turned(send(give, "core"))
    wo_part = contract("tc,td->cd", attended, grad_attn).astype(BF).reshape(n_exp, rows_w, width)
    wo_gives = [pick(wo_part, slot(step, 1)) for step in range(4)]
    shared_far = pick(shared_grads, lax.rem(z + 2, 4))
    shared_grads, shared_far, keep, arrived, flying_out, wo_part, wo_gives, ed_grad, x_blocks, routed_sets = sync(
        shared_grads, shared_far, keep, arrived, flying_out, wo_part, wo_gives, ed_grad, x_blocks, routed_sets)
    hidden_out = (after_attn + out_sums[0] + flying_out.astype(F32)).astype(BF)
    e_got = [send(ed_grad[1], "y")]
    shared_z = {2: send(shared_far, "z2")}
    def wo_pair(first, second):
        arrived = send(jnp.stack([wo_gives[first], wo_gives[second]]), "x")
        for k, step in enumerate((first, second)):
            wo_sums[step] = [pick(wo_part, slot(step, 0)), arrived[k]]

    wo_sums = {}
    wo_pair(1, 2)
    behind_rows = 8
    panel_shape = (n_exp, n_fsdp * rows_w + behind_rows, 3 * wide)
    grad_lin, grad_normed_one, gain_one_part, panel = attend(
        normed_seq, wqkv, bias, tables, seq, (keep, arrived, qkv_seq), core_place, panel_shape)
    shared_far = {k: pick(shared_grads, lax.rem(z + k, 4)) for k in (1, 3)}
    shared_z[0] = pick(shared_grads, z)
    give_x = pick(shared_z[0], 1 - x)
    (grad_lin, grad_normed_one, gain_one_part, panel, hidden_out, e_got, shared_z, shared_far, give_x, wo_part, wo_gives,
     wo_sums, ed_grad, x_blocks, routed_sets) = sync(
        grad_lin, grad_normed_one, gain_one_part, panel, hidden_out, e_got, shared_z, shared_far, give_x, wo_part, wo_gives,
        wo_sums, ed_grad, x_blocks, routed_sets)
    parts = grad_normed_one.reshape(micro, 2, 2, tok, width)
    parts = parts[:, :, 0] + send(parts[:, :, 1].astype(BF), "core").astype(F32)
    near, last = parts[:, 0], parts[:, 1].astype(BF)
    e_got.append(send(ed_grad[2], "y"))
    rest = ex_cols // 16 * 5 // 16 * 16
    g_parts, u_parts = (ex_cols, ex_cols - rest, rest), (ex_cols, rest, ex_cols - rest)
    eg_grad = weight_grads(y_place, x_blocks, [routed_sets[1]], width, g_parts)
    for k in (1, 3):
        shared_z[k] = send(shared_far[k], f"z{k}")
    wo_pair(3, 0)
    gain_one_part = gain_one_part[0] / gain_one
    bias_place = put(jnp.zeros((n_fsdp, 1, 3 * wide), F32), jnp.sum(grad_lin.astype(F32), axis=0)[None], my_fsdp)
    bias_place = from_fsdp(bias_place)[:, 0]
    small_part = jnp.concatenate([router_part, gain_one_part[None], gain_two_part[None], bias_place], axis=0)
    small_part = small_part.astype(BF).reshape(n_small, n_exp, n_fsdp, rows_w).transpose(1, 2, 0, 3)
    small_part = small_part.reshape(n_exp, n_fsdp * n_small * rows_w)
    small_part = jnp.pad(small_part, ((0, 0), (0, behind_rows * 3 * wide - small_part.shape[1])))
    panel = lax.dynamic_update_slice_in_dim(
        panel, small_part.reshape(n_exp, behind_rows, 3 * wide), n_fsdp * rows_w, 1)
    gives = [pick(panel, slot(step, 1)) for step in range(4)]
    (gives, panel, last, near, e_got, shared_z, give_x, wo_sums, wo_part, wo_gives, eg_grad, x_blocks,
     routed_sets) = sync(gives, panel, last, near, e_got, shared_z, give_x, wo_sums, wo_part, wo_gives, eg_grad,
                         x_blocks, routed_sets)

    far = send(last, "y")
    eu_grad = weight_grads(y_place, x_blocks, [routed_sets[2]], width, u_parts)
    e_grads = (eg_grad, eu_grad, ed_grad)
    shared_x, sums = [], {}

    for turn, step in enumerate((1, 2, 3, 0)):
        sums[step] = panel_sum(panel, gives, step)
        shared_x.append(send(give_x, "x"))
        if turn < 3:
            give_x = pick(shared_z[turn + 1], 1 - x)
        if turn:
            e_got.append(send(e_gives[turn - 1], "y"))
        if turn == 0:
            flying_wo = send(two(wo_sums[1]).astype(BF), "z1")
            e_gives = [eg_grad[1], jnp.concatenate([eg_grad[2], eu_grad[1]]), eu_grad[2]]
            (far, near, sums, e_got, shared_x, give_x, shared_z, e_grads, e_gives, panel, gives, flying_wo,
             wo_sums) = sync(far, near, sums, e_got, shared_x, give_x, shared_z, e_grads, e_gives, panel, gives,
                             flying_wo, wo_sums)
            continue
        if turn == 1:
            routed_grads = {2: ed_grad[0].astype(F32) + jnp.concatenate(e_got[:2]).astype(F32)}
            flying = send(two(sums[1]).astype(BF), "z1")
            grad_normed_one = (near + far.astype(F32)).reshape(own, width)
            in_grad = grad_after + norm_back(grad_normed_one, scaled_one, inverse_one, gain_one)
        else:
            flying = send((two(sums[turn]) + flying.astype(F32)).astype(BF), "z1")
        if turn == 3:
            rest = eg_grad[2].shape[0]
            got_g, got_u = e_got[3][:rest], e_got[3][rest:]
            routed_grads[0] = (eg_grad[0].astype(F32) + jnp.concatenate([e_got[2], got_g]).astype(F32)).T
        if turn < 3:
            flying_wo = send((two(wo_sums[turn + 1]) + flying_wo.astype(F32)).astype(BF), "z1")
            (sums, e_got, shared_x, give_x, shared_z, flying, e_grads, e_gives, panel, gives, flying_wo, in_grad,
             routed_grads, wo_part, wo_gives) = sync(
                sums, e_got, shared_x, give_x, shared_z, flying, e_grads, e_gives, panel, gives, flying_wo, in_grad,
                routed_grads, wo_part, wo_gives)
        else:
            out_own = two(wo_sums[0]) + flying_wo.astype(F32)
            flying, sums, out_own, e_got, shared_x = sync(flying, sums, out_own, e_got, shared_x)
    shared_blocks = jnp.stack([in_order(pick(shared_z[k], x), shared_x[k], x, 0) for k in range(4)])
    places = (lax.rem(z + 4 - jnp.arange(4), 4)[:, None] * 4 + jnp.arange(4)[None]).reshape(16)
    shared_own = unpack_shared(
        shared_blocks.reshape(16, rows_w, unit_cols), places.astype(jnp.int32), full_cols, rest_cols)
    routed_grads[1] = (eu_grad[0].astype(F32) + jnp.concatenate([got_u, e_got[4]]).astype(F32)).T
    total = (two(sums[0]) + flying.astype(F32)).astype(BF)

    count = n_fsdp * rows_w
    small_sum = total[count:].reshape(-1)[: n_fsdp * n_small * rows_w].reshape(n_fsdp, n_small * rows_w)
    small_sum = jnp.pad(small_sum, ((0, 0), (0, 3 * wide - n_small * rows_w)))
    blocks = jnp.concatenate([total[:count, : 3 * wide].reshape(n_fsdp, rows_w, 3 * wide), small_sum[:, None]], axis=1)
    qkv_own = blocks
    for k, link in ((1, "core"), (2, "y"), (3, "yc")):
        place = lax.bitwise_xor(my_fsdp, k)
        qkv_own = put(qkv_own, send(pick(blocks, place), link), place)
    small_own = jnp.sum(qkv_own[:, rows_w, : n_small * rows_w].astype(F32), axis=0).reshape(n_small, rows_w)
    qkv_own = from_fsdp(qkv_own[:, :rows_w]).astype(F32)
    return (
        hidden_out.reshape(micro, tok, width),
        in_grad.reshape(micro, tok, width),
        small_own[experts + 1],
        qkv_own[0],
        qkv_own[1],
        qkv_own[2],
        small_own[experts + 3 :],
        out_own,
        small_own[experts + 2],
        small_own[:experts].T,
        small_own[experts],
        shared_own[0],
        shared_own[1],
        shared_own[2],
        routed_grads[0][None],
        routed_grads[1][None],
        routed_grads[2][None],
    )


def on_device_any(
    hidden_in, seg_ids, routes, out_grad, norm_gain1, w_query, w_key, w_value, b_qkv, w_out,
    norm_gain2, w_router, shared_gate, sh_gate, sh_up, sh_down, ex_gate, ex_up, ex_down,
):
    links = Links()
    micro, tok, width = hidden_in.shape
    experts = w_router.shape[1]
    rows_w = w_query.shape[0]
    n_exp, n_fsdp, n_all = links.n_exp, links.n_fsdp, links.n_all
    my_exp, my_fsdp = links.my_exp, links.my_fsdp
    half_f, core_f = my_fsdp // 2, lax.rem(my_fsdp, 2)
    heads_dev = HEADS // n_fsdp
    wide = heads_dev * HEAD
    seq = tok * n_fsdp
    own = micro * tok
    sh_cols = SHARED_FF // n_all
    ex_cols = ex_gate.shape[2]

    def by_fsdp(three):
        rows = three.shape[0]
        split = three.reshape(rows, 3, 2, 2, heads_dev // 2, 2, HEAD)
        return split.transpose(5, 2, 0, 3, 1, 4, 6).reshape(n_fsdp, rows, 3 * wide)

    def from_fsdp(blocks):
        rows = blocks.shape[1]
        split = blocks.reshape(2, 2, rows, 2, 3, heads_dev // 2, HEAD)
        return split.transpose(4, 2, 1, 3, 5, 0, 6).reshape(3, rows, width)

    small = jnp.concatenate([w_router.T, shared_gate[None], norm_gain1[None], norm_gain2[None], b_qkv], axis=0)
    n_small = small.shape[0]
    small = lax.all_gather(small, ALL, axis=1, tiled=True)
    router_rows = small[: experts + 1]
    gain_one = small[experts + 1].astype(F32)
    gain_two = small[experts + 2].astype(F32)
    bias = by_fsdp(small[experts + 3 :].astype(F32)[None])
    bias = lax.dynamic_index_in_dim(bias, my_fsdp, 0, keepdims=False)

    x = hidden_in.reshape(own, width).astype(F32)
    scaled_one, inverse_one = normalize(x)
    normed_one = (scaled_one * gain_one).astype(BF)
    normed_seq = links.gather_seq(normed_one.reshape(micro, tok, width)).reshape(micro * seq, width)

    qkv = by_fsdp(jnp.stack([w_query, w_key, w_value], axis=1))
    qkv = links.swap_fsdp(qkv).reshape(n_fsdp * rows_w, 3 * wide)
    wqkv = links.gather_rows(qkv).reshape(width, 3 * wide)
    wo = lax.all_gather(w_out, ALL, axis=0, tiled=True).reshape(2, heads_dev, 2, HEAD, width)
    wo = lax.dynamic_index_in_dim(wo, core_f, 0, keepdims=False)
    wo = lax.dynamic_index_in_dim(wo, half_f, 1, keepdims=False).reshape(wide, width)

    tile_cols = sh_cols // LANES * LANES
    rest_cols = sh_cols - tile_cols

    def by_owner(weight):
        full = weight[:, : n_all * tile_cols].reshape(rows_w, n_all, tile_cols).transpose(1, 0, 2)
        rest = weight[:, n_all * tile_cols :].reshape(rows_w, n_all, rest_cols).transpose(1, 0, 2)
        return full, rest

    def from_owner(full, rest):
        return jnp.concatenate(
            [full.transpose(1, 0, 2).reshape(rows_w, -1), rest.transpose(1, 0, 2).reshape(rows_w, -1)], axis=1
        )

    pieces = [by_owner(weight) for weight in (sh_gate, sh_up, sh_down)]
    shared_w = jnp.concatenate([piece[0] for piece in pieces] + [piece[1] for piece in pieces], axis=2)
    shared_w = lax.all_to_all(shared_w, ALL, split_axis=0, concat_axis=0, tiled=True)
    shared_w = shared_w.reshape(width, 3 * sh_cols).T

    def three(rows):
        return [
            jnp.concatenate(
                [rows[k * tile_cols : (k + 1) * tile_cols],
                 rows[3 * tile_cols + k * rest_cols : 3 * tile_cols + (k + 1) * rest_cols]], axis=0)
            for k in range(3)
        ]

    shared_other = links.partner(shared_w, 2)
    routed_w = jnp.concatenate([ex_gate[0].T, ex_up[0].T, ex_down[0]], axis=0)
    halves = [[0, 2], [1, 3]]
    routed_w = lax.all_gather(routed_w, "fsdp", axis=0, axis_index_groups=halves)
    routed_w = [routed_w[:, k * ex_cols : (k + 1) * ex_cols].reshape(2 * ex_cols, width) for k in range(3)]
    units = 2 * (sh_cols + ex_cols)
    pad_rows = -(units + experts + 1) % LANES
    pad = jnp.zeros((pad_rows + experts + 1, width), BF)
    behind = (jnp.pad(router_rows, ((0, pad_rows), (0, 0))), pad, pad)
    wg, wu, wd = [
        jnp.concatenate(pieces, axis=0)
        for pieces in zip(three(shared_w), three(shared_other), routed_w, behind)
    ]
    shared_units = 2 * sh_cols

    grad_own = out_grad.reshape(own, width)
    names = jnp.pad(routes.reshape(own, -1).astype(BF), ((0, 0), (0, LANES - routes.shape[2])))
    grad_near = lax.all_gather(jnp.concatenate([grad_own, names], axis=1), "expert", axis=0)
    grad_far = links.partner(grad_near, 1)

    order = lax.bitwise_xor(my_fsdp, jnp.arange(n_fsdp))
    places = (order[:, None] * tok + jnp.arange(tok)[None]).reshape(seq)
    seg_seq = links.gather_seq(seg_ids)
    cosine, sine = angle_tables(places)
    tables = (cosine, sine, places[:, None], seg_seq.reshape(micro * seq, 1), places[None], seg_seq)
    qkv_seq, attended = attend(normed_seq, wqkv, bias, tables, seq)
    attn_part = contract("tc,cd->td", attended, wo).reshape(micro, n_fsdp, tok, width)
    attn_sum = links.sum_four([attn_part[:, k] for k in range(4)]).reshape(own, width)
    after_attn = x + attn_sum
    scaled_two, inverse_two = normalize(after_attn)
    normed_two = (scaled_two * gain_two).astype(BF)

    near = lax.all_gather(normed_two, "expert", axis=0, tiled=True)
    normed_all = jnp.concatenate([near, links.partner(near, 1)], axis=0)
    grad_all = jnp.concatenate([grad_near, grad_far], axis=0).reshape(2 * n_exp * own, -1)
    named = jnp.sum((grad_all[:, width : width + routes.shape[2]] == my_exp.astype(BF)).astype(F32), axis=1)
    grad_part, out_part, wg_grad, wu_grad, wd_grad = feed_plain(
        normed_all, grad_all[:, :width], named, my_exp, wg, wu, wd, router_rows, experts, shared_units
    )

    def summed(part):
        count = n_exp * own
        total = part[:count] + links.partner(part[count:].astype(BF), 1).astype(F32)
        return links.sum_rows(total.reshape(n_exp, own, -1))

    grad_sum, out_sum = summed(grad_part), summed(out_part)
    wg_grad, wu_grad, wd_grad = [item.astype(BF) for item in (wg_grad, wu_grad, wd_grad)]
    hidden_out = (after_attn + out_sum).astype(BF)

    own_logits = contract("td,cd->tc", normed_two, router_rows)
    own_probs = jax.nn.softmax(own_logits[:, :experts], axis=-1)
    own_scale = jax.nn.sigmoid(own_logits[:, experts])
    grad_probs = grad_sum[:, width : width + experts]
    grad_router = own_probs * (grad_probs - jnp.sum(own_probs * grad_probs, axis=-1, keepdims=True))
    grad_gate = grad_sum[:, width + experts] * own_scale * (1.0 - own_scale)
    grad_logits = jnp.concatenate([grad_router, grad_gate[:, None]], axis=1).astype(BF)
    grad_normed_two = grad_sum[:, :width] + contract("tc,cd->td", grad_logits, router_rows)
    router_part = contract("tc,td->cd", grad_logits, normed_two)

    grad_after = grad_own.astype(F32) + norm_back(grad_normed_two, scaled_two, inverse_two, gain_two)
    gain_two_part = jnp.sum(grad_normed_two * scaled_two, axis=0)

    grad_attn = links.gather_seq(grad_after.astype(BF).reshape(micro, tok, width)).reshape(micro * seq, width)
    grad_lin, grad_normed_one, gain_one_part = attend(normed_seq, wqkv, bias, tables, seq, (grad_attn, wo, qkv_seq))
    gain_one_part = gain_one_part[0] / gain_one
    grad_normed_one = grad_normed_one.reshape(micro, n_fsdp, tok, width)
    grad_normed_one = links.sum_four([grad_normed_one[:, k] for k in range(4)]).reshape(own, width)
    in_grad = grad_after + norm_back(grad_normed_one, scaled_one, inverse_one, gain_one)
    out_grad_part = contract("tc,td->cd", attended, grad_attn).astype(BF)
    qkv_part = contract("td,tc->dc", normed_seq, grad_lin).astype(BF)
    bias_part = jnp.sum(grad_lin.astype(F32), axis=0)

    out_place = jnp.zeros((2, heads_dev, 2, HEAD, width), BF)
    out_place = lax.dynamic_update_slice(
        out_place, out_grad_part.reshape(1, heads_dev, 1, HEAD, width), (core_f, 0, half_f, 0, 0)
    )
    out_own = lax.psum_scatter(
        out_place.reshape(width, width), ALL, scatter_dimension=0, tiled=True
    ).astype(F32)
    bias_place = jnp.zeros((n_fsdp, 1, 3 * wide), F32)
    bias_place = from_fsdp(lax.dynamic_update_index_in_dim(bias_place, bias_part[None], my_fsdp, 0))[:, 0]
    small_part = jnp.concatenate([router_part, gain_one_part[None], gain_two_part[None], bias_place], axis=0)
    small_part = small_part.astype(BF).reshape(n_small, n_exp, n_fsdp, rows_w).transpose(1, 2, 0, 3)
    behind_rows = -(-n_fsdp * n_small * rows_w // (3 * wide) // 8) * 8
    room = behind_rows * 3 * wide
    small_part = small_part.reshape(n_exp, n_fsdp * n_small * rows_w)
    small_part = jnp.pad(small_part, ((0, 0), (0, room - small_part.shape[1])))
    qkv_part = jnp.concatenate(
        [qkv_part.reshape(n_exp, n_fsdp * rows_w, 3 * wide), small_part.reshape(n_exp, behind_rows, 3 * wide)], axis=1
    )
    qkv_sum = links.sum_rows(qkv_part).astype(BF)
    small_sum = qkv_sum[n_fsdp * rows_w :].reshape(-1)[: n_fsdp * n_small * rows_w].reshape(n_fsdp, n_small * rows_w)
    small_sum = jnp.pad(small_sum, ((0, 0), (0, 3 * wide - n_small * rows_w)))
    qkv_sum = qkv_sum[: n_fsdp * rows_w].reshape(n_fsdp, rows_w, 3 * wide)
    qkv_own = links.swap_fsdp(jnp.concatenate([qkv_sum, small_sum[:, None]], axis=1))
    small_own = jnp.sum(qkv_own[:, rows_w, : n_small * rows_w].astype(F32), axis=0).reshape(n_small, rows_w)
    qkv_own = from_fsdp(qkv_own[:, :rows_w]).astype(F32)

    grads = (wg_grad, wu_grad, wd_grad)
    shared_mine = jnp.concatenate(
        [grad[:tile_cols] for grad in grads] + [grad[tile_cols:sh_cols] for grad in grads], axis=0)
    shared_give = jnp.concatenate(
        [grad[sh_cols : sh_cols + tile_cols] for grad in grads]
        + [grad[sh_cols + tile_cols : 2 * sh_cols] for grad in grads], axis=0)
    shared_got = links.partner(shared_give, 2)
    shared_grads = (shared_mine.astype(F32) + shared_got.astype(F32)).astype(BF)
    shared_own = lax.all_to_all(
        shared_grads.T.reshape(n_all, rows_w, 3 * sh_cols), ALL, split_axis=0, concat_axis=0, tiled=True
    )
    cut = 3 * tile_cols
    shared_own = [
        from_owner(
            shared_own[:, :, k * tile_cols : (k + 1) * tile_cols],
            shared_own[:, :, cut + k * rest_cols : cut + (k + 1) * rest_cols],
        ).astype(F32)
        for k in range(3)
    ]
    routed_grads = jnp.stack(
        [
            jnp.concatenate([grad[low : low + ex_cols] for grad in grads], axis=0)
            for low in (shared_units, shared_units + ex_cols)
        ]
    )
    routed_grads = lax.psum_scatter(routed_grads, "fsdp", scatter_dimension=0, axis_index_groups=halves).astype(F32)
    routed_grads = [routed_grads[k * ex_cols : (k + 1) * ex_cols] for k in range(3)]
    return (
        hidden_out.reshape(micro, tok, width),
        in_grad.reshape(micro, tok, width),
        small_own[experts + 1],
        qkv_own[0],
        qkv_own[1],
        qkv_own[2],
        small_own[experts + 3 :],
        out_own,
        small_own[experts + 2],
        small_own[:experts].T,
        small_own[experts],
        shared_own[0],
        shared_own[1],
        shared_own[2],
        routed_grads[0].T[None],
        routed_grads[1].T[None],
        routed_grads[2][None],
    )


def solution(mesh):
    rows = P(ALL, None)
    tokens = P(None, ALL, None)
    in_specs = (
        tokens, P(None, ALL), tokens, tokens, P(ALL), rows, rows, rows, P(None, ALL), rows,
        P(ALL), rows, P(ALL), rows, rows, rows,
        P("expert", None, "fsdp"), P("expert", None, "fsdp"), P("expert", "fsdp", None),
    )
    out_specs = (
        tokens, tokens, P(ALL), rows, rows, rows, P(None, ALL), rows, P(ALL), rows, P(ALL),
        rows, rows, rows,
        P("expert", None, "fsdp"), P("expert", None, "fsdp"), P("expert", "fsdp", None),
    )
    on_device = on_device_ring if mesh.shape["expert"] == 8 and mesh.shape["fsdp"] == 4 else on_device_any
    return jax.shard_map(on_device, mesh=mesh, in_specs=in_specs, out_specs=out_specs, check_vma=False)
```

```python
import functools

import jax
import jax.numpy as jnp
from jax import lax
from jax.experimental import pallas as pl
from jax.experimental.pallas import tpu as pltpu
from jax.sharding import PartitionSpec as P

HEADS = 16
HEAD = 128
SHARED_FF = 5632
EPSILON = 1e-06
ROPE_BASE = 1000000.0
MASKED = -1e30
ALL = ("expert", "fsdp")
BF = jnp.bfloat16
F32 = jnp.float32
LANES = 128
COLS = 1024
GRAD_TILE = 384


def normalize(values):
    inverse = lax.rsqrt(jnp.mean(values * values, axis=-1, keepdims=True) + EPSILON)
    return (values * inverse, inverse)


def norm_back(grad_normed, scaled, inverse, gain_vec):
    grad_scaled = grad_normed * gain_vec
    return inverse * (grad_scaled - scaled * jnp.mean(grad_scaled * scaled, axis=-1, keepdims=True))


def angle_tables(places):
    inverse = 1.0 / ROPE_BASE ** (jnp.arange(0, HEAD, 2).astype(F32) / HEAD)
    angles = places.astype(F32)[:, None] * inverse[None, :]
    cosine, sine = jnp.cos(angles), jnp.sin(angles)
    return jnp.concatenate([cosine, cosine], axis=1), jnp.concatenate([-sine, sine], axis=1)


def silu_parts(pre_act):
    logistic = 1.0 / (1.0 + jnp.exp(-pre_act))
    return (pre_act * logistic, logistic * (1.0 + pre_act * (1.0 - logistic)))


def contract(pattern, left_op, right_op):
    return jnp.einsum(pattern, left_op, right_op, preferred_element_type=F32)


def dot_nt(left_op, right_op):
    return lax.dot_general(left_op, right_op, (((1,), (1,)), ((), ())), preferred_element_type=F32)


def dot_nn(left_op, right_op):
    return lax.dot_general(left_op, right_op, (((1,), (0,)), ((), ())), preferred_element_type=F32)


def dot_tn(left_op, right_op):
    return lax.dot_general(left_op, right_op, (((0,), (0,)), ((), ())), preferred_element_type=F32)


def after(value, *earlier):
    return lax.optimization_barrier((value, earlier))[0]


class Links:
    def __init__(self):
        self.n_exp = lax.axis_size("expert")
        self.n_fsdp = lax.axis_size("fsdp")
        self.my_exp = lax.axis_index("expert")
        self.my_fsdp = lax.axis_index("fsdp")
        self.n_all = self.n_exp * self.n_fsdp

    def partner(self, value, bit):
        pairs = [
            (e * self.n_fsdp + f, e * self.n_fsdp + (f ^ bit)) for e in range(self.n_exp) for f in range(self.n_fsdp)
        ]
        return lax.ppermute(value, ALL, pairs)

    def gather_rows(self, value):
        return lax.all_gather(value, "expert", axis=0)

    def sum_rows(self, value):
        return lax.psum_scatter(value.astype(BF), "expert", scatter_dimension=0).astype(F32)

    def swap_fsdp(self, value):
        result = value
        for bit in range(1, self.n_fsdp):
            other = lax.bitwise_xor(self.my_fsdp, bit)
            block = lax.dynamic_index_in_dim(value, other, 0, keepdims=False)
            result = lax.dynamic_update_index_in_dim(result, self.partner(block, bit), other, 0)
        return result

    def gather_four(self, value):
        far = self.partner(value, 2)
        return [value, self.partner(value, 1), far, self.partner(far, 1)]

    def gather_seq(self, value):
        return jnp.concatenate(self.gather_four(value), axis=1)

    def sum_four(self, parts):
        far = (parts[2].astype(F32) + self.partner(parts[3].astype(BF), 1).astype(F32)).astype(BF)
        near = parts[0].astype(F32) + self.partner(parts[1].astype(BF), 1).astype(F32)
        return near + self.partner(far, 2).astype(F32)


def attend_kernel(heads, seq, scale, split, x_ref, w_ref, bias_ref, cos_ref, sin_ref, place_ref, seg_ref,
                  place_row_ref, seg_row_ref, core_ref, qkv_ref, *out_refs):
    lin = dot_nn(x_ref[...], w_ref[...]) + bias_ref[...]
    cosine, sine = cos_ref[...], sin_ref[...]
    span = heads * HEAD
    for micro in range(x_ref.shape[0] // seq):
        low, high = micro * seq, (micro + 1) * seq
        visible = (place_row_ref[...] <= place_ref[...]) & (seg_row_ref[micro : micro + 1, :] == seg_ref[low:high, :])
        found = []
        for head in range(heads):
            at = head * HEAD
            query = lin[low:high, at : at + HEAD]
            key = lin[low:high, span + at : span + at + HEAD]
            value = lin[low:high, 2 * span + at : 2 * span + at + HEAD].astype(BF)
            query = (query * cosine + pltpu.roll(query, HEAD // 2, 1) * sine).astype(BF)
            key = (key * cosine + pltpu.roll(key, HEAD // 2, 1) * sine).astype(BF)
            scores = jnp.where(visible, dot_nt(query, key) * scale, MASKED)
            exps = jnp.exp(scores - jnp.max(scores, axis=1, keepdims=True))
            probs = exps / jnp.sum(exps, axis=1, keepdims=True)
            found.append(dot_nn(probs.astype(BF), value))
            qkv_ref[low:high, at : at + HEAD] = query
            qkv_ref[low:high, span + at : span + at + HEAD] = key
            qkv_ref[low:high, 2 * span + at : 2 * span + at + HEAD] = value
        if not split:
            out_refs[0][low:high, :] = jnp.concatenate(found, axis=1).astype(BF)
            continue
        first = jnp.concatenate([item[:, : HEAD // 2] for item in found], axis=1)
        second = jnp.concatenate([item[:, HEAD // 2 :] for item in found], axis=1)
        out_refs[0][low:high, :] = jnp.where(core_ref[0] == 0, first, second).astype(BF)
        out_refs[1][low:high, :] = jnp.where(core_ref[0] == 0, second, first).astype(BF)


def attend_back_kernel(heads, seq, scale, split, grad_ref, other_ref, qkv_ref, cos_ref, sin_ref, place_ref, seg_ref,
                       place_row_ref, seg_row_ref, core_ref, w_ref, x_ref, lin_ref, normed_ref, gain_ref, *panel_refs):
    cosine, sine = cos_ref[...], sin_ref[...]
    span = heads * HEAD
    if split:
        first = jnp.where(core_ref[0] == 0, grad_ref[...], other_ref[...])
        second = jnp.where(core_ref[0] == 0, other_ref[...], grad_ref[...])
        half = HEAD // 2
        grad_out = jnp.concatenate(
            [part[:, k * half : (k + 1) * half] for k in range(heads) for part in (first, second)], axis=1)
    else:
        grad_out = dot_nt(grad_ref[...], other_ref[...]).astype(BF)
    for micro in range(grad_ref.shape[0] // seq):
        low, high = micro * seq, (micro + 1) * seq
        visible = (place_row_ref[...] <= place_ref[...]) & (seg_row_ref[micro : micro + 1, :] == seg_ref[low:high, :])
        for head in range(heads):
            at = head * HEAD
            query = qkv_ref[low:high, at : at + HEAD]
            key = qkv_ref[low:high, span + at : span + at + HEAD]
            value = qkv_ref[low:high, 2 * span + at : 2 * span + at + HEAD]
            grad = grad_out[low:high, at : at + HEAD]
            scores = jnp.where(visible, dot_nt(query, key) * scale, MASKED)
            exps = jnp.exp(scores - jnp.max(scores, axis=1, keepdims=True))
            probs = exps / jnp.sum(exps, axis=1, keepdims=True)
            grad_probs = dot_nt(grad, value)
            grad_value = dot_tn(probs.astype(BF), grad)
            grad_scores = probs * (grad_probs - jnp.sum(probs * grad_probs, axis=1, keepdims=True))
            grad_scores = grad_scores.astype(BF)
            grad_query = dot_nn(grad_scores, key) * scale
            grad_key = dot_tn(grad_scores, query) * scale
            grad_query = grad_query * cosine - pltpu.roll(grad_query, HEAD // 2, 1) * sine
            grad_key = grad_key * cosine - pltpu.roll(grad_key, HEAD // 2, 1) * sine
            lin_ref[low:high, at : at + HEAD] = grad_query.astype(BF)
            lin_ref[low:high, span + at : span + at + HEAD] = grad_key.astype(BF)
            lin_ref[low:high, 2 * span + at : 2 * span + at + HEAD] = grad_value.astype(BF)
    if split:
        panel_ref = panel_refs[0]
        count, rows = panel_ref.shape[0], x_ref.shape[1] // panel_ref.shape[0]
        grad_w = dot_tn(x_ref[...], lin_ref[...]).astype(BF)
        for k in range(count):
            panel_ref[k, :rows, :] = grad_w[k * rows : (k + 1) * rows, :]
        behind = panel_ref.shape[1] - rows
        panel_ref[:, rows:, :] = jnp.zeros((count, behind, panel_ref.shape[2]), BF)
    part = dot_nt(lin_ref[...], w_ref[...])

    @pl.when(pl.program_id(0) == 0)
    def _():
        normed_ref[...] = part

    @pl.when(pl.program_id(0) > 0)
    def _():
        total = normed_ref[...] + part
        normed_ref[...] = total
        gain_ref[...] = jnp.sum(total * x_ref[...].astype(F32), axis=0, keepdims=True)


def whole(shape):
    return pl.BlockSpec(shape, lambda *_: (0,) * len(shape))


def attend(normed, wqkv, bias, tables, seq, back=None, core=None, panel=None):
    cosine, sine, place, seg, place_row, seg_row = tables
    rows = normed.shape[0]
    pairs = 2
    wide3 = bias.shape[1]
    heads = wide3 // 3 // HEAD // pairs
    span = heads * HEAD
    scale = HEAD ** (-0.5)
    split = core is not None
    common = (cosine, sine, place, seg, place_row, seg_row, core if split else jnp.zeros((1,), jnp.int32))
    common_specs = [whole(item.shape) for item in common[:-1]] + [pl.BlockSpec(memory_space=pltpu.SMEM)]
    params = pltpu.CompilerParams(vmem_limit_bytes=48 * 2**20)
    cost = pl.CostEstimate(flops=10**8, bytes_accessed=10**6, transcendentals=10**5)
    columns, count = (span // 2, 2) if split else (span, 1)
    kept = pl.BlockSpec((rows, columns), lambda p: (0, p))
    if back is None:
        return pl.pallas_call(
            functools.partial(attend_kernel, heads, seq, scale, split),
            grid=(pairs,),
            in_specs=[
                whole(normed.shape),
                pl.BlockSpec((wqkv.shape[0], 3 * span), lambda p: (0, p)),
                pl.BlockSpec((1, 3 * span), lambda p: (0, p)),
            ] + common_specs,
            out_specs=[pl.BlockSpec((rows, 3 * span), lambda p: (0, p))] + [kept] * count,
            out_shape=[jax.ShapeDtypeStruct((rows, wide3), BF)]
            + [jax.ShapeDtypeStruct((rows, pairs * columns), BF)] * count,
            compiler_params=params,
            cost_estimate=cost,
            name="attend",
        )(normed, wqkv, bias, *common)
    grad, other, qkv = back
    return pl.pallas_call(
        functools.partial(attend_back_kernel, heads, seq, scale, split),
        grid=(pairs,),
        in_specs=([kept, kept] if split else [whole(grad.shape), pl.BlockSpec((span, other.shape[1]), lambda p: (p, 0))])
        + [pl.BlockSpec((rows, 3 * span), lambda p: (0, p))]
        + common_specs
        + [pl.BlockSpec((wqkv.shape[0], 3 * span), lambda p: (0, p)), whole(normed.shape)],
        out_specs=[
            pl.BlockSpec((rows, 3 * span), lambda p: (0, p)), whole((rows, wqkv.shape[0])), whole((1, wqkv.shape[0]))]
        + ([pl.BlockSpec(panel[:2] + (3 * span,), lambda p: (0, 0, p))] if split else []),
        out_shape=[jax.ShapeDtypeStruct((rows, wide3), BF)]
        + [jax.ShapeDtypeStruct((count, wqkv.shape[0]), F32) for count in (rows, 1)]
        + ([jax.ShapeDtypeStruct(panel, BF)] if split else []),
        compiler_params=params,
        cost_estimate=cost,
        name="attend_back",
    )(grad, other, qkv, *common, wqkv, normed)


def feed_kernel(experts, shared, expert_ref, *refs):
    x_refs, g_refs = refs[:3], refs[3:6]
    weights = (refs[6:9], refs[9:12])
    unit_refs, gn_refs, out_refs = refs[12:18], refs[18:21], refs[21:24]
    x_all, g_all = refs[24:26]
    units = (refs[26:29], refs[29:32])
    gn, out, sems = refs[32:]
    own, width = x_refs[0].shape
    rows = 4 * own
    expert = expert_ref[0]

    def block(k):
        return pl.ds(k * own, 2 * own if k == 2 else own)

    def start(number, source, target):
        copy = pltpu.make_async_copy(source, target, sems.at[number])
        copy.start()
        return copy

    x_copies = [start(k, x_refs[k], x_all.at[block(k), :]) for k in range(3)]
    g_copies = [start(3 + k, g_refs[k], g_all.at[block(k), :]) for k in range(3)]
    for copy in x_copies:
        copy.wait()
    gates = [dot_nt(x_all[...], weights[k][0][...]) for k in range(2)]
    for copy in g_copies:
        copy.wait()
    names = g_all[:, width:].astype(F32)
    lane = lax.broadcasted_iota(jnp.int32, names.shape, 1)
    hit = jnp.where((lane < 4) & (names == expert.astype(F32)), 1.0, 0.0)
    hit = jnp.sum(hit, axis=1, keepdims=True)
    first = shared // LANES * LANES
    logits = gates[0][:, first : first + LANES]
    lane = lane - (shared - first)
    is_expert = (lane >= 0) & (lane < experts)
    scores = jnp.where(is_expert, logits, MASKED)
    exps = jnp.where(is_expert, jnp.exp(scores - jnp.max(scores, axis=1, keepdims=True)), 0.0)
    mine = jnp.sum(jnp.where(lane == expert, exps, 0.0), axis=1, keepdims=True)
    mine = mine / jnp.sum(exps, axis=1, keepdims=True)
    last = jnp.sum(jnp.where(lane == experts, logits, 0.0), axis=1, keepdims=True)
    scales = (1.0 / (1.0 + jnp.exp(-last)), mine * hit)
    dots, copies = [], []
    for k in range(2):
        hs, dg, du = units[k]
        act, slope = silu_parts(gates[k])
        up = dot_nt(x_all[...], weights[k][1][...])
        grad = dot_nt(g_all[:, :width], weights[k][2][...])
        hidden = act * up
        dots.append(jnp.sum(hidden * grad, axis=1, keepdims=True))
        grad = grad * scales[k]
        hs[...] = (hidden * scales[k]).astype(BF)
        dg[...] = (grad * up * slope).astype(BF)
        du[...] = (grad * act).astype(BF)
        copies += [
            start(3 * k + j, source, target) for j, (source, target) in enumerate(zip((hs, dg, du), unit_refs[3 * k :]))
        ]
    lane = lax.broadcasted_iota(jnp.int32, (rows, LANES), 1)
    extra = jnp.where(lane == expert, dots[1] * hit, 0.0) + jnp.where(lane == experts, dots[0], 0.0)
    gn[:, width:] = extra.astype(BF)
    total = dot_nn(units[0][1][...], weights[0][0][...]) + dot_nn(units[0][2][...], weights[0][1][...])
    total += dot_nn(units[1][1][...], weights[1][0][...]) + dot_nn(units[1][2][...], weights[1][1][...])
    gn[:, :width] = total.astype(BF)
    copies += [start(6 + k, gn.at[block(k), :], gn_refs[k]) for k in range(3)]
    total = dot_nn(units[0][0][...], weights[0][2][...]) + dot_nn(units[1][0][...], weights[1][2][...])
    out[...] = total.astype(BF)
    copies += [start(9 + k, out.at[block(k), :], out_refs[k]) for k in range(3)]
    for copy in copies:
        copy.wait()


def feed(expert, x_blocks, g_blocks, shared_w, routed_w, experts, shared):
    own, width = x_blocks[0].shape
    rows = 4 * own
    wide = g_blocks[0].shape[1]
    counts = (shared_w[0].shape[0], routed_w[0].shape[0])
    anywhere = pl.BlockSpec(memory_space=pl.ANY)
    weights = [pltpu.with_memory_space_constraint(weight, pltpu.VMEM) for weight in (*shared_w, *routed_w)]
    found = pl.pallas_call(
        functools.partial(feed_kernel, experts, shared),
        in_specs=[pl.BlockSpec(memory_space=pltpu.SMEM)]
        + [anywhere] * 6
        + [pl.BlockSpec(memory_space=pltpu.VMEM)] * 6,
        out_specs=[anywhere] * 12,
        scratch_shapes=[pltpu.VMEM((rows, width), BF), pltpu.VMEM((rows, wide), BF)]
        + [pltpu.VMEM((rows, count), BF) for count in counts for _ in range(3)]
        + [pltpu.VMEM((rows, wide), BF), pltpu.VMEM((rows, width), BF), pltpu.SemaphoreType.DMA((12,))],
        out_shape=[jax.ShapeDtypeStruct((rows, count), BF) for count in counts for _ in range(3)]
        + [jax.ShapeDtypeStruct((count, columns), BF) for columns in (wide, width) for count in (own, own, 2 * own)],
        compiler_params=pltpu.CompilerParams(vmem_limit_bytes=42 * 2**20),
        cost_estimate=pl.CostEstimate(flops=16 * 10**9, bytes_accessed=3 * 10**7, transcendentals=10**6),
        name="feed",
    )(expert, *x_blocks, *g_blocks, *weights)
    return found[:3], found[3:6], found[6:9], found[9:12]


SMALL_COST = pl.CostEstimate(flops=0, bytes_accessed=10**6, transcendentals=0)


def pack_kernel(full, rest, gate_ref, up_ref, down_ref, out_ref):
    count = out_ref.shape[0]
    refs = (gate_ref, up_ref, down_ref)
    for j in range(count):
        for k in range(3):
            out_ref[j, :, k * full : (k + 1) * full] = refs[k][:, j * full : (j + 1) * full]
        low = count * full + j * rest
        out_ref[j, :, 3 * full :] = jnp.concatenate([ref[:, low : low + rest] for ref in refs], axis=1)


def pack_shared(gate, up, down, count, full, rest):
    vmem = pl.BlockSpec(memory_space=pltpu.VMEM)
    return pl.pallas_call(
        functools.partial(pack_kernel, full, rest),
        in_specs=[vmem] * 3,
        out_specs=vmem,
        out_shape=jax.ShapeDtypeStruct((count, gate.shape[0], 3 * (full + rest)), BF),
        compiler_params=pltpu.CompilerParams(vmem_limit_bytes=16 * 2**20),
        cost_estimate=SMALL_COST,
        name="pack_shared",
    )(gate, up, down)


def unpack_kernel(full, rest, order_ref, in_ref, *out_refs):
    count = in_ref.shape[0]
    for k in range(3):
        for j in range(count):
            out_refs[k][:, j * full : (j + 1) * full] = in_ref[order_ref[j], :, k * full : (k + 1) * full].astype(F32)
        low = 3 * full + k * rest
        for j in range(0, count, 4):
            at = count * full + j * rest
            piece = jnp.concatenate([in_ref[order_ref[j + i], :, low : low + rest] for i in range(4)], axis=1)
            out_refs[k][:, at : at + 4 * rest] = piece.astype(F32)


def unpack_shared(blocks, order, full, rest):
    count, rows, _ = blocks.shape
    vmem = pl.BlockSpec(memory_space=pltpu.VMEM)
    return pl.pallas_call(
        functools.partial(unpack_kernel, full, rest),
        in_specs=[pl.BlockSpec(memory_space=pltpu.SMEM), vmem],
        out_specs=[vmem] * 3,
        out_shape=[jax.ShapeDtypeStruct((rows, count * (full + rest)), F32)] * 3,
        compiler_params=pltpu.CompilerParams(vmem_limit_bytes=16 * 2**20),
        cost_estimate=SMALL_COST,
        name="unpack_shared",
    )(order, blocks)


def fold_kernel(full, rest, *refs):
    out_ref, rests = refs[6], []
    for k in range(3):
        total = refs[2 * k][...].astype(F32) + refs[2 * k + 1][...].astype(F32)
        total = total.T.astype(BF)
        out_ref[:, k * full : (k + 1) * full] = total[:, :full]
        rests.append(total[:, full : full + rest])
    out_ref[:, 3 * full :] = jnp.concatenate(rests, axis=1)


def fold_shared(pairs, full, rest):
    vmem = pl.BlockSpec(memory_space=pltpu.VMEM)
    return pl.pallas_call(
        functools.partial(fold_kernel, full, rest),
        in_specs=[vmem] * 6,
        out_specs=vmem,
        out_shape=jax.ShapeDtypeStruct((pairs[0][0].shape[1], 3 * (full + rest)), BF),
        compiler_params=pltpu.CompilerParams(vmem_limit_bytes=24 * 2**20),
        cost_estimate=SMALL_COST,
        name="fold_shared",
    )(*[item for pair in pairs for item in pair])


def join_kernel(cuts, places_ref, *refs):
    mine_refs, far_refs, behind_ref, out_refs = refs[:2], refs[2:4], refs[4], refs[5:]
    n_blocks = mine_refs[0].shape[1] // LANES
    y = places_ref[2 * n_blocks]
    for k, pieces in enumerate(cuts):
        at = 0
        for low, count in pieces:
            for block in range(2 * n_blocks):
                half, column = block // n_blocks, block % n_blocks * LANES
                for source, side in ((mine_refs[half], y), (far_refs[half], 1 - y)):
                    target = pl.ds(pl.multiple_of((2 * places_ref[block] + side) * LANES, LANES), LANES)
                    out_refs[k][at : at + count, target] = source[low : low + count, column : column + LANES]
            at += count
        rest = out_refs[k].shape[0] - at
        out_refs[k][at:, :] = behind_ref[...] if k == 0 else jnp.zeros((rest, out_refs[k].shape[1]), BF)


def join_shared(places, mine, far, behind, cuts):
    rows = sum(count for _, count in cuts[0]) + behind.shape[0]
    vmem = pl.BlockSpec(memory_space=pltpu.VMEM)
    return pl.pallas_call(
        functools.partial(join_kernel, cuts),
        in_specs=[pl.BlockSpec(memory_space=pltpu.SMEM)] + [vmem] * 5,
        out_specs=[vmem] * 3,
        out_shape=[jax.ShapeDtypeStruct((rows, 4 * mine[0].shape[1]), BF)] * 3,
        compiler_params=pltpu.CompilerParams(vmem_limit_bytes=24 * 2**20),
        cost_estimate=SMALL_COST,
        name="join_shared",
    )(places, *mine, *far, behind)


def weights_kernel(n_sets, split, y_ref, *refs):
    sources, lhs_refs = refs[:12], refs[12 : 12 + 4 * n_sets]
    out_refs, (held, sems) = refs[12 + 4 * n_sets : -2], refs[-2:]
    rows, width = held.shape
    own = rows // 16

    @pl.when(pl.program_id(0) == 0)
    def _():
        copies = []
        for k in range(12):
            at, count = (k // 3 * 4 + k % 3) * own, 2 * own if k % 3 == 2 else own
            copies.append(
                pltpu.make_async_copy(sources[k].at[:, pl.ds(0, width)], held.at[pl.ds(at, count), :], sems.at[k]))
        for copy in copies:
            copy.start()
        for copy in copies:
            copy.wait()

    for k in range(n_sets):
        lhs = jnp.concatenate([ref[...] for ref in lhs_refs[4 * k : 4 * k + 4]], axis=0)
        total = dot_tn(lhs, held[...])
        if not split:
            for tile in range(2):
                at = 0
                for out_ref in out_refs:
                    low, high = max(at, tile * GRAD_TILE), min(at + out_ref.shape[0], (tile + 1) * GRAD_TILE)
                    if low < high:

                        @pl.when(pl.program_id(0) == tile)
                        def _(out_ref=out_ref, low=low, high=high, at=at, tile=tile):
                            out_ref[low - at : high - at, :] = total[
                                low - tile * GRAD_TILE : high - tile * GRAD_TILE, :].astype(BF)

                    at += out_ref.shape[0]
            continue
        for block in range(width // LANES // 2):
            even = total[:, 2 * block * LANES : (2 * block + 1) * LANES]
            odd = total[:, (2 * block + 1) * LANES : (2 * block + 2) * LANES]
            columns = slice(block * LANES, (block + 1) * LANES)
            out_refs[2 * k][:, columns] = jnp.where(y_ref[0] == 0, even, odd).astype(BF)
            out_refs[2 * k + 1][:, columns] = jnp.where(y_ref[0] == 0, odd, even).astype(BF)


def weight_grads(y, sources, lhs_sets, width, parts=None):
    rows, units = lhs_sets[0][0].shape
    n_sets = len(lhs_sets)
    n_tiles = units // GRAD_TILE
    split = parts is None
    if split:
        shapes = [(GRAD_TILE, width // 2)] * (2 * n_sets)
    else:
        shapes = [(count, width) for count in parts]
    return pl.pallas_call(
        functools.partial(weights_kernel, n_sets, split),
        grid=(n_tiles,),
        in_specs=[pl.BlockSpec(memory_space=pltpu.SMEM)]
        + [pl.BlockSpec(memory_space=pl.ANY)] * 12
        + [pl.BlockSpec((rows, GRAD_TILE), lambda i: (0, i))] * (4 * n_sets),
        out_specs=[whole(shape) for shape in shapes],
        scratch_shapes=[pltpu.VMEM((4 * rows, width), BF), pltpu.SemaphoreType.DMA((12,))],
        out_shape=[jax.ShapeDtypeStruct(shape, BF) for shape in shapes],
        compiler_params=pltpu.CompilerParams(vmem_limit_bytes=56 * 2**20),
        cost_estimate=pl.CostEstimate(
            flops=4 * 10**9 * n_sets * n_tiles, bytes_accessed=2 * 10**7, transcendentals=0),
        name="weight_grads",
    )(y, *sources, *[item for lhs in lhs_sets for item in lhs])


def feed_plain(normed, grad, named, expert, wg, wu, wd, router, experts, shared):
    logits = contract("td,cd->tc", normed, router)
    router_probs = jax.nn.softmax(logits[:, :experts], axis=-1)
    shared_scale = jax.nn.sigmoid(logits[:, experts : experts + 1])
    hot = (jnp.arange(experts) == expert).astype(F32)
    gate_here = jnp.sum(router_probs * hot, axis=1, keepdims=True) * named[:, None]
    is_shared = (jnp.arange(wg.shape[0]) < shared)[None]
    row_scale = jnp.where(is_shared, shared_scale, gate_here)
    act, slope = silu_parts(contract("td,cd->tc", normed, wg))
    up = contract("td,cd->tc", normed, wu)
    hidden = act * up
    hidden_scaled = (hidden * row_scale).astype(BF)
    grad_hidden = contract("td,fd->tf", grad, wd)
    dots = hidden * grad_hidden
    dot_shared = jnp.sum(jnp.where(is_shared, dots, 0.0), axis=1, keepdims=True)
    dot_expert = jnp.sum(jnp.where(is_shared, 0.0, dots), axis=1, keepdims=True) * named[:, None]
    grad_pre = grad_hidden * row_scale
    grad_gate = (grad_pre * up * slope).astype(BF)
    grad_up = (grad_pre * act).astype(BF)
    grad_normed = contract("tc,cd->td", grad_gate, wg) + contract("tc,cd->td", grad_up, wu)
    extra = jnp.concatenate([dot_expert * hot, dot_shared], axis=1)
    extra = jnp.pad(extra, ((0, 0), (0, LANES - extra.shape[1])))
    out = contract("tf,fd->td", hidden_scaled, wd)
    return (
        jnp.concatenate([grad_normed, extra], axis=1),
        out,
        contract("tc,td->cd", grad_gate, normed),
        contract("tc,td->cd", grad_up, normed),
        contract("tf,td->fd", hidden_scaled, grad),
    )


def ring_perm(move):
    pairs = []
    for me in range(32):
        z, x, y, c = me // 8, me // 4 % 2, me // 2 % 2, me % 2
        z, x, y, c = move(z, x, y, c)
        pairs.append((me, ((z * 2 + x) * 2 + y) * 2 + c))
    return pairs


MOVES = {
    "core": lambda z, x, y, c: (z, x, y, 1 - c),
    "y": lambda z, x, y, c: (z, x, 1 - y, c),
    "yc": lambda z, x, y, c: (z, x, 1 - y, 1 - c),
    "x": lambda z, x, y, c: (z, 1 - x, y, c),
    "z1": lambda z, x, y, c: ((z + 1) % 4, x, y, c),
    "z2": lambda z, x, y, c: ((z + 2) % 4, x, y, c),
    "z3": lambda z, x, y, c: ((z + 3) % 4, x, y, c),
}


def send(value, link):
    return lax.ppermute(value, ALL, ring_perm(MOVES[link]))


def sync(*values):
    return lax.optimization_barrier(values)


def pick(value, place, axis=0):
    return lax.dynamic_index_in_dim(value, place, axis, keepdims=False)


def put(value, block, place, axis=0):
    return lax.dynamic_update_index_in_dim(value, block, place, axis)


def in_order(mine, other, bit, axis):
    return jnp.where(bit == 0, jnp.stack([mine, other], axis=axis), jnp.stack([other, mine], axis=axis))


def on_device_ring(
    hidden_in, seg_ids, routes, out_grad, norm_gain1, w_query, w_key, w_value, b_qkv, w_out,
    norm_gain2, w_router, shared_gate, sh_gate, sh_up, sh_down, ex_gate, ex_up, ex_down,
):
    micro, tok, width = hidden_in.shape
    experts = w_router.shape[1]
    rows_w = w_query.shape[0]
    top_count = routes.shape[2]
    my_exp, my_fsdp = lax.axis_index("expert"), lax.axis_index("fsdp")
    z, x, y, c = my_exp // 2, lax.rem(my_exp, 2), my_fsdp // 2, lax.rem(my_fsdp, 2)
    n_exp, n_fsdp, n_all = 8, 4, 32
    heads_dev = HEADS // n_fsdp
    wide = heads_dev * HEAD
    seq, own = tok * n_fsdp, micro * tok
    ex_cols = ex_gate.shape[2]
    sh_cols = SHARED_FF // 16
    full_cols = sh_cols // LANES * LANES
    rest_cols = sh_cols - full_cols
    unit_cols = 3 * sh_cols

    def slot(step, other):
        return lax.rem(z + 4 - step, 4) * 2 + (1 - x if other else x)

    def by_fsdp(three):
        rows = three.shape[0]
        split = three.reshape(rows, 3, 2, 2, heads_dev // 2, 2, HEAD)
        return split.transpose(5, 2, 0, 3, 1, 4, 6).reshape(n_fsdp, rows, 3 * wide)

    def from_fsdp(blocks):
        rows = blocks.shape[1]
        split = blocks.reshape(2, 2, rows, 2, 3, heads_dev // 2, HEAD)
        return split.transpose(4, 2, 1, 3, 5, 0, 6).reshape(3, rows, width)

    def swap_core(blocks):
        mine, give = pick(blocks, c, 2), pick(blocks, 1 - c, 2)
        return in_order(mine, send(give, "core"), c, 2)

    def swap_z(blocks, k):
        return send(pick(blocks, lax.rem(z + k, 4)), f"z{k}")

    small = jnp.concatenate(
        [w_router.T, shared_gate[None], norm_gain1[None], norm_gain2[None], b_qkv, seg_ids.astype(BF)], axis=0)
    n_small = experts + 6
    small = [small.reshape(1, (n_small + micro) * rows_w)]
    for _ in range(3):
        small.append(send(small[-1], "z1"))
    small = jnp.concatenate(small)
    qkv = by_fsdp(jnp.stack([w_query, w_key, w_value], axis=1))
    arrived = [send(pick(qkv, lax.bitwise_xor(my_fsdp, k)), link) for k, link in ((1, "core"), (2, "y"), (3, "yc"))]
    grad_own = out_grad.reshape(own, width)
    names = jnp.pad(routes.reshape(own, top_count).astype(BF), ((0, 0), (0, LANES - top_count)))
    g_own = [jnp.concatenate([grad_own, names], axis=1)]
    g_pair = []
    routed_mine = jnp.concatenate([ex_gate[0].T, ex_up[0].T, ex_down[0]], axis=0)
    small, arrived, g_own[0], routed_mine = sync(small, arrived, g_own[0], routed_mine)
    for k in range(3):
        qkv = put(qkv, arrived[k], lax.bitwise_xor(my_fsdp, k + 1))
    block = jnp.concatenate([w_out[:, k * wide : (k + 1) * wide] for k in range(n_fsdp)], axis=0)
    block = jnp.concatenate([qkv.reshape(n_fsdp * rows_w, 3 * wide), block], axis=1)
    following = send(block, "z1")
    small = jnp.concatenate([small, send(small, "x")])
    at_pair = send(sync(block, small)[0], "x")
    small = jnp.concatenate([small, send(small, "y")])
    got = send(sync(routed_mine[:264], small)[0], "y")
    small = jnp.concatenate([small, send(small, "core")])
    block, following, at_pair, small, got, routed_mine, sh_gate, sh_up, sh_down, hidden_in = sync(
        block, following, at_pair, small, got, routed_mine, sh_gate, sh_up, sh_down, hidden_in)
    a_blocks = [routed_mine[k * 264 : (k + 1) * 264] for k in range(4)]
    got_blocks = [got]
    weights = jnp.zeros((n_exp,) + block.shape, BF)

    def ring_put(weights, step, mine, other):
        return put(put(weights, mine, slot(step, 0)), other, slot(step, 1))

    first_pair, mine = at_pair, following
    at_pair, following = send(mine, "x"), send(mine, "z1")
    places = jnp.stack(
        [slot(step, other) * 4 + lax.bitwise_xor(my_fsdp, k) for k in (0, 2, 1, 3) for other in range(2) for step in range(4)])
    choice = (jnp.arange(n_all)[:, None] == places[None]).astype(BF)
    small = dot_nn(choice, small).astype(BF).reshape(n_all, n_small + micro, rows_w)
    small = small.transpose(1, 0, 2).reshape(n_small + micro, width)
    router_rows = small[: experts + 1]
    gain_one = small[experts + 1].astype(F32)
    gain_two = small[experts + 2].astype(F32)
    bias = pick(by_fsdp(small[experts + 3 : n_small].astype(F32)[None]), my_fsdp)
    seg_seq = lax.dynamic_slice_in_dim(small[n_small:], my_exp * seq, seq, 1).reshape(micro, n_fsdp, tok)
    hidden = hidden_in.reshape(own, width).astype(F32)
    scaled_one, inverse_one = normalize(hidden)
    normed_one = (scaled_one * gain_one).astype(BF).reshape(micro, tok, width)
    seq_far, seq_near = send(normed_one, "y"), send(normed_one, "core")

    (block, mine, following, at_pair, seq_far, seq_near, normed_one, a_blocks, bias, router_rows, seg_seq,
     sh_gate, sh_up, sh_down) = sync(
        block, mine, following, at_pair, seq_far, seq_near, normed_one, a_blocks, bias, router_rows, seg_seq,
        sh_gate, sh_up, sh_down)

    previous, previous_pair, mine = mine, at_pair, following
    at_pair, following = send(mine, "x"), send(mine, "z1")
    shared_w = pack_shared(sh_gate, sh_up, sh_down, 16, full_cols, rest_cols)
    shared_w = swap_core(shared_w.reshape(4, 2, 2, rows_w, unit_cols))
    weights = ring_put(ring_put(weights, 0, block, first_pair), 1, previous, previous_pair)
    seq_last = send(seq_far, "core")
    got = send(a_blocks[1], "y")
    mine, following, at_pair, got, a_blocks, shared_w, seq_last, weights = sync(
        mine, following, at_pair, got, a_blocks, shared_w, seq_last, weights)
    got_blocks.append(got)

    weights = ring_put(weights, 2, mine, at_pair)
    at_pair = send(following, "x")
    got = send(a_blocks[2], "y")
    shared_z = {1: swap_z(shared_w, 1), 3: swap_z(shared_w, 3)}
    order = lax.bitwise_xor(my_fsdp, jnp.arange(n_fsdp))
    places = (order[:, None] * tok + jnp.arange(tok)[None]).reshape(seq)
    seg_seq = jnp.take(seg_seq, order, axis=1).reshape(micro, seq).astype(jnp.int32)
    normed_seq = jnp.concatenate([normed_one, seq_near, seq_far, seq_last], axis=1).reshape(micro * seq, width)
    cosine, sine = angle_tables(places)
    tables = (cosine, sine, places[:, None], seg_seq.reshape(micro * seq, 1), places[None], seg_seq)
    following, at_pair, got, shared_z, shared_w, a_blocks, weights, tables, normed_seq, g_own[0] = sync(
        following, at_pair, got, shared_z, shared_w, a_blocks, weights, tables, normed_seq, g_own[0])
    got_blocks.append(got)
    weights = ring_put(weights, 3, following, at_pair)
    wqkv = weights.reshape(width, 4 * wide)

    def turned(value):
        value = value.reshape(micro, 2, 2, tok, -1)
        return jnp.concatenate([value[:, :, 1:], value[:, :, :1]], axis=2).reshape(micro * seq, -1)

    core_place = c.reshape(1)
    got = send(a_blocks[3], "y")
    far_w = pick(shared_w, lax.rem(z + 2, 4))
    shared_z[2] = [send(far_w[0], "z2")]
    shared_z[0] = pick(shared_w, z)
    shared_x = {}

    def swap_x(steps):
        arrived = send(jnp.stack([pick(shared_z[step], 1 - x) for step in steps]), "x")
        return arrived, [pick(shared_z[step], x) for step in steps]

    def as_columns(parts):
        blocks = [
            in_order(mine, arrived[k], x, 0) for arrived, all_mine in parts for k, mine in enumerate(all_mine)
        ]
        return jnp.stack(blocks).reshape(-1, unit_cols).T

    shared_x = [swap_x((0, 1))]
    g_pair.append(send(g_own[0], "x"))
    qkv_seq, keep, give = attend(normed_seq, wqkv, bias, tables, seq, core=core_place)
    wo = sync(weights, give)[0]
    wo = [wo[:, k * rows_w : (k + 1) * rows_w, 3 * wide :].reshape(n_exp * rows_w, wide) for k in range(n_fsdp)]
    wo = jnp.concatenate(wo, axis=1)
    got, shared_z, shared_x, qkv_seq, keep, give, wqkv, wo, far_w, g_pair = sync(
        got, shared_z, shared_x, qkv_seq, keep, give, wqkv, wo, far_w, g_pair)
    got_blocks.append(got)
    shared_w = [as_columns(shared_x)]
    arrived = turned(send(give, "core"))
    shared_z, shared_w, arrived, keep, wo, far_w, g_own, g_pair = sync(
        shared_z, shared_w, arrived, keep, wo, far_w, g_own, g_pair)
    shared_z[2].append(send(far_w[1], "z2"))
    arrived_w = [send(shared_w[0], "y")]
    shared_x = [swap_x((3,))]
    attended = jnp.where(c == 0, jnp.concatenate([keep, arrived], axis=1), jnp.concatenate([arrived, keep], axis=1))
    attn_part = contract("tc,cd->td", attended, wo).reshape(micro, 2, 2, tok, width)
    attn_part = attn_part[:, :, 0] + send(attn_part[:, :, 1].astype(BF), "core").astype(F32)
    near, last = attn_part[:, 0], attn_part[:, 1].astype(BF)
    last, near, shared_z, shared_x, shared_w, arrived_w, g_own, g_pair = sync(
        last, near, shared_z, shared_x, shared_w, arrived_w, g_own, g_pair)
    shared_z[2] = jnp.stack(shared_z[2])

    last = send(last, "y")
    shared_x.append(swap_x((2,)))
    g_own.append(send(g_own[0], "z1"))

    def blocks_of(mine, other):
        return [mine, other, send(jnp.concatenate([mine, other]), "core")]

    g_four = [blocks_of(g_own[0], g_pair[0])]
    after_attn = hidden + near.reshape(own, width) + last.astype(F32).reshape(own, width)
    scaled_two, inverse_two = normalize(after_attn)
    normed_two = (scaled_two * gain_two).astype(BF)
    x_own, x_pair = [normed_two], []
    shared_w.append(as_columns(shared_x))
    shared_w, arrived_w, x_own, after_attn, scaled_two, g_own, g_pair, got_blocks, g_four = sync(
        shared_w, arrived_w, x_own, after_attn, scaled_two, g_own, g_pair, got_blocks, g_four)

    arrived_w.append(send(shared_w[1], "y"))
    x_pair.append(send(x_own[0], "x"))
    g_pair.append(send(g_own[1], "x"))
    x_own.append(send(x_own[0], "z1"))
    g_own.append(send(g_own[1], "z1"))
    routed_other = jnp.concatenate(got_blocks, axis=0)
    pad = jnp.zeros((2 * GRAD_TILE - 2 * ex_cols, width), BF)
    routed_w = [
        jnp.concatenate(
            [routed_mine[k * ex_cols : (k + 1) * ex_cols], routed_other[k * ex_cols : (k + 1) * ex_cols], pad], axis=0)
        for k in range(3)
    ]

    shared_w, arrived_w, x_own, g_own, x_pair, g_pair, routed_w = sync(
        shared_w, arrived_w, x_own, g_own, x_pair, g_pair, routed_w)
    x_pair.append(send(x_own[1], "x"))
    x_own.append(send(x_own[1], "z1"))
    g_four.append(blocks_of(g_own[1], g_pair[1]))
    x_four = [blocks_of(x_own[0], x_pair[0])]
    behind = jnp.pad(router_rows, ((0, GRAD_TILE - sh_cols - experts - 1), (0, 0)))
    rest_at = 3 * full_cols
    cuts = [
        [(k * full_cols, full_cols), (rest_at + k * rest_cols, rest_cols)] for k in range(3)
    ]
    y_place = y.reshape(1)
    places = jnp.stack([lax.rem(z + 4 - step, 4) * 2 + side for step in (0, 1, 3, 2) for side in range(2)] + [y])
    shared_w = join_shared(places, shared_w, arrived_w, behind, cuts)

    expert = my_exp.reshape(1)
    fed, near_sums, sums, out_near, out_sums = [], [], [], [], []

    def core_sums(found):
        arrived = send(found[2], "core")
        return [found[0].astype(F32) + arrived[:own].astype(F32), found[1].astype(F32) + arrived[own:].astype(F32)]

    def pair_sums(parts):
        return parts[0] + send(parts[1].astype(BF), "x").astype(F32)

    for step in range(4):
        shared_w, routed_w, x_four, g_four, x_own, g_own, x_pair, g_pair, near_sums, sums, fed, out_near, out_sums = sync(
            shared_w, routed_w, x_four, g_four, x_own, g_own, x_pair, g_pair, near_sums, sums, fed, out_near, out_sums)
        if step == 0:
            x_pair.append(send(x_own[2], "x"))
            x_own.append(send(x_own[2], "z1"))
            g_own.append(send(g_own[2], "z1"))
            g_pair.append(send(g_own[2], "x"))
            x_four.append(blocks_of(x_own[1], x_pair[1]))
        if step == 1:
            x_pair.append(send(x_own[3], "x"))
            g_pair.append(send(g_own[3], "x"))
            x_four.append(blocks_of(x_own[2], x_pair[2]))
            g_four.append(blocks_of(g_own[2], g_pair[2]))
        if step == 2:
            x_four.append(blocks_of(x_own[3], x_pair[3]))
            g_four.append(blocks_of(g_own[3], g_pair[3]))
        if step >= 1:
            near_sums.append(core_sums(fed[step - 1][2]))
        if step >= 2:
            sums.append(pair_sums(near_sums[step - 2]))
            out_near.append(core_sums(fed[step - 2][3]))
        if step == 3:
            out_sums.append(pair_sums(out_near[0]))
        fed.append(feed(expert, x_four[step], g_four[step], shared_w, routed_w, experts, sh_cols))
    near_sums, sums, fed, x_four, g_four, out_near, out_sums, normed_two = sync(
        near_sums, sums, fed, x_four, g_four, out_near, out_sums, normed_two)

    x_blocks = [item for four_of in x_four for item in four_of]
    g_blocks = [item for four_of in g_four for item in four_of]
    shared_sets = [[fed[step][0][item] for step in range(4)] for item in range(3)]
    routed_sets = [[fed[step][1][item] for step in range(4)] for item in range(3)]
    flying = send(sums[1].astype(BF), "z1")
    sums.append(pair_sums(near_sums[2]))
    near_sums.append(core_sums(fed[3][2]))
    out_near.append(core_sums(fed[2][3]))
    sg_mine, sg_give, su_mine, su_give = weight_grads(y_place, x_blocks, [shared_sets[1], shared_sets[2]], width)
    (sums, near_sums, flying, sg_mine, sg_give, su_mine, su_give, x_blocks, g_blocks, shared_sets, routed_sets,
     out_near, fed) = sync(sums, near_sums, flying, sg_mine, sg_give, su_mine, su_give, x_blocks, g_blocks,
                           shared_sets, routed_sets, out_near, fed)
    sums.append(pair_sums(near_sums[3]))
    flying = send((sums[2] + flying.astype(F32)).astype(BF), "z1")
    sg_got = send(sg_give, "y")
    out_near.append(core_sums(fed[3][3]))
    sd_mine, sd_give = weight_grads(y_place, g_blocks, [shared_sets[0]], width)
    sums, flying, sg_got, su_give, sd_mine, sd_give, x_blocks, g_blocks, routed_sets, out_near, out_sums = sync(
        sums, flying, sg_got, su_give, sd_mine, sd_give, x_blocks, g_blocks, routed_sets, out_near, out_sums)
    flying = send((sums[3] + flying.astype(F32)).astype(BF), "z1")
    su_got = send(su_give, "y")
    out_sums.append(pair_sums(out_near[1]))
    e_parts = (ex_cols, ex_cols // 2, ex_cols // 2)
    ed_grad = weight_grads(y_place, g_blocks, [routed_sets[0]], width, e_parts)
    grad_sum, out_near, out_sums, su_got, sd_give, ed_grad, x_blocks, routed_sets = sync(
        sums[0] + flying.astype(F32), out_near, out_sums, su_got, sd_give, ed_grad, x_blocks, routed_sets)

    own_logits = contract("td,cd->tc", normed_two, router_rows)
    own_probs = jax.nn.softmax(own_logits[:, :experts], axis=-1)
    own_scale = jax.nn.sigmoid(own_logits[:, experts])
    grad_probs = grad_sum[:, width : width + experts]
    grad_router = own_probs * (grad_probs - jnp.sum(own_probs * grad_probs, axis=-1, keepdims=True))
    grad_gate = grad_sum[:, width + experts] * own_scale * (1.0 - own_scale)
    grad_logits = jnp.concatenate([grad_router, grad_gate[:, None]], axis=1).astype(BF)
    grad_normed_two = grad_sum[:, :width] + contract("tc,cd->td", grad_logits, router_rows)
    router_part = contract("tc,td->cd", grad_logits, normed_two)
    grad_after = grad_own.astype(F32) + norm_back(grad_normed_two, scaled_two, inverse_two, gain_two)
    gain_two_part = jnp.sum(grad_normed_two * scaled_two, axis=0)
    low = grad_after.astype(BF).reshape(micro, tok, width)
    sd_got = send(sd_give, "y")
    out_sums.append(pair_sums(out_near[2]))
    flying_out = send(out_sums[1].astype(BF), "z1")
    low, grad_after, out_sums, out_near, sd_got, flying_out, gain_two_part, router_part, x_blocks, routed_sets = sync(
        low, grad_after, out_sums, out_near, sd_got, flying_out, gain_two_part, router_part, x_blocks, routed_sets)
    far, near = send(low, "y"), send(low, "core")
    out_sums.append(pair_sums(out_near[3]))
    flying_out = send((out_sums[2] + flying_out.astype(F32)).astype(BF), "z1")
    shared_grads = fold_shared([(sg_mine, sg_got), (su_mine, su_got), (sd_mine, sd_got)], full_cols, rest_cols)
    shared_grads = shared_grads.reshape(4, 2, 2, rows_w, unit_cols)
    far, near, low, out_sums, flying_out, shared_grads, ed_grad, x_blocks, routed_sets = sync(
        far, near, low, out_sums, flying_out, shared_grads, ed_grad, x_blocks, routed_sets)

    def panel_sum(panel, gives, step):
        return [pick(panel, slot(step, 0)), send(gives[step], "x")]

    def two(parts):
        return parts[0].astype(F32) + parts[1].astype(F32)

    shared_grads = swap_core(shared_grads)
    flying_out = send((out_sums[3] + flying_out.astype(F32)).astype(BF), "z1")
    grad_attn = jnp.concatenate([low, near, far, send(far, "core")], axis=1).reshape(micro * seq, width)
    grad_attended = contract("td,cd->tc", grad_attn, wo).astype(BF)
    half = wide // 2
    keep = lax.dynamic_slice_in_dim(grad_attended, c * half, half, 1)
    give = lax.dynamic_slice_in_dim(grad_attended, (1 - c) * half, half, 1)
    arrived = turned(send(give, "core"))
    wo_part = contract("tc,td->cd", attended, grad_attn).astype(BF).reshape(n_exp, rows_w, width)
    wo_gives = [pick(wo_part, slot(step, 1)) for step in range(4)]
    shared_far = pick(shared_grads, lax.rem(z + 2, 4))
    shared_grads, shared_far, keep, arrived, flying_out, wo_part, wo_gives, ed_grad, x_blocks, routed_sets = sync(
        shared_grads, shared_far, keep, arrived, flying_out, wo_part, wo_gives, ed_grad, x_blocks, routed_sets)
    hidden_out = (after_attn + out_sums[0] + flying_out.astype(F32)).astype(BF)
    e_got = [send(ed_grad[1], "y")]
    shared_z = {2: send(shared_far, "z2")}
    def wo_pair(first, second):
        arrived = send(jnp.stack([wo_gives[first], wo_gives[second]]), "x")
        for k, step in enumerate((first, second)):
            wo_sums[step] = [pick(wo_part, slot(step, 0)), arrived[k]]

    wo_sums = {}
    wo_pair(1, 2)
    behind_rows = 16
    panel_shape = (n_exp, n_fsdp * rows_w + behind_rows, 3 * wide)
    grad_lin, grad_normed_one, gain_one_part, panel = attend(
        normed_seq, wqkv, bias, tables, seq, (keep, arrived, qkv_seq), core_place, panel_shape)
    shared_far = {k: pick(shared_grads, lax.rem(z + k, 4)) for k in (1, 3)}
    shared_z[0] = pick(shared_grads, z)
    give_x = pick(shared_z[0], 1 - x)
    (grad_lin, grad_normed_one, gain_one_part, panel, hidden_out, e_got, shared_z, shared_far, give_x, wo_part, wo_gives,
     wo_sums, ed_grad, x_blocks, routed_sets) = sync(
        grad_lin, grad_normed_one, gain_one_part, panel, hidden_out, e_got, shared_z, shared_far, give_x, wo_part, wo_gives,
        wo_sums, ed_grad, x_blocks, routed_sets)
    parts = grad_normed_one.reshape(micro, 2, 2, tok, width)
    parts = parts[:, :, 0] + send(parts[:, :, 1].astype(BF), "core").astype(F32)
    near, last = parts[:, 0], parts[:, 1].astype(BF)
    e_got.append(send(ed_grad[2], "y"))
    rest = ex_cols // 16 * 5 // 16 * 16
    g_parts, u_parts = (ex_cols, ex_cols - rest, rest), (ex_cols, rest, ex_cols - rest)
    eg_grad = weight_grads(y_place, x_blocks, [routed_sets[1]], width, g_parts)
    for k in (1, 3):
        shared_z[k] = send(shared_far[k], f"z{k}")
    wo_pair(3, 0)
    gain_one_part = gain_one_part[0] / gain_one
    bias_place = put(jnp.zeros((n_fsdp, 1, 3 * wide), F32), jnp.sum(grad_lin.astype(F32), axis=0)[None], my_fsdp)
    bias_place = from_fsdp(bias_place)[:, 0]
    small_part = jnp.concatenate([router_part, gain_one_part[None], gain_two_part[None], bias_place], axis=0)
    small_part = small_part.astype(BF).reshape(n_small, n_exp, n_fsdp, rows_w).transpose(1, 2, 0, 3)
    small_part = small_part.reshape(n_exp, n_fsdp * n_small * rows_w)
    small_part = jnp.pad(small_part, ((0, 0), (0, behind_rows * 3 * wide - small_part.shape[1])))
    panel = lax.dynamic_update_slice_in_dim(
        panel, small_part.reshape(n_exp, behind_rows, 3 * wide), n_fsdp * rows_w, 1)
    gives = [pick(panel, slot(step, 1)) for step in range(4)]
    (gives, panel, last, near, e_got, shared_z, give_x, wo_sums, wo_part, wo_gives, eg_grad, x_blocks,
     routed_sets) = sync(gives, panel, last, near, e_got, shared_z, give_x, wo_sums, wo_part, wo_gives, eg_grad,
                         x_blocks, routed_sets)

    far = send(last, "y")
    eu_grad = weight_grads(y_place, x_blocks, [routed_sets[2]], width, u_parts)
    e_grads = (eg_grad, eu_grad, ed_grad)
    shared_x, sums = [], {}

    for turn, step in enumerate((1, 2, 3, 0)):
        sums[step] = panel_sum(panel, gives, step)
        shared_x.append(send(give_x, "x"))
        if turn < 3:
            give_x = pick(shared_z[turn + 1], 1 - x)
        if turn:
            e_got.append(send(e_gives[turn - 1], "y"))
        if turn == 0:
            flying_wo = send(two(wo_sums[1]).astype(BF), "z1")
            e_gives = [eg_grad[1], jnp.concatenate([eg_grad[2], eu_grad[1]]), eu_grad[2]]
            (far, near, sums, e_got, shared_x, give_x, shared_z, e_grads, e_gives, panel, gives, flying_wo,
             wo_sums) = sync(far, near, sums, e_got, shared_x, give_x, shared_z, e_grads, e_gives, panel, gives,
                             flying_wo, wo_sums)
            continue
        if turn == 1:
            routed_grads = {2: ed_grad[0].astype(F32) + jnp.concatenate(e_got[:2]).astype(F32)}
            flying = send(two(sums[1]).astype(BF), "z1")
            grad_normed_one = (near + far.astype(F32)).reshape(own, width)
            in_grad = grad_after + norm_back(grad_normed_one, scaled_one, inverse_one, gain_one)
        else:
            flying = send((two(sums[turn]) + flying.astype(F32)).astype(BF), "z1")
        if turn == 3:
            rest = eg_grad[2].shape[0]
            got_g, got_u = e_got[3][:rest], e_got[3][rest:]
            routed_grads[0] = (eg_grad[0].astype(F32) + jnp.concatenate([e_got[2], got_g]).astype(F32)).T
        if turn < 3:
            flying_wo = send((two(wo_sums[turn + 1]) + flying_wo.astype(F32)).astype(BF), "z1")
            (sums, e_got, shared_x, give_x, shared_z, flying, e_grads, e_gives, panel, gives, flying_wo, in_grad,
             routed_grads, wo_part, wo_gives) = sync(
                sums, e_got, shared_x, give_x, shared_z, flying, e_grads, e_gives, panel, gives, flying_wo, in_grad,
                routed_grads, wo_part, wo_gives)
        else:
            out_own = two(wo_sums[0]) + flying_wo.astype(F32)
            flying, sums, out_own, e_got, shared_x = sync(flying, sums, out_own, e_got, shared_x)
    shared_blocks = jnp.stack([in_order(pick(shared_z[k], x), shared_x[k], x, 0) for k in range(4)])
    places = (lax.rem(z + 4 - jnp.arange(4), 4)[:, None] * 4 + jnp.arange(4)[None]).reshape(16)
    shared_own = unpack_shared(
        shared_blocks.reshape(16, rows_w, unit_cols), places.astype(jnp.int32), full_cols, rest_cols)
    routed_grads[1] = (eu_grad[0].astype(F32) + jnp.concatenate([got_u, e_got[4]]).astype(F32)).T
    total = (two(sums[0]) + flying.astype(F32)).astype(BF)

    count = n_fsdp * rows_w
    small_sum = total[count:].reshape(-1)[: n_fsdp * n_small * rows_w].reshape(n_fsdp, n_small * rows_w)
    small_sum = jnp.pad(small_sum, ((0, 0), (0, 3 * wide - n_small * rows_w)))
    blocks = jnp.concatenate([total[:count, : 3 * wide].reshape(n_fsdp, rows_w, 3 * wide), small_sum[:, None]], axis=1)
    qkv_own = blocks
    for k, link in ((1, "core"), (2, "y"), (3, "yc")):
        place = lax.bitwise_xor(my_fsdp, k)
        qkv_own = put(qkv_own, send(pick(blocks, place), link), place)
    small_own = jnp.sum(qkv_own[:, rows_w, : n_small * rows_w].astype(F32), axis=0).reshape(n_small, rows_w)
    qkv_own = from_fsdp(qkv_own[:, :rows_w]).astype(F32)
    return (
        hidden_out.reshape(micro, tok, width),
        in_grad.reshape(micro, tok, width),
        small_own[experts + 1],
        qkv_own[0],
        qkv_own[1],
        qkv_own[2],
        small_own[experts + 3 :],
        out_own,
        small_own[experts + 2],
        small_own[:experts].T,
        small_own[experts],
        shared_own[0],
        shared_own[1],
        shared_own[2],
        routed_grads[0][None],
        routed_grads[1][None],
        routed_grads[2][None],
    )


def on_device_any(
    hidden_in, seg_ids, routes, out_grad, norm_gain1, w_query, w_key, w_value, b_qkv, w_out,
    norm_gain2, w_router, shared_gate, sh_gate, sh_up, sh_down, ex_gate, ex_up, ex_down,
):
    links = Links()
    micro, tok, width = hidden_in.shape
    experts = w_router.shape[1]
    rows_w = w_query.shape[0]
    n_exp, n_fsdp, n_all = links.n_exp, links.n_fsdp, links.n_all
    my_exp, my_fsdp = links.my_exp, links.my_fsdp
    half_f, core_f = my_fsdp // 2, lax.rem(my_fsdp, 2)
    heads_dev = HEADS // n_fsdp
    wide = heads_dev * HEAD
    seq = tok * n_fsdp
    own = micro * tok
    sh_cols = SHARED_FF // n_all
    ex_cols = ex_gate.shape[2]

    def by_fsdp(three):
        rows = three.shape[0]
        split = three.reshape(rows, 3, 2, 2, heads_dev // 2, 2, HEAD)
        return split.transpose(5, 2, 0, 3, 1, 4, 6).reshape(n_fsdp, rows, 3 * wide)

    def from_fsdp(blocks):
        rows = blocks.shape[1]
        split = blocks.reshape(2, 2, rows, 2, 3, heads_dev // 2, HEAD)
        return split.transpose(4, 2, 1, 3, 5, 0, 6).reshape(3, rows, width)

    small = jnp.concatenate([w_router.T, shared_gate[None], norm_gain1[None], norm_gain2[None], b_qkv], axis=0)
    n_small = small.shape[0]
    small = lax.all_gather(small, ALL, axis=1, tiled=True)
    router_rows = small[: experts + 1]
    gain_one = small[experts + 1].astype(F32)
    gain_two = small[experts + 2].astype(F32)
    bias = by_fsdp(small[experts + 3 :].astype(F32)[None])
    bias = lax.dynamic_index_in_dim(bias, my_fsdp, 0, keepdims=False)

    x = hidden_in.reshape(own, width).astype(F32)
    scaled_one, inverse_one = normalize(x)
    normed_one = (scaled_one * gain_one).astype(BF)
    normed_seq = links.gather_seq(normed_one.reshape(micro, tok, width)).reshape(micro * seq, width)

    qkv = by_fsdp(jnp.stack([w_query, w_key, w_value], axis=1))
    qkv = links.swap_fsdp(qkv).reshape(n_fsdp * rows_w, 3 * wide)
    wqkv = links.gather_rows(qkv).reshape(width, 3 * wide)
    wo = lax.all_gather(w_out, ALL, axis=0, tiled=True).reshape(2, heads_dev, 2, HEAD, width)
    wo = lax.dynamic_index_in_dim(wo, core_f, 0, keepdims=False)
    wo = lax.dynamic_index_in_dim(wo, half_f, 1, keepdims=False).reshape(wide, width)

    tile_cols = sh_cols // LANES * LANES
    rest_cols = sh_cols - tile_cols

    def by_owner(weight):
        full = weight[:, : n_all * tile_cols].reshape(rows_w, n_all, tile_cols).transpose(1, 0, 2)
        rest = weight[:, n_all * tile_cols :].reshape(rows_w, n_all, rest_cols).transpose(1, 0, 2)
        return full, rest

    def from_owner(full, rest):
        return jnp.concatenate(
            [full.transpose(1, 0, 2).reshape(rows_w, -1), rest.transpose(1, 0, 2).reshape(rows_w, -1)], axis=1
        )

    pieces = [by_owner(weight) for weight in (sh_gate, sh_up, sh_down)]
    shared_w = jnp.concatenate([piece[0] for piece in pieces] + [piece[1] for piece in pieces], axis=2)
    shared_w = lax.all_to_all(shared_w, ALL, split_axis=0, concat_axis=0, tiled=True)
    shared_w = shared_w.reshape(width, 3 * sh_cols).T

    def three(rows):
        return [
            jnp.concatenate(
                [rows[k * tile_cols : (k + 1) * tile_cols],
                 rows[3 * tile_cols + k * rest_cols : 3 * tile_cols + (k + 1) * rest_cols]], axis=0)
            for k in range(3)
        ]

    shared_other = links.partner(shared_w, 2)
    routed_w = jnp.concatenate([ex_gate[0].T, ex_up[0].T, ex_down[0]], axis=0)
    halves = [[0, 2], [1, 3]]
    routed_w = lax.all_gather(routed_w, "fsdp", axis=0, axis_index_groups=halves)
    routed_w = [routed_w[:, k * ex_cols : (k + 1) * ex_cols].reshape(2 * ex_cols, width) for k in range(3)]
    units = 2 * (sh_cols + ex_cols)
    pad_rows = -(units + experts + 1) % LANES
    pad = jnp.zeros((pad_rows + experts + 1, width), BF)
    behind = (jnp.pad(router_rows, ((0, pad_rows), (0, 0))), pad, pad)
    wg, wu, wd = [
        jnp.concatenate(pieces, axis=0)
        for pieces in zip(three(shared_w), three(shared_other), routed_w, behind)
    ]
    shared_units = 2 * sh_cols

    grad_own = out_grad.reshape(own, width)
    names = jnp.pad(routes.reshape(own, -1).astype(BF), ((0, 0), (0, LANES - routes.shape[2])))
    grad_near = lax.all_gather(jnp.concatenate([grad_own, names], axis=1), "expert", axis=0)
    grad_far = links.partner(grad_near, 1)

    order = lax.bitwise_xor(my_fsdp, jnp.arange(n_fsdp))
    places = (order[:, None] * tok + jnp.arange(tok)[None]).reshape(seq)
    seg_seq = links.gather_seq(seg_ids)
    cosine, sine = angle_tables(places)
    tables = (cosine, sine, places[:, None], seg_seq.reshape(micro * seq, 1), places[None], seg_seq)
    qkv_seq, attended = attend(normed_seq, wqkv, bias, tables, seq)
    attn_part = contract("tc,cd->td", attended, wo).reshape(micro, n_fsdp, tok, width)
    attn_sum = links.sum_four([attn_part[:, k] for k in range(4)]).reshape(own, width)
    after_attn = x + attn_sum
    scaled_two, inverse_two = normalize(after_attn)
    normed_two = (scaled_two * gain_two).astype(BF)

    near = lax.all_gather(normed_two, "expert", axis=0, tiled=True)
    normed_all = jnp.concatenate([near, links.partner(near, 1)], axis=0)
    grad_all = jnp.concatenate([grad_near, grad_far], axis=0).reshape(2 * n_exp * own, -1)
    named = jnp.sum((grad_all[:, width : width + routes.shape[2]] == my_exp.astype(BF)).astype(F32), axis=1)
    grad_part, out_part, wg_grad, wu_grad, wd_grad = feed_plain(
        normed_all, grad_all[:, :width], named, my_exp, wg, wu, wd, router_rows, experts, shared_units
    )

    def summed(part):
        count = n_exp * own
        total = part[:count] + links.partner(part[count:].astype(BF), 1).astype(F32)
        return links.sum_rows(total.reshape(n_exp, own, -1))

    grad_sum, out_sum = summed(grad_part), summed(out_part)
    wg_grad, wu_grad, wd_grad = [item.astype(BF) for item in (wg_grad, wu_grad, wd_grad)]
    hidden_out = (after_attn + out_sum).astype(BF)

    own_logits = contract("td,cd->tc", normed_two, router_rows)
    own_probs = jax.nn.softmax(own_logits[:, :experts], axis=-1)
    own_scale = jax.nn.sigmoid(own_logits[:, experts])
    grad_probs = grad_sum[:, width : width + experts]
    grad_router = own_probs * (grad_probs - jnp.sum(own_probs * grad_probs, axis=-1, keepdims=True))
    grad_gate = grad_sum[:, width + experts] * own_scale * (1.0 - own_scale)
    grad_logits = jnp.concatenate([grad_router, grad_gate[:, None]], axis=1).astype(BF)
    grad_normed_two = grad_sum[:, :width] + contract("tc,cd->td", grad_logits, router_rows)
    router_part = contract("tc,td->cd", grad_logits, normed_two)

    grad_after = grad_own.astype(F32) + norm_back(grad_normed_two, scaled_two, inverse_two, gain_two)
    gain_two_part = jnp.sum(grad_normed_two * scaled_two, axis=0)

    grad_attn = links.gather_seq(grad_after.astype(BF).reshape(micro, tok, width)).reshape(micro * seq, width)
    grad_lin, grad_normed_one, gain_one_part = attend(normed_seq, wqkv, bias, tables, seq, (grad_attn, wo, qkv_seq))
    gain_one_part = gain_one_part[0] / gain_one
    grad_normed_one = grad_normed_one.reshape(micro, n_fsdp, tok, width)
    grad_normed_one = links.sum_four([grad_normed_one[:, k] for k in range(4)]).reshape(own, width)
    in_grad = grad_after + norm_back(grad_normed_one, scaled_one, inverse_one, gain_one)
    out_grad_part = contract("tc,td->cd", attended, grad_attn).astype(BF)
    qkv_part = contract("td,tc->dc", normed_seq, grad_lin).astype(BF)
    bias_part = jnp.sum(grad_lin.astype(F32), axis=0)

    out_place = jnp.zeros((2, heads_dev, 2, HEAD, width), BF)
    out_place = lax.dynamic_update_slice(
        out_place, out_grad_part.reshape(1, heads_dev, 1, HEAD, width), (core_f, 0, half_f, 0, 0)
    )
    out_own = lax.psum_scatter(
        out_place.reshape(width, width), ALL, scatter_dimension=0, tiled=True
    ).astype(F32)
    bias_place = jnp.zeros((n_fsdp, 1, 3 * wide), F32)
    bias_place = from_fsdp(lax.dynamic_update_index_in_dim(bias_place, bias_part[None], my_fsdp, 0))[:, 0]
    small_part = jnp.concatenate([router_part, gain_one_part[None], gain_two_part[None], bias_place], axis=0)
    small_part = small_part.astype(BF).reshape(n_small, n_exp, n_fsdp, rows_w).transpose(1, 2, 0, 3)
    behind_rows = -(-n_fsdp * n_small * rows_w // (3 * wide) // 8) * 8
    room = behind_rows * 3 * wide
    small_part = small_part.reshape(n_exp, n_fsdp * n_small * rows_w)
    small_part = jnp.pad(small_part, ((0, 0), (0, room - small_part.shape[1])))
    qkv_part = jnp.concatenate(
        [qkv_part.reshape(n_exp, n_fsdp * rows_w, 3 * wide), small_part.reshape(n_exp, behind_rows, 3 * wide)], axis=1
    )
    qkv_sum = links.sum_rows(qkv_part).astype(BF)
    small_sum = qkv_sum[n_fsdp * rows_w :].reshape(-1)[: n_fsdp * n_small * rows_w].reshape(n_fsdp, n_small * rows_w)
    small_sum = jnp.pad(small_sum, ((0, 0), (0, 3 * wide - n_small * rows_w)))
    qkv_sum = qkv_sum[: n_fsdp * rows_w].reshape(n_fsdp, rows_w, 3 * wide)
    qkv_own = links.swap_fsdp(jnp.concatenate([qkv_sum, small_sum[:, None]], axis=1))
    small_own = jnp.sum(qkv_own[:, rows_w, : n_small * rows_w].astype(F32), axis=0).reshape(n_small, rows_w)
    qkv_own = from_fsdp(qkv_own[:, :rows_w]).astype(F32)

    grads = (wg_grad, wu_grad, wd_grad)
    shared_mine = jnp.concatenate(
        [grad[:tile_cols] for grad in grads] + [grad[tile_cols:sh_cols] for grad in grads], axis=0)
    shared_give = jnp.concatenate(
        [grad[sh_cols : sh_cols + tile_cols] for grad in grads]
        + [grad[sh_cols + tile_cols : 2 * sh_cols] for grad in grads], axis=0)
    shared_got = links.partner(shared_give, 2)
    shared_grads = (shared_mine.astype(F32) + shared_got.astype(F32)).astype(BF)
    shared_own = lax.all_to_all(
        shared_grads.T.reshape(n_all, rows_w, 3 * sh_cols), ALL, split_axis=0, concat_axis=0, tiled=True
    )
    cut = 3 * tile_cols
    shared_own = [
        from_owner(
            shared_own[:, :, k * tile_cols : (k + 1) * tile_cols],
            shared_own[:, :, cut + k * rest_cols : cut + (k + 1) * rest_cols],
        ).astype(F32)
        for k in range(3)
    ]
    routed_grads = jnp.stack(
        [
            jnp.concatenate([grad[low : low + ex_cols] for grad in grads], axis=0)
            for low in (shared_units, shared_units + ex_cols)
        ]
    )
    routed_grads = lax.psum_scatter(routed_grads, "fsdp", scatter_dimension=0, axis_index_groups=halves).astype(F32)
    routed_grads = [routed_grads[k * ex_cols : (k + 1) * ex_cols] for k in range(3)]
    return (
        hidden_out.reshape(micro, tok, width),
        in_grad.reshape(micro, tok, width),
        small_own[experts + 1],
        qkv_own[0],
        qkv_own[1],
        qkv_own[2],
        small_own[experts + 3 :],
        out_own,
        small_own[experts + 2],
        small_own[:experts].T,
        small_own[experts],
        shared_own[0],
        shared_own[1],
        shared_own[2],
        routed_grads[0].T[None],
        routed_grads[1].T[None],
        routed_grads[2][None],
    )


def solution(mesh):
    rows = P(ALL, None)
    tokens = P(None, ALL, None)
    in_specs = (
        tokens, P(None, ALL), tokens, tokens, P(ALL), rows, rows, rows, P(None, ALL), rows,
        P(ALL), rows, P(ALL), rows, rows, rows,
        P("expert", None, "fsdp"), P("expert", None, "fsdp"), P("expert", "fsdp", None),
    )
    out_specs = (
        tokens, tokens, P(ALL), rows, rows, rows, P(None, ALL), rows, P(ALL), rows, P(ALL),
        rows, rows, rows,
        P("expert", None, "fsdp"), P("expert", None, "fsdp"), P("expert", "fsdp", None),
    )
    on_device = on_device_ring if mesh.shape["expert"] == 8 and mesh.shape["fsdp"] == 4 else on_device_any
    return jax.shard_map(on_device, mesh=mesh, in_specs=in_specs, out_specs=out_specs, check_vma=False)
```
